32 devices in a mesh: tunnel: 16 (over z, x, core), group: 2 (over y).
Axes of the slice: x: 2, y: 2, z: 4, core: 2. Of those that a mesh axis runs over, the one named last changes fastest.
Arguments:
- velocity: float32 [3, 64, 512, 256], P(None, ('tunnel', 'group')), may hold values from -6 to 6
- obstacle: int32 [64, 512, 256], P(('tunnel', 'group')), may hold values 0 or 1
- pressure: float32 [64, 512, 256], P('tunnel', 'group'), may hold values from -6 to 6
Outputs:
- corrected: float32 [3, 64, 512, 256], P(None, ('tunnel', 'group'))
- potential: float32 [64, 512, 256], P('tunnel', 'group')
The draws below stay inside these ranges and needn't reach their ends.
All inputs are finite; a program needn't handle non-finite values. No bound on the sum of `obstacle` on one device may be relied on, other than what follows from the above.
Results may differ from the reference program's by a relative error of at most 0.00018.
Values sent between devices are 32-bit elements; how exact they have to be, the bound alone decides.
No kernel may reach another device: no remote copies, remote signals or barrier semaphores. Data moves between devices by JAX's collectives and lax.ppermute only.
A program may use at most 256 MiB of HBM per device.

```python
import math
import jax
import jax.numpy as jnp
from jax import lax

NY = 512
NZ = 256
LEVELS = 3
SWEEPS = 2
COARSE_SWEEPS = 4
X = 64


def plant(values, own_key, smallest, high):
    place = [jax.random.randint(jax.random.fold_in(own_key, axis), (), 0, length) for axis, length in enumerate(values.shape)]
    main_axis = values.shape.index(max(values.shape))
    neighbour = place[:main_axis] + [(place[main_axis] + 1) % values.shape[main_axis]] + place[main_axis + 1:]
    return values.at[tuple(place)].set(smallest).at[tuple(neighbour)].set(high)


def block_scale(own_key, dims, split, least, top_value):
    def one(position, shards_of):
        steps = jax.random.uniform(jax.random.fold_in(jax.random.fold_in(own_key, 6), position), (shards_of,), jnp.float32, least / len(split), top_value / len(split))
        return jnp.repeat(jnp.exp(steps), dims[position] // shards_of).reshape((-1,) + (1,) * (len(dims) - position - 1))

    factor_of = one(*split[0])
    for cut in split[1:]:
        factor_of = factor_of * one(*cut)
    return factor_of


def bell_draw(rng, dims, deviation, limit, split=(), kind=jnp.bfloat16):
    entries = deviation * jax.random.normal(rng, dims, jnp.float32)
    if split:
        entries = entries * block_scale(rng, dims, split, -0.22, 0.18)
    return jnp.clip(entries, -limit, limit).astype(kind)


def setup_inputs(seed: int = 0) -> dict:
    streams_of = jax.random.split(jax.random.key(seed), 4)
    return {
        "velocity": bell_draw(streams_of[0], (3, X, NY, NZ), 1.0, 6.0, ((1, 32),), jnp.float32),
        "obstacle": plant((jax.random.randint(streams_of[1], (X, NY, NZ), 0, 8) < 1).astype(jnp.int32), jax.random.fold_in(streams_of[1], 1), 0, 1),
        "pressure": bell_draw(streams_of[2], (X, NY, NZ), 1.0, 6.0, ((0, 16), (1, 2)), jnp.float32),
    }


time_step = 0.1
viscosity = 0.05
relax_weight = 0.8
highest = lax.Precision.HIGHEST


def compact_tables(count):
    indices = jnp.arange(count, dtype=jnp.int32)
    product = (indices[:, None] * indices[None, :]) % count
    angles = product.astype(jnp.float32) * (2.0 * math.pi / count)
    cosines = jnp.cos(angles)
    sines = jnp.sin(angles)
    theta = indices.astype(jnp.float32) * (2.0 * math.pi / count)
    first_wave = (14.0 / 9.0 * jnp.sin(theta) + jnp.sin(2.0 * theta) / 18.0) / (1.0 + 2.0 / 3.0 * jnp.cos(theta))
    second_wave = (24.0 / 11.0 * (1.0 - jnp.cos(theta)) + 3.0 / 22.0 * (1.0 - jnp.cos(2.0 * theta))) / (1.0 + 4.0 / 11.0 * jnp.cos(theta))
    first_matrix = (jnp.dot(cosines * first_wave, sines.T, precision=highest) - jnp.dot(sines * first_wave, cosines.T, precision=highest)) / count
    second_matrix = -(jnp.dot(cosines * second_wave, cosines.T, precision=highest) + jnp.dot(sines * second_wave, sines.T, precision=highest)) / count
    return first_matrix, second_matrix


def along_rows(matrix, field):
    return jnp.einsum('ij,...jz->...iz', matrix, field, precision=highest)


def along_depth(matrix, field):
    return jnp.einsum('...j,ij->...i', field, matrix, precision=highest)


def stream_first(field, axis):
    ahead = jnp.roll(field, -1, axis)
    behind = jnp.roll(field, 1, axis)
    ahead_two = jnp.roll(field, -2, axis)
    behind_two = jnp.roll(field, 2, axis)
    return (8.0 * (ahead - behind) - (ahead_two - behind_two)) / 12.0


def stream_second(field, axis):
    ahead = jnp.roll(field, -1, axis)
    behind = jnp.roll(field, 1, axis)
    ahead_two = jnp.roll(field, -2, axis)
    behind_two = jnp.roll(field, 2, axis)
    return (16.0 * (ahead + behind) - (ahead_two + behind_two) - 30.0 * field) / 12.0


def neighbours(field):
    total = jnp.roll(field, -1, 0) + jnp.roll(field, 1, 0)
    total = total + jnp.roll(field, -1, 1) + jnp.roll(field, 1, 1)
    return total + jnp.roll(field, -1, 2) + jnp.roll(field, 1, 2)


def relax(field, source_term, scale):
    return field + relax_weight / 6.0 * (neighbours(field) - 6.0 * field - scale * source_term)


def restrict(field):
    planes, rows, depth = field.shape
    blocks = field.reshape(planes // 2, 2, rows // 2, 2, depth // 2, 2)
    return jnp.sum(blocks, axis=(1, 3, 5)) * 0.125


def prolong(field):
    return jnp.repeat(jnp.repeat(jnp.repeat(field, 2, 0), 2, 1), 2, 2)


def cycle(field, source_term, level):
    scale = 4.0 ** level
    if level == LEVELS - 1:
        field = jnp.zeros_like(source_term)
        for sweep_index in range(COARSE_SWEEPS):
            field = relax(field, source_term, scale)
        return field
    for sweep_index in range(SWEEPS):
        field = relax(field, source_term, scale)
    leftover = source_term - (neighbours(field) - 6.0 * field) / scale
    coarse_source = restrict(leftover)
    coarse = cycle(jnp.zeros_like(coarse_source), coarse_source, level + 1)
    field = field + prolong(coarse)
    for sweep_index in range(SWEEPS):
        field = relax(field, source_term, scale)
    return field


def reference(velocity, obstacle, pressure):
    rows_first, rows_second = compact_tables(NY)
    depth_first, depth_second = compact_tables(NZ)
    keep = 1.0 - obstacle.astype(jnp.float32)
    advect = velocity[0] * stream_first(velocity, 1)
    advect = advect + velocity[1] * along_rows(rows_first, velocity)
    advect = advect + velocity[2] * along_depth(depth_first, velocity)
    diffusion = stream_second(velocity, 1) + along_rows(rows_second, velocity) + along_depth(depth_second, velocity)
    tendency = -advect + viscosity * diffusion
    star = (velocity + time_step * tendency) * keep
    source = stream_first(star[0], 0) + along_rows(rows_first, star[1]) + along_depth(depth_first, star[2])
    potential = cycle(pressure, source, 0)
    gradient = jnp.stack([stream_first(potential, 0), along_rows(rows_first, potential), along_depth(depth_first, potential)])
    corrected = (star - gradient) * keep
    return corrected, potential
```

```python
import math

import jax
import jax.numpy as jnp
import ml_dtypes
import numpy as np
from jax import lax
from jax.experimental import pallas as pl
from jax.experimental.pallas import tpu as pltpu
from jax.sharding import PartitionSpec as P

LEVELS = 3
SWEEPS = 2
COARSE_SWEEPS = 4


time_step = 0.1
viscosity = 0.05
relax_weight = 0.8
highest = lax.Precision.HIGHEST


def extended(value, sides, width):
    for axis, dim in sides:
        size, length = (lax.axis_size(axis), value.shape[dim])
        up = [(i, (i + 1) % size) for i in range(size)]
        down = [(j, i) for i, j in up]
        last = lax.slice_in_dim(value, length - width, length, axis=dim)
        initial = lax.slice_in_dim(value, 0, width, axis=dim)
        before = lax.ppermute(last, axis, up)
        after = lax.ppermute(initial, axis, down)
        value = jnp.concatenate([before, value, after], axis=dim)
    return value


def compact_tables(count):
    indices = jnp.arange(count, dtype=jnp.int32)
    product = indices[:, None] * indices[None, :] % count
    angles = product.astype(jnp.float32) * (2.0 * math.pi / count)
    cosines = jnp.cos(angles)
    sines = jnp.sin(angles)
    theta = indices.astype(jnp.float32) * (2.0 * math.pi / count)
    first_wave = (14.0 / 9.0 * jnp.sin(theta) + jnp.sin(2.0 * theta) / 18.0) / (
        1.0 + 2.0 / 3.0 * jnp.cos(theta)
    )
    second_wave = (
        24.0 / 11.0 * (1.0 - jnp.cos(theta)) + 3.0 / 22.0 * (1.0 - jnp.cos(2.0 * theta))
    ) / (1.0 + 4.0 / 11.0 * jnp.cos(theta))
    first_matrix = (
        jnp.dot(cosines * first_wave, sines.T, precision=highest)
        - jnp.dot(sines * first_wave, cosines.T, precision=highest)
    ) / count
    second_matrix = (
        -(
            jnp.dot(cosines * second_wave, cosines.T, precision=highest)
            + jnp.dot(sines * second_wave, sines.T, precision=highest)
        )
        / count
    )
    return (first_matrix, second_matrix)


def along_rows(matrix, field):
    return jnp.einsum("ij,...jz->...iz", matrix, field, precision=highest)


def along_depth(matrix, field):
    return jnp.einsum("...j,ij->...i", field, matrix, precision=highest)


def shifted(padded, offset, axis):
    count = padded.shape[axis] - 4
    return lax.slice_in_dim(padded, 2 + offset, 2 + offset + count, axis=axis)


def stream_first(padded, axis):
    ahead = shifted(padded, 1, axis) - shifted(padded, -1, axis)
    further = shifted(padded, 2, axis) - shifted(padded, -2, axis)
    return (8.0 * ahead - further) / 12.0


def stream_second(padded, axis):
    ahead = shifted(padded, 1, axis) + shifted(padded, -1, axis)
    further = shifted(padded, 2, axis) + shifted(padded, -2, axis)
    return (16.0 * ahead - further - 30.0 * shifted(padded, 0, axis)) / 12.0


def padded_neighbours(padded):
    interior = padded[1:-1, 1:-1]
    total = padded[2:, 1:-1] + padded[:-2, 1:-1]
    total = total + padded[1:-1, 2:] + padded[1:-1, :-2]
    return total + jnp.roll(interior, -1, 2) + jnp.roll(interior, 1, 2)


def relax_padded(padded, source_term, scale):
    interior = padded[1:-1, 1:-1]
    return interior + relax_weight / 6.0 * (
        padded_neighbours(padded) - 6.0 * interior - scale * source_term
    )


def faces(field):
    return extended(field, (("tunnel", 0), ("group", 1)), 1)


def thin_sweeps(field, source_term, scale, count):
    for sweep_index in range(count):
        field = relax_padded(faces(field), source_term, scale)
    return field


def smooth(field, source_term, scale, level):
    if level == 0:
        return thin_sweeps(field, source_term, scale, SWEEPS)
    return thin_sweeps(field, source_term, scale, SWEEPS)


def coarsest(source_term, scale):
    return thin_sweeps(jnp.zeros_like(source_term), source_term, scale, COARSE_SWEEPS)


def restrict(field):
    planes, rows, depth = field.shape
    blocks = field.reshape(planes // 2, 2, rows // 2, 2, depth // 2, 2)
    return jnp.sum(blocks, axis=(1, 3, 5)) * 0.125


def prolong(field):
    return jnp.repeat(jnp.repeat(jnp.repeat(field, 2, 0), 2, 1), 2, 2)


def cycle(field, source_term, level):
    scale = 4.0**level
    if level == LEVELS - 1:
        return coarsest(source_term, scale)
    field = smooth(field, source_term, scale, level)
    leftover = source_term - (padded_neighbours(faces(field)) - 6.0 * field) / scale
    coarse_source = restrict(leftover)
    coarse = cycle(jnp.zeros_like(coarse_source), coarse_source, level + 1)
    field = field + prolong(coarse)
    return smooth(field, source_term, scale, level)


def local(velocity, obstacle, pressure):
    row_count = velocity.shape[2]
    depth_count = velocity.shape[3]
    rows_first, rows_second = compact_tables(row_count)
    depth_first, depth_second = compact_tables(depth_count)
    rows_both = jnp.concatenate([rows_first, rows_second], axis=0)
    depth_both = jnp.concatenate([depth_first, depth_second], axis=0)
    keep = 1.0 - obstacle.astype(jnp.float32)
    row_terms = along_rows(rows_both, velocity)
    depth_terms = along_depth(depth_both, velocity)
    transverse = (
        velocity[1] * row_terms[:, :, :row_count] + velocity[2] * depth_terms[..., :depth_count]
    )
    diffusion = row_terms[:, :, row_count:] + depth_terms[..., depth_count:]
    padded = extended(velocity, ((("tunnel", "group"), 1),), 2)
    streamwise = -velocity[0] * stream_first(padded, 1) + viscosity * stream_second(padded, 1)
    tendency = streamwise - transverse + viscosity * diffusion
    star = (velocity + time_step * tendency) * keep
    star_padded = extended(star[0], ((("tunnel", "group"), 0),), 2)
    source = (
        stream_first(star_padded, 0)
        + along_rows(rows_first, star[1])
        + along_depth(depth_first, star[2])
    )
    source_tile = lax.all_to_all(source, "group", split_axis=1, concat_axis=0, tiled=True)
    potential = cycle(pressure, source_tile, 0)
    potential_padded = extended(potential, (("tunnel", 0),), 2)
    streamwise_grad = stream_first(potential_padded, 0)
    returned = lax.all_to_all(
        jnp.stack([potential, streamwise_grad]), "group", split_axis=1, concat_axis=2, tiled=True
    )
    gradient = jnp.stack(
        [returned[1], along_rows(rows_first, returned[0]), along_depth(depth_first, returned[0])]
    )
    corrected = (star - gradient) * keep
    return (corrected, potential)


HALO = 16
weight = relax_weight / 6.0
bf16 = jnp.bfloat16
f32 = jnp.float32
VMEM = pl.BlockSpec(memory_space=pltpu.VMEM)
ANY = pl.BlockSpec(memory_space=pl.ANY)


def wave_tables(count):
    index = np.arange(count)
    angles = 2.0 * np.pi * (np.outer(index, index) % count) / count
    theta = 2.0 * np.pi * index / count
    first_wave = (14.0 / 9.0 * np.sin(theta) + np.sin(2.0 * theta) / 18.0) / (
        1.0 + 2.0 / 3.0 * np.cos(theta)
    )
    second_wave = (
        24.0 / 11.0 * (1.0 - np.cos(theta)) + 3.0 / 22.0 * (1.0 - np.cos(2.0 * theta))
    ) / (1.0 + 4.0 / 11.0 * np.cos(theta))
    cosines, sines = (np.cos(angles), np.sin(angles))
    first = ((cosines * first_wave) @ sines.T - (sines * first_wave) @ cosines.T) / count
    second = -((cosines * second_wave) @ cosines.T + (sines * second_wave) @ sines.T) / count
    return (first, second)


def high_low(table):
    high = table.astype(np.float32).astype(ml_dtypes.bfloat16)
    low = (table - high.astype(np.float64)).astype(np.float32).astype(ml_dtypes.bfloat16)
    return (high, low)


def half_tables(count):
    first, second = wave_tables(count)
    half = count // 2
    index = np.arange(half)
    root_first = (math.sqrt(5.0) - 3.0) / 2.0
    root_second = (math.sqrt(105.0) - 11.0) / 4.0
    basis = np.zeros((8, half))
    basis[0, 0] = 1.0
    basis[1, -1] = 1.0
    basis[2] = root_first**index
    basis[3] = basis[2][::-1]
    basis[4] = root_second**index
    basis[5] = basis[4][::-1]
    spread = []
    for table, used in ((first, (0, 1, 2, 3)), (second, (0, 1, 4, 5))):
        solved = np.linalg.lstsq(basis[list(used)].T, table[:half, half:].T, rcond=None)[0].T
        wide = np.zeros((half, 8))
        wide[:, list(used)] = solved
        spread.append(wide)
    own = np.concatenate([first[:half, :half], second[:half, :half]], axis=0)
    return (own, np.concatenate(spread, axis=0), basis, first)


def split(value):
    high = value.astype(bf16)
    low = (value - high.astype(f32)).astype(bf16)
    return (high, low)


def dot(left, right):
    return jnp.dot(left, right, preferred_element_type=f32)


def dot_left(table_high, table_low, value):
    high, low = split(value)
    return dot(table_high, high) + (dot(table_high, low) + dot(table_low, high))


def dot_right(value, table_high, table_low):
    high, low = split(value)
    return dot(high, table_high) + (dot(low, table_high) + dot(high, table_low))


def pick_left(zero_one, value):
    high, low = split(value)
    return dot(zero_one, high) + dot(zero_one, low)


def pick_right(value, zero_one):
    high, low = split(value)
    return dot(high, zero_one) + dot(low, zero_one)


def summary(basis_both, value):
    high, low = split(value)
    main = dot(basis_both, high)
    rest = dot(basis_both, low)
    return main[:8] + main[8:] + rest[:8]


def summary_operand(value):
    high = value.astype(bf16).astype(f32)
    return jnp.concatenate([high, value - high, high, jnp.zeros_like(high)], axis=0).astype(bf16)


def turn(value, shift, axis):
    return pltpu.roll(value, shift % value.shape[axis], axis)


def cross_sum(value):
    return (turn(value, 1, 0) + turn(value, -1, 0)) + (turn(value, 1, 1) + turn(value, -1, 1))


def first_of(values):
    return (8.0 * (values[3] - values[1]) - (values[4] - values[0])) * (1.0 / 12.0)


def second_of(values):
    return (
        16.0 * (values[3] + values[1]) - (values[4] + values[0]) - 30.0 * values[2]
    ) * (1.0 / 12.0)


def kernel_call(body, outs, scratch, specs, flops, *args, grid=None, out_specs=None):
    total = sum(math.prod(a.shape) * a.dtype.itemsize for a in args)
    total += sum(4 * math.prod(s) for s in outs)
    options = {} if grid is None else {"grid": grid}
    return pl.pallas_call(
        body,
        out_shape=[jax.ShapeDtypeStruct(s, f32) for s in outs],
        in_specs=specs,
        out_specs=[VMEM] * len(outs) if out_specs is None else out_specs,
        scratch_shapes=scratch,
        compiler_params=pltpu.CompilerParams(vmem_limit_bytes=56 * 1024 * 1024),
        cost_estimate=pl.CostEstimate(flops=flops, bytes_accessed=total, transcendentals=0),
        **options,
    )(*args)


def summaries_kernel(velocity_ref, basis_ref, kept_ref, sent_ref):
    side = lax.axis_index("group")
    half = basis_ref.shape[1]
    for part in range(2):
        rows = pl.ds(pl.multiple_of((side if part else 1 - side) * half, half), half)
        out = sent_ref if part else kept_ref
        for c in range(3):
            for plane in range(2):
                out[c, plane] = summary(basis_ref[...], velocity_ref[c, plane, rows])


def tendency_kernel(
    velocity_ref, peer_u, peer_v, peer_w, one_ref, other_u, other_v, other_w,
    kept_ref, peer_sum_ref, rows_high, rows_low, spread_ref, depth_high, depth_low,
    out_ref, field, sums, sems,
):
    side = lax.axis_index("group")
    half = rows_high.shape[1]
    step = pl.program_id(0)
    own_at, peer_at = (2 + 2 * side, 4 - 2 * side)
    one_at, other_at = (6 - 6 * side, 6 * side)

    @pl.when(step == 0)
    def _():
        rows = pl.ds(pl.multiple_of(side * half, half), half)
        copies = []
        peers, others = ((peer_u, peer_v, peer_w), (other_u, other_v, other_w))
        for c in range(3):
            for source, place in (
                (velocity_ref.at[c, :, rows], own_at),
                (peers[c], peer_at),
                (one_ref.at[c], one_at),
                (others[c], other_at),
            ):
                copies.append(
                    pltpu.make_async_copy(
                        source, field.at[c, pl.ds(place, 2)], sems.at[len(copies)]
                    )
                )
        for copy in copies:
            copy.start()
        sums[:, pl.ds(2 * side, 2)] = kept_ref[...]
        sums[:, pl.ds(2 - 2 * side, 2)] = peer_sum_ref[...]
        for copy in copies:
            copy.wait()

    u, v, w = (field[c, step + 2] for c in range(3))
    for c in range(3):
        value = field[c, step + 2]
        high, low = split(value)
        across = (
            dot(rows_high[...], high)
            + (dot(rows_high[...], low) + dot(rows_low[...], high))
            + dot(spread_ref[...], summary_operand(sums[c, step]))
        )
        along = dot(high, depth_high[...]) + (
            dot(low, depth_high[...]) + dot(high, depth_low[...])
        )
        width = value.shape[1]
        near = [field[c, step + k] for k in range(5)]
        advect = u * first_of(near) + v * across[:half] + w * along[:, :width]
        diffuse = second_of(near) + across[half:] + along[:, width:]
        out_ref[c, 0] = value + time_step * (viscosity * diffuse - advect)


def star_kernel(raw_ref, solid_own, solid_peer, basis_ref, low_u, high_u, star_v, star_w, sum_v, solid):
    side = lax.axis_index("group")
    solid[pl.ds(2 * side, 2)] = solid_own[...]
    solid[pl.ds(2 - 2 * side, 2)] = solid_peer[...]
    for plane in range(4):
        keep = 1.0 - solid[plane].astype(f32)
        out_u = low_u if plane < 2 else high_u
        out_u[plane % 2] = raw_ref[0, plane] * keep
        value = raw_ref[1, plane] * keep
        star_v[plane] = value
        sum_v[plane] = summary(basis_ref[...], value)
        star_w[plane] = raw_ref[2, plane] * keep


def cross_kernel(star_v, star_w, rows_high, rows_low, depth_high, depth_low, out_ref):
    half = rows_high.shape[1]
    out_ref[0] = dot_left(rows_high[:half], rows_low[:half], star_v[0]) + dot_right(
        star_w[0], depth_high[:, : star_w.shape[2]], depth_low[:, : star_w.shape[2]]
    )


def source_kernel(low_u, high_u, left_ref, right_ref, cross_ref, sum_ref, spread_ref, low_r, high_r, edge):
    half = cross_ref.shape[1]
    planes = [left_ref[0], left_ref[1], low_u[0], low_u[1], high_u[0], high_u[1], right_ref[0], right_ref[1]]
    for plane in range(4):
        value = (
            first_of(planes[plane : plane + 5])
            + cross_ref[plane]
            + dot(spread_ref[:half], summary_operand(sum_ref[plane]))
        )
        out = low_r if plane < 2 else high_r
        out[plane % 2] = value
        edge[plane, :HALO] = value[:HALO]
        edge[plane, HALO:] = value[half - HALO :]


def fine_kernel(
    pressure_ref, low_r, high_r, left_ref, right_ref, edge_ref, left_edge, right_edge, depth_pick, rows_pick,
    base_ref, source_ref, coarse_ref, one, two,
):
    half = low_r.shape[1]
    for plane in range(8):
        body, edge = (
            (left_ref, left_edge) if plane < 2 else
            (low_r, edge_ref) if plane < 4 else
            (high_r, edge_ref) if plane < 6 else (right_ref, right_edge)
        )
        at = plane - 2 if 2 <= plane < 6 else plane % 2
        source_ref[plane, HALO : HALO + half] = body[plane % 2]
        source_ref[plane, :HALO] = edge[at, HALO:]
        source_ref[plane, HALO + half :] = edge[at, :HALO]
    for k in range(8):
        centre = pressure_ref[k + 1]
        total = pressure_ref[k] + pressure_ref[k + 2] + cross_sum(centre)
        one[k] = centre + weight * (total - 6.0 * centre - source_ref[k])
    for k in range(6):
        centre = one[k + 1]
        total = one[k] + one[k + 2] + cross_sum(centre)
        two[k] = centre + weight * (total - 6.0 * centre - source_ref[k + 1])
    for pair in range(2):
        left = []
        for k in (2 * pair, 2 * pair + 1):
            centre = two[k + 1]
            total = two[k] + two[k + 2] + cross_sum(centre)
            residual = source_ref[k + 2] - (total - 6.0 * centre)
            base_ref[k] = centre - weight * residual
            left.append(residual)
        coarse_ref[pair] = 0.125 * pick_left(rows_pick[...], pick_right(left[0] + left[1], depth_pick[...]))


def middle_kernel(own_ref, left_ref, right_ref, depth_pick, rows_pick, base_ref, coarse_ref, one, two):
    source = [left_ref[0], left_ref[1], own_ref[0], own_ref[1], right_ref[0], right_ref[1]]
    for k in range(6):
        one[k] = (-4.0 * weight) * source[k]
    for k in range(4):
        centre = one[k + 1]
        total = one[k] + one[k + 2] + cross_sum(centre)
        two[k] = centre + weight * (total - 6.0 * centre - 4.0 * source[k + 1])
    left = []
    for k in range(2):
        centre = two[k + 1]
        total = two[k] + two[k + 2] + cross_sum(centre)
        residual = source[k + 2] - 0.25 * (total - 6.0 * centre)
        base_ref[k] = centre - (4.0 * weight) * residual
        left.append(residual)
    coarse_ref[...] = 0.125 * pick_left(rows_pick[...], pick_right(left[0] + left[1], depth_pick[...]))


def middle_base_kernel(base_ref, left_ref, right_ref, source_ref, out_ref):
    rows = out_ref.shape[1]
    planes = [left_ref[0], base_ref[0], base_ref[1], right_ref[0]]
    for k in range(2):
        centre = planes[k + 1]
        total = planes[k] + planes[k + 2] + cross_sum(centre)
        value = centre + weight * (total - 6.0 * centre - 4.0 * source_ref[k])
        out_ref[k] = value[HALO // 2 : HALO // 2 + rows]


def base_kernel(base_ref, left_ref, right_ref, source_ref, low_ref, high_ref):
    rows = low_ref.shape[1]
    for k in range(4):
        before = left_ref[0] if k == 0 else base_ref[k - 1]
        after = right_ref[0] if k == 3 else base_ref[k + 1]
        centre = base_ref[k]
        total = before + after + cross_sum(centre)
        value = centre + weight * (total - 6.0 * centre - source_ref[k + 2])
        out = low_ref if k < 2 else high_ref
        out[k % 2] = value[HALO : HALO + rows]


def stream_kernel(low_ref, high_ref, left_ref, right_ref, low_u, high_u, own_ref, sent_ref):
    side = lax.axis_index("group")
    planes = [left_ref[0], left_ref[1], low_ref[0], low_ref[1], high_ref[0], high_ref[1], right_ref[0], right_ref[1]]
    value = []
    for plane in range(4):
        star = (low_u if plane < 2 else high_u)[plane % 2]
        value.append(star - first_of(planes[plane : plane + 5]))

    @pl.when(side == 0)
    def _():
        for k in range(2):
            own_ref[k] = value[k]
            sent_ref[k] = value[2 + k]

    @pl.when(side == 1)
    def _():
        for k in range(2):
            own_ref[k] = value[2 + k]
            sent_ref[k] = value[k]


def final_kernel(
    coarse_ref, own_mid, left_mid, right_mid, low_base, high_base, peer_base, own_u, peer_u,
    star_v, peer_v, star_w, peer_w, solid_ref,
    sum_high, sum_low, diff_high, diff_low, depth_high, depth_low,
    mid_depth, mid_rows, fine_depth, fine_rows,
    out_ref, potential_ref, bottom, bottom_next, spread2, mid, mid_next, fine, first_sweep, delta, section,
):
    side = lax.axis_index("group")
    place = lax.axis_index("tunnel")
    count = coarse_ref.shape[0]
    half = own_u.shape[1]
    own_rows = pl.ds(pl.multiple_of(side * half, half), half)
    peer_rows = pl.ds(pl.multiple_of((1 - side) * half, half), half)
    for k in range(11):
        bottom[k] = (-16.0 * weight) * coarse_ref[lax.rem(place + (k + 2 * count - 5), count)]
    source_at, target = (bottom, bottom_next)
    for sweep_index in range(1, COARSE_SWEEPS):
        for k in range(sweep_index, 11 - sweep_index):
            centre = source_at[k]
            total = source_at[k - 1] + source_at[k + 1] + cross_sum(centre)
            right = coarse_ref[lax.rem(place + (k + 2 * count - 5), count)]
            target[k] = centre + weight * (total - 6.0 * centre - 16.0 * right)
        source_at, target = (target, source_at)
    for k in range(5):
        spread2[k] = pick_left(mid_rows[...], pick_right(source_at[k + 3], mid_depth[...]))
    for k in range(9):
        mid[k] = spread2[(side + k) // 2]
    for k in range(1, 8):
        centre = mid[k]
        total = mid[k - 1] + mid[k + 1] + cross_sum(centre)
        mid_next[k] = centre + weight * (total - 6.0 * centre)
    held = (left_mid, own_mid, right_mid)
    for k in range(6):
        mid[9 + k] = held[k // 2][k % 2]
    for k in range(2, 7):
        centre = mid_next[k]
        total = mid_next[k - 1] + mid_next[k + 1] + cross_sum(centre)
        value = mid[9 + side + (k - 2)] + centre + weight * (total - 6.0 * centre)
        fine[k - 2] = pick_left(fine_rows[...], pick_right(value, fine_depth[...]))
    for j in range(5):
        centre = fine[j]
        shared = centre + weight * (centre + cross_sum(centre) - 6.0 * centre)
        if j > 0:
            first_sweep[2 * j - 1] = shared + weight * fine[j - 1]
        if j < 4:
            first_sweep[2 * j] = shared + weight * fine[j + 1]
    for k in range(6):
        centre = first_sweep[k + 1]
        total = first_sweep[k] + first_sweep[k + 2] + cross_sum(centre)
        delta[k] = centre + weight * (total - 6.0 * centre)
    for k in range(4):
        base = (low_base if k < 2 else high_base)[k % 2]
        potential_ref[k] = base + delta[k + 2 - 2 * side, own_rows]
    for k in range(2):
        at = 2 + k
        section[peer_rows] = delta[at, peer_rows] + peer_base[k]
        section[own_rows] = potential_ref[2 * side + k]
        value = section[...]
        keep = 1.0 - solid_ref[k].astype(f32)
        out_ref[2, k, own_rows] = star_w[2 * side + k]
        out_ref[2, k, peer_rows] = peer_w[k]
        out_ref[2, k] = (out_ref[2, k] - dot_right(value, depth_high[...], depth_low[...])) * keep
        out_ref[1, k, own_rows] = star_v[2 * side + k]
        out_ref[1, k, peer_rows] = peer_v[k]
        top, low = (value[:half], value[half:])
        even = dot_left(sum_high[...], sum_low[...], top + low)
        odd = dot_left(diff_high[...], diff_low[...], top - low)
        out_ref[1, k, :half] = (out_ref[1, k, :half] - (even + odd)) * keep[:half]
        out_ref[1, k, half:] = (out_ref[1, k, half:] - (even - odd)) * keep[half:]
        out_ref[0, k, own_rows] = own_u[k]
        out_ref[0, k, peer_rows] = peer_u[k]
        gradient = first_of([delta[at + offset] for offset in range(-2, 3)])
        out_ref[0, k] = (out_ref[0, k] - gradient) * keep


def pair_sums(fine, coarse):
    return (np.arange(fine)[:, None] // 2 == np.arange(coarse)[None, :]).astype(ml_dtypes.bfloat16)


def paired(velocity, obstacle, pressure):
    rows, depth = velocity.shape[2:]
    half = rows // 2
    wide = half + 2 * HALO
    tunnel_size = lax.axis_size("tunnel")
    side = lax.axis_index("group")
    both = ("tunnel", "group")
    own, spread, basis, rows_first = half_tables(rows)
    depth_first, depth_second = wave_tables(depth)
    rows_high, rows_low = high_low(own)
    spread_high, spread_low = high_low(spread)
    spread_all = np.concatenate([spread_high, spread_high, spread_low, np.zeros_like(spread_low)], axis=1)
    basis_both = np.concatenate(high_low(basis), axis=0)
    depth_high, depth_low = high_low(np.concatenate([depth_first.T, depth_second.T], axis=1))
    sum_high, sum_low = high_low((rows_first[:half, :half] + rows_first[:half, half:]) / 2.0)
    diff_high, diff_low = high_low((rows_first[:half, :half] - rows_first[:half, half:]) / 2.0)

    def swap(value):
        return lax.ppermute(value, "group", [(0, 1), (1, 0)])

    def forward(value):
        return lax.ppermute(value, "tunnel", [(i, (i + 1) % tunnel_size) for i in range(tunnel_size)])

    def backward(value):
        return lax.ppermute(value, "tunnel", [((i + 1) % tunnel_size, i) for i in range(tunnel_size)])

    own_way, swapped_way = ([], [])
    for i in range(tunnel_size):
        ahead, behind = ((i + 1) % tunnel_size, (i - 1) % tunnel_size)
        own_way += [(2 * i + 1, 2 * ahead + 1), (2 * i, 2 * behind)]
        swapped_way += [(2 * i, 2 * ahead), (2 * i + 1, 2 * behind + 1)]

    def half_of(value, which, axis):
        return lax.dynamic_slice_in_dim(value, which * half, half, axis=axis)

    def pair_of(value, which):
        return lax.dynamic_slice_in_dim(value, 2 * which, 2, axis=0)

    plane = (half, depth)
    peers, others = ([], [])
    for c in range(3):
        peers.append(swap(half_of(velocity[c], 1 - side, 1)))
    one = lax.ppermute(half_of(velocity, side, 2), both, own_way)
    for c in range(3):
        others.append(lax.ppermute(peers[c], both, swapped_way))
    kept_sum, sent_sum = kernel_call(
        summaries_kernel, [(3, 2, 8, depth)] * 2, [], [VMEM] * 2, 10**8, velocity, basis_both
    )
    peer_sum = swap(sent_sum)
    solid_peer = swap(half_of(obstacle, 1 - side, 1))

    edge = swap(jnp.concatenate([pressure[:, :HALO], pressure[:, half - HALO :]], axis=1))
    tall = jnp.concatenate([edge[:, HALO:], pressure, edge[:, :HALO]], axis=1)
    pressure_wide = jnp.concatenate([forward(tall[1:]), tall, backward(tall[:3])], axis=0)

    full = lambda shape: pl.BlockSpec(shape, lambda i: (0,) * len(shape))
    (raw,) = kernel_call(
        tendency_kernel,
        [(3, 4) + plane],
        [
            pltpu.VMEM((3, 8) + plane, f32),
            pltpu.VMEM((3, 4, 8, depth), f32),
            pltpu.SemaphoreType.DMA((12,)),
        ],
        [ANY] * 8 + [full((3, 2, 8, depth))] * 2
        + [full(rows_high.shape)] * 2 + [full(spread_all.shape)] + [full(depth_high.shape)] * 2,
        6 * 10**9,
        velocity, *peers, one, *others, kept_sum, peer_sum, rows_high, rows_low, spread_all, depth_high, depth_low,
        grid=(4,),
        out_specs=[pl.BlockSpec((3, 1) + plane, lambda i: (0, i, 0, 0))],
    )
    two_planes, four_planes = ((2,) + plane, (4,) + plane)
    low_u, high_u, star_v, star_w, sum_v = kernel_call(
        star_kernel,
        [two_planes, two_planes, four_planes, four_planes, (4, 8, depth)],
        [pltpu.VMEM(four_planes, jnp.int32)],
        [VMEM] * 4,
        10**8,
        raw, half_of(obstacle, side, 1), solid_peer, basis_both,
    )
    left_u, right_u = (forward(high_u), backward(low_u))
    peer_sum_v = swap(sum_v)
    by_plane = pl.BlockSpec((1,) + plane, lambda i: (i, 0, 0))
    (cross,) = kernel_call(
        cross_kernel,
        [four_planes],
        [],
        [by_plane] * 2 + [full(rows_high.shape)] * 2 + [full(depth_high.shape)] * 2,
        10**9,
        star_v, star_w, rows_high, rows_low, depth_high, depth_low,
        grid=(4,),
        out_specs=[by_plane],
    )
    low_r, high_r, edge_r = kernel_call(
        source_kernel,
        [two_planes, two_planes, (4, 2 * HALO, depth)],
        [],
        [VMEM] * 7,
        10**8,
        low_u, high_u, left_u, right_u, cross, peer_sum_v, spread_all,
    )
    edges = swap(edge_r)
    left_r, right_r = (forward(high_r), backward(low_r))
    left_edge, right_edge = (forward(edges[2:]), backward(edges[:2]))
    peer_v, peer_w = (swap(pair_of(star_v, 1 - side)), swap(pair_of(star_w, 1 - side)))

    mid_rows, mid_depth = (wide // 2, depth // 2)
    base_one, source_wide, mid_source = kernel_call(
        fine_kernel,
        [(4, wide, depth), (8, wide, depth), (2, mid_rows, mid_depth)],
        [pltpu.VMEM((8, wide, depth), f32), pltpu.VMEM((6, wide, depth), f32)],
        [VMEM] * 10,
        10**8,
        pressure_wide, low_r, high_r, left_r, right_r, edges, left_edge, right_edge,
        pair_sums(depth, mid_depth), pair_sums(wide, mid_rows).T,
    )
    left_mid, right_mid = (forward(mid_source), backward(mid_source))
    low_depth = mid_depth // 2
    twice = np.concatenate([pair_sums(mid_depth, low_depth)] * 2, axis=1)
    own_pairs = pair_sums(half // 2, half // 4).T
    own_pairs = np.pad(own_pairs, ((0, 0), (HALO // 2, HALO // 2)))
    mid_one, low_source = kernel_call(
        middle_kernel,
        [(2, mid_rows, mid_depth), (half // 4, mid_depth)],
        [pltpu.VMEM((6, mid_rows, mid_depth), f32), pltpu.VMEM((4, mid_rows, mid_depth), f32)],
        [VMEM] * 5,
        10**8,
        mid_source, left_mid, right_mid, twice, own_pairs,
    )
    low_all = lax.all_gather(low_source, both)
    low_all = low_all.reshape(tunnel_size, half // 2, mid_depth)
    left_one, right_one = (forward(mid_one[1:]), backward(mid_one[:1]))
    (mid_base,) = kernel_call(
        middle_base_kernel,
        [(2, half // 2, mid_depth)],
        [],
        [VMEM] * 4,
        10**7,
        mid_one, left_one, right_one, mid_source,
    )
    other_mid = swap(mid_base)
    mid_base = jnp.where(
        side == 0,
        jnp.concatenate([mid_base, other_mid], axis=1),
        jnp.concatenate([other_mid, mid_base], axis=1),
    )
    left_mid, right_mid = (forward(mid_base), backward(mid_base))

    left_base, right_base = (forward(base_one[3:]), backward(base_one[:1]))
    low_base, high_base = kernel_call(
        base_kernel,
        [two_planes, two_planes],
        [],
        [VMEM] * 4,
        10**8,
        base_one, left_base, right_base, source_wide,
    )
    peer_base = swap(jnp.where(side == 0, high_base, low_base))
    left_b, right_b = (forward(high_base), backward(low_base))
    own_u, sent_u = kernel_call(
        stream_kernel,
        [two_planes, two_planes],
        [],
        [VMEM] * 6,
        10**8,
        low_base, high_base, left_b, right_b, low_u, high_u,
    )
    peer_u = swap(sent_u)
    low_plane = (half // 2, mid_depth)
    mid_plane = (half, mid_depth)
    fine_plane = (rows, depth)
    expand_low = np.zeros((mid_depth, mid_depth), ml_dtypes.bfloat16)
    expand_low[:low_depth] = pair_sums(mid_depth, low_depth).T
    return kernel_call(
        final_kernel,
        [(3, 2) + fine_plane, four_planes],
        [
            pltpu.VMEM((11,) + low_plane, f32),
            pltpu.VMEM((11,) + low_plane, f32),
            pltpu.VMEM((5,) + mid_plane, f32),
            pltpu.VMEM((15,) + mid_plane, f32),
            pltpu.VMEM((9,) + mid_plane, f32),
            pltpu.VMEM((5,) + fine_plane, f32),
            pltpu.VMEM((8,) + fine_plane, f32),
            pltpu.VMEM((6,) + fine_plane, f32),
            pltpu.VMEM(fine_plane, f32),
        ],
        [VMEM] * 24,
        10**9,
        low_all, mid_base, left_mid, right_mid, low_base, high_base, peer_base, own_u, peer_u,
        star_v, peer_v, star_w, peer_w, obstacle,
        sum_high, sum_low, diff_high, diff_low,
        np.ascontiguousarray(depth_high[:, :depth]), np.ascontiguousarray(depth_low[:, :depth]),
        expand_low, pair_sums(half, half // 2),
        np.ascontiguousarray(pair_sums(depth, mid_depth).T), pair_sums(rows, half),
    )


def step(velocity, obstacle, pressure):
    planes, rows, depth = velocity.shape[1:]
    fits = lax.axis_size("group") == 2 and planes == 2 and pressure.shape[0] == 4
    fits = fits and lax.axis_size("tunnel") > 10 and rows % 512 == 0 and depth % 256 == 0
    if fits:
        return tuple(paired(velocity, obstacle, pressure))
    return local(velocity, obstacle, pressure)


def solution(mesh):
    in_specs = (
        P(None, ("tunnel", "group"), None, None),
        P(("tunnel", "group"), None, None),
        P("tunnel", "group", None),
    )
    out_specs = (P(None, ("tunnel", "group"), None, None), P("tunnel", "group", None))
    return jax.shard_map(step, mesh=mesh, in_specs=in_specs, out_specs=out_specs, check_vma=False)
```

```python
import functools
import math

import jax
import jax.numpy as jnp
import ml_dtypes
import numpy as np
from jax import lax
from jax.experimental import pallas as pl
from jax.experimental.pallas import tpu as pltpu
from jax.sharding import PartitionSpec as P

LEVELS = 3
SWEEPS = 2
COARSE_SWEEPS = 4


time_step = 0.1
viscosity = 0.05
relax_weight = 0.8
highest = lax.Precision.HIGHEST


def extended(value, sides, width):
    for axis, dim in sides:
        size, length = (lax.axis_size(axis), value.shape[dim])
        up = [(i, (i + 1) % size) for i in range(size)]
        down = [(j, i) for i, j in up]
        last = lax.slice_in_dim(value, length - width, length, axis=dim)
        initial = lax.slice_in_dim(value, 0, width, axis=dim)
        before = lax.ppermute(last, axis, up)
        after = lax.ppermute(initial, axis, down)
        value = jnp.concatenate([before, value, after], axis=dim)
    return value


def compact_tables(count):
    indices = jnp.arange(count, dtype=jnp.int32)
    product = indices[:, None] * indices[None, :] % count
    angles = product.astype(jnp.float32) * (2.0 * math.pi / count)
    cosines = jnp.cos(angles)
    sines = jnp.sin(angles)
    theta = indices.astype(jnp.float32) * (2.0 * math.pi / count)
    first_wave = (14.0 / 9.0 * jnp.sin(theta) + jnp.sin(2.0 * theta) / 18.0) / (
        1.0 + 2.0 / 3.0 * jnp.cos(theta)
    )
    second_wave = (
        24.0 / 11.0 * (1.0 - jnp.cos(theta)) + 3.0 / 22.0 * (1.0 - jnp.cos(2.0 * theta))
    ) / (1.0 + 4.0 / 11.0 * jnp.cos(theta))
    first_matrix = (
        jnp.dot(cosines * first_wave, sines.T, precision=highest)
        - jnp.dot(sines * first_wave, cosines.T, precision=highest)
    ) / count
    second_matrix = (
        -(
            jnp.dot(cosines * second_wave, cosines.T, precision=highest)
            + jnp.dot(sines * second_wave, sines.T, precision=highest)
        )
        / count
    )
    return (first_matrix, second_matrix)


def along_rows(matrix, field):
    return jnp.einsum("ij,...jz->...iz", matrix, field, precision=highest)


def along_depth(matrix, field):
    return jnp.einsum("...j,ij->...i", field, matrix, precision=highest)


def shifted(padded, offset, axis):
    count = padded.shape[axis] - 4
    return lax.slice_in_dim(padded, 2 + offset, 2 + offset + count, axis=axis)


def stream_first(padded, axis):
    ahead = shifted(padded, 1, axis) - shifted(padded, -1, axis)
    further = shifted(padded, 2, axis) - shifted(padded, -2, axis)
    return (8.0 * ahead - further) / 12.0


def stream_second(padded, axis):
    ahead = shifted(padded, 1, axis) + shifted(padded, -1, axis)
    further = shifted(padded, 2, axis) + shifted(padded, -2, axis)
    return (16.0 * ahead - further - 30.0 * shifted(padded, 0, axis)) / 12.0


def padded_neighbours(padded):
    interior = padded[1:-1, 1:-1]
    total = padded[2:, 1:-1] + padded[:-2, 1:-1]
    total = total + padded[1:-1, 2:] + padded[1:-1, :-2]
    return total + jnp.roll(interior, -1, 2) + jnp.roll(interior, 1, 2)


def relax_padded(padded, source_term, scale):
    interior = padded[1:-1, 1:-1]
    return interior + relax_weight / 6.0 * (
        padded_neighbours(padded) - 6.0 * interior - scale * source_term
    )


def faces(field):
    return extended(field, (("tunnel", 0), ("group", 1)), 1)


def thin_sweeps(field, source_term, scale, count):
    for sweep_index in range(count):
        field = relax_padded(faces(field), source_term, scale)
    return field


def smooth(field, source_term, scale, level):
    if level == 0:
        return thin_sweeps(field, source_term, scale, SWEEPS)
    return thin_sweeps(field, source_term, scale, SWEEPS)


def coarsest(source_term, scale):
    return thin_sweeps(jnp.zeros_like(source_term), source_term, scale, COARSE_SWEEPS)


def restrict(field):
    planes, rows, depth = field.shape
    blocks = field.reshape(planes // 2, 2, rows // 2, 2, depth // 2, 2)
    return jnp.sum(blocks, axis=(1, 3, 5)) * 0.125


def prolong(field):
    return jnp.repeat(jnp.repeat(jnp.repeat(field, 2, 0), 2, 1), 2, 2)


def cycle(field, source_term, level):
    scale = 4.0**level
    if level == LEVELS - 1:
        return coarsest(source_term, scale)
    field = smooth(field, source_term, scale, level)
    leftover = source_term - (padded_neighbours(faces(field)) - 6.0 * field) / scale
    coarse_source = restrict(leftover)
    coarse = cycle(jnp.zeros_like(coarse_source), coarse_source, level + 1)
    field = field + prolong(coarse)
    return smooth(field, source_term, scale, level)


def local(velocity, obstacle, pressure):
    row_count = velocity.shape[2]
    depth_count = velocity.shape[3]
    rows_first, rows_second = compact_tables(row_count)
    depth_first, depth_second = compact_tables(depth_count)
    rows_both = jnp.concatenate([rows_first, rows_second], axis=0)
    depth_both = jnp.concatenate([depth_first, depth_second], axis=0)
    keep = 1.0 - obstacle.astype(jnp.float32)
    row_terms = along_rows(rows_both, velocity)
    depth_terms = along_depth(depth_both, velocity)
    transverse = (
        velocity[1] * row_terms[:, :, :row_count] + velocity[2] * depth_terms[..., :depth_count]
    )
    diffusion = row_terms[:, :, row_count:] + depth_terms[..., depth_count:]
    padded = extended(velocity, ((("tunnel", "group"), 1),), 2)
    streamwise = -velocity[0] * stream_first(padded, 1) + viscosity * stream_second(padded, 1)
    tendency = streamwise - transverse + viscosity * diffusion
    star = (velocity + time_step * tendency) * keep
    star_padded = extended(star[0], ((("tunnel", "group"), 0),), 2)
    source = (
        stream_first(star_padded, 0)
        + along_rows(rows_first, star[1])
        + along_depth(depth_first, star[2])
    )
    source_tile = lax.all_to_all(source, "group", split_axis=1, concat_axis=0, tiled=True)
    potential = cycle(pressure, source_tile, 0)
    potential_padded = extended(potential, (("tunnel", 0),), 2)
    streamwise_grad = stream_first(potential_padded, 0)
    returned = lax.all_to_all(
        jnp.stack([potential, streamwise_grad]), "group", split_axis=1, concat_axis=2, tiled=True
    )
    gradient = jnp.stack(
        [returned[1], along_rows(rows_first, returned[0]), along_depth(depth_first, returned[0])]
    )
    corrected = (star - gradient) * keep
    return (corrected, potential)


HALO = 16
weight = relax_weight / 6.0
bf16 = jnp.bfloat16
f32 = jnp.float32
VMEM = pl.BlockSpec(memory_space=pltpu.VMEM)
ANY = pl.BlockSpec(memory_space=pl.ANY)


def wave_tables(count):
    index = np.arange(count)
    angles = 2.0 * np.pi * (np.outer(index, index) % count) / count
    theta = 2.0 * np.pi * index / count
    first_wave = (14.0 / 9.0 * np.sin(theta) + np.sin(2.0 * theta) / 18.0) / (
        1.0 + 2.0 / 3.0 * np.cos(theta)
    )
    second_wave = (
        24.0 / 11.0 * (1.0 - np.cos(theta)) + 3.0 / 22.0 * (1.0 - np.cos(2.0 * theta))
    ) / (1.0 + 4.0 / 11.0 * np.cos(theta))
    cosines, sines = (np.cos(angles), np.sin(angles))
    first = ((cosines * first_wave) @ sines.T - (sines * first_wave) @ cosines.T) / count
    second = -((cosines * second_wave) @ cosines.T + (sines * second_wave) @ sines.T) / count
    return (first, second)


def high_low(table):
    high = table.astype(np.float32).astype(ml_dtypes.bfloat16)
    low = (table - high.astype(np.float64)).astype(np.float32).astype(ml_dtypes.bfloat16)
    return (high, low)


def half_tables(count):
    first, second = wave_tables(count)
    half = count // 2
    index = np.arange(half)
    root_first = (math.sqrt(5.0) - 3.0) / 2.0
    root_second = (math.sqrt(105.0) - 11.0) / 4.0
    basis = np.zeros((8, half))
    basis[0, 0] = 1.0
    basis[1, -1] = 1.0
    basis[2] = root_first**index
    basis[3] = basis[2][::-1]
    basis[4] = root_second**index
    basis[5] = basis[4][::-1]
    spread = []
    for table, used in ((first, (0, 1, 2, 3)), (second, (0, 1, 4, 5))):
        solved = np.linalg.lstsq(basis[list(used)].T, table[:half, half:].T, rcond=None)[0].T
        wide = np.zeros((half, 8))
        wide[:, list(used)] = solved
        spread.append(wide)
    own = np.concatenate([first[:half, :half], second[:half, :half]], axis=0)
    return (own, np.concatenate(spread, axis=0), basis, first)


def split(value):
    high = value.astype(bf16)
    low = (value - high.astype(f32)).astype(bf16)
    return (high, low)


def dot(left, right):
    return jnp.dot(left, right, preferred_element_type=f32)


def dot_left(table_high, table_low, value):
    high, low = split(value)
    return dot(table_high, high) + (dot(table_high, low) + dot(table_low, high))


def dot_right(value, table_high, table_low):
    high, low = split(value)
    return dot(high, table_high) + (dot(low, table_high) + dot(high, table_low))


def pick_left(zero_one, value):
    high, low = split(value)
    return dot(zero_one, high) + dot(zero_one, low)


def pick_right(value, zero_one):
    high, low = split(value)
    return dot(high, zero_one) + dot(low, zero_one)


def summary(basis_both, value):
    high, low = split(value)
    main = dot(basis_both, high)
    rest = dot(basis_both, low)
    return main[:8] + main[8:] + rest[:8]


def summary_operand(value):
    high = value.astype(bf16).astype(f32)
    return jnp.concatenate([high, value - high, high, jnp.zeros_like(high)], axis=0).astype(bf16)


def turn(value, shift, axis):
    return pltpu.roll(value, shift % value.shape[axis], axis)


def cross_sum(value):
    return (turn(value, 1, 0) + turn(value, -1, 0)) + (turn(value, 1, 1) + turn(value, -1, 1))


def first_of(values):
    return (8.0 * (values[3] - values[1]) - (values[4] - values[0])) * (1.0 / 12.0)


def second_of(values):
    return (
        16.0 * (values[3] + values[1]) - (values[4] + values[0]) - 30.0 * values[2]
    ) * (1.0 / 12.0)


def kernel_call(body, outs, scratch, specs, flops, *args, grid=None, out_specs=None, aliases=None):
    total = sum(math.prod(a.shape) * a.dtype.itemsize for a in args)
    total += sum(4 * math.prod(s) for s in outs)
    options = {} if grid is None else {"grid": grid}
    if aliases is not None:
        options["input_output_aliases"] = aliases
    return pl.pallas_call(
        body,
        out_shape=[jax.ShapeDtypeStruct(s, f32) for s in outs],
        in_specs=specs,
        out_specs=[VMEM] * len(outs) if out_specs is None else out_specs,
        scratch_shapes=scratch,
        compiler_params=pltpu.CompilerParams(vmem_limit_bytes=56 * 1024 * 1024),
        cost_estimate=pl.CostEstimate(flops=flops, bytes_accessed=total if flops > 1 else 1, transcendentals=0),
        **options,
    )(*args)


def mirror(side, index, count):
    return index + side * (count - 1 - 2 * index)


def sign_of(side):
    return (1 - 2 * side).astype(f32)


def transverse(u, v, w, value, other_sum, rows_high, rows_low, spread, depth_high, depth_low):
    half, width = value.shape
    high, low = split(value)
    across = (
        dot(rows_high[...], high)
        + (dot(rows_high[...], low) + dot(rows_low[...], high))
        + dot(spread[...], summary_operand(other_sum))
    )
    along = dot(high, depth_high[...]) + (dot(low, depth_high[...]) + dot(high, depth_low[...]))
    advect = v * across[:half] + w * along[:, :width]
    return value + time_step * (viscosity * (across[half:] + along[:, width:]) - advect)


def own_planes_kernel(
    velocity_ref, basis_ref, rows_high, rows_low, spread, depth_high, depth_low, out_ref, sent_ref
):
    side = lax.axis_index("group")
    half = basis_ref.shape[1]
    own = pl.ds(pl.multiple_of(side * half, half), half)
    other = pl.ds(pl.multiple_of((1 - side) * half, half), half)
    u, v, w = (velocity_ref[c, 0, own] for c in range(3))
    sent_ref[0, :half] = velocity_ref[2, 0, other]
    for c in range(3):
        value = velocity_ref[c, 0, own]
        kept = summary(basis_ref[...], velocity_ref[c, 0, other])
        sent_ref[0, half + 8 * c : half + 8 * c + 8] = summary(basis_ref[...], value)
        out_ref[c, 0] = transverse(u, v, w, value, kept, rows_high, rows_low, spread, depth_high, depth_low)


def peer_planes_kernel(
    uv_ref, w_ref, rows_high, rows_low, spread, depth_high, depth_low, out_ref
):
    half = uv_ref.shape[2]
    u, v, w = (uv_ref[0, 0], uv_ref[1, 0], w_ref[0, :half])
    for c in range(3):
        other_sum = w_ref[0, half + 8 * c : half + 8 * c + 8]
        out_ref[c, 0] = transverse(
            u, v, w, (u, v, w)[c], other_sum, rows_high, rows_low, spread, depth_high, depth_low
        )


def star_planes(side, planes, raws, solids, u_of, outs):
    sign = sign_of(side) * (time_step / 12.0)
    for plane in range(4):
        index = mirror(side, plane % 2, 2)
        keep = 1.0 - solids[plane // 2][index].astype(f32)
        near = planes[plane : plane + 5]
        first = 8.0 * (near[3] - near[1]) - (near[4] - near[0])
        second = 16.0 * (near[3] + near[1]) - (near[4] + near[0]) - 30.0 * near[2]
        raw = raws[plane // 2][index]
        outs[plane // 2][plane % 2] = (
            raw + (time_step * viscosity / 12.0) * second - (u_of(plane) * sign) * first
        ) * keep


def eight(side, groups):
    return [group[mirror(side, k, 2)] for group in groups for k in range(2)]


def star_u_kernel(raw_own, raw_peer, own_ref, one_ref, peers, others, solid_own, solid_peer, near_ref, far_ref):
    side = lax.axis_index("group")
    planes = eight(side, (others.at[0], own_ref.at[0], peers.at[0], one_ref.at[0]))
    star_planes(
        side, planes, (raw_own.at[0], raw_peer.at[0]), (solid_own, solid_peer),
        lambda plane: planes[plane + 2], (near_ref, far_ref),
    )


def star_vw_kernel(
    raw_own, raw_peer, own_ref, one_ref, peers, peer_w, others, other_w, solid_own, solid_peer, basis_ref,
    near_v, far_v, near_w, far_w, sum_ref,
):
    side = lax.axis_index("group")
    step = pl.program_id(0)

    def u_of(plane):
        return (own_ref if plane < 2 else peers)[0, mirror(side, plane % 2, 2)]

    for c, peer, other, outs in (
        (1, peers.at[1], others.at[0], (near_v, far_v)),
        (2, peer_w, other_w, (near_w, far_w)),
    ):
        planes = eight(side, (other, own_ref.at[c], peer, one_ref.at[c]))
        star_planes(side, planes, (raw_own.at[c], raw_peer.at[c]), (solid_own, solid_peer), u_of, outs)

    @pl.when(step == 0)
    def _():
        sum_ref[...] = jnp.zeros_like(sum_ref)

    for plane in range(4):
        sum_ref[plane] += summary(basis_ref[0], (near_v if plane < 2 else far_v)[plane % 2])


def cross_kernel(near_v, far_v, near_w, far_w, rows_high, rows_low, depth_high, depth_low, out_ref):
    half = near_v.shape[1]
    for plane in range(4):
        v, w = ((near_v, near_w) if plane < 2 else (far_v, far_w))
        out_ref[plane] = dot_left(rows_high[:half], rows_low[:half], v[plane % 2]) + dot_right(
            w[plane % 2], depth_high[...], depth_low[...]
        )


def source_kernel(
    near_u, far_u, left_ref, right_ref, cross_ref, sum_ref, spread, near_r, far_r, head, tail
):
    sign = sign_of(lax.axis_index("group"))
    rows = cross_ref.shape[1]
    step = pl.program_id(0)
    planes = [ref[k] for ref in (left_ref, near_u, far_u, right_ref) for k in range(2)]
    values = []
    for plane in range(4):
        value = sign * first_of(planes[plane : plane + 5]) + cross_ref[plane]
        value = value + dot(spread[...], summary_operand(sum_ref[3 - plane]))
        (near_r if plane < 2 else far_r)[plane % 2] = value
        values.append(value)

    @pl.when(step == 0)
    def _():
        for plane in range(4):
            head[plane] = values[plane][:HALO]

    @pl.when(step == pl.num_programs(0) - 1)
    def _():
        for plane in range(4):
            tail[plane] = values[plane][rows - HALO :]


def fine_kernel(
    pressure_tall, pressure_left, pressure_right,
    near_r, far_r, left_ref, right_ref, edge_ref, left_edge, right_edge, depth_pick, rows_pick,
    base_ref, coarse_ref, ahead_ref, behind_ref, source_ref, pressure_ref, one, two,
):
    side = lax.axis_index("group")
    half = near_r.shape[1]

    def fill(target, at, body, edge):
        target[at, HALO : HALO + half] = body
        target[at, :HALO] = edge[HALO:]
        target[at, HALO + half :] = edge[:HALO]

    for plane in range(2):
        fill(source_ref, plane, left_ref[plane], left_edge[1 - plane])
        fill(source_ref, 2 + plane, near_r[plane], edge_ref[3 - plane])
        fill(source_ref, 4 + plane, far_r[plane], edge_ref[1 - plane])
        fill(source_ref, 6 + plane, right_ref[plane], right_edge[1 - plane])
    for plane in range(3):
        at = mirror(side, plane, 3)
        pressure_ref[plane] = pressure_left[at]
        pressure_ref[7 + plane] = pressure_right[at]
    for plane in range(4):
        pressure_ref[3 + plane] = pressure_tall[mirror(side, plane, 4)]
    for k in range(8):
        centre = pressure_ref[k + 1]
        total = pressure_ref[k] + pressure_ref[k + 2] + cross_sum(centre)
        one[k] = centre + weight * (total - 6.0 * centre - source_ref[k])
    for k in range(6):
        centre = one[k + 1]
        total = one[k] + one[k + 2] + cross_sum(centre)
        two[k] = centre + weight * (total - 6.0 * centre - source_ref[k + 1])
    for pair in range(2):
        left = []
        for k in (2 * pair, 2 * pair + 1):
            centre = two[k + 1]
            total = two[k] + two[k + 2] + cross_sum(centre)
            residual = source_ref[k + 2] - (total - 6.0 * centre)
            base_ref[k] = centre - weight * residual
            left.append(residual)
        coarse = 0.125 * pick_left(rows_pick[...], pick_right(left[0] + left[1], depth_pick[...]))
        coarse_ref[pair] = coarse
        rows, width = coarse.shape
        ahead_ref[:rows, width * pair : width * (pair + 1)] = coarse
        behind_ref[:rows, width * pair : width * (pair + 1)] = coarse
    ahead_ref[rows:] = base_ref[3]
    behind_ref[rows:] = base_ref[0]


def middle_kernel(own_ref, left_ref, right_ref, depth_pick, rows_pick, base_ref, coarse_ref, one, two):
    rows, width = own_ref.shape[1:]
    source = []
    for ref in (left_ref, own_ref, right_ref):
        for k in range(2):
            source.append(ref[k] if ref is own_ref else ref[:rows, width * k : width * (k + 1)])
    for k in range(6):
        one[k] = (-4.0 * weight) * source[k]
    for k in range(4):
        centre = one[k + 1]
        total = one[k] + one[k + 2] + cross_sum(centre)
        two[k] = centre + weight * (total - 6.0 * centre - 4.0 * source[k + 1])
    left = []
    for k in range(2):
        centre = two[k + 1]
        total = two[k] + two[k + 2] + cross_sum(centre)
        residual = source[k + 2] - 0.25 * (total - 6.0 * centre)
        base_ref[k] = centre - (4.0 * weight) * residual
        left.append(residual)
    width = own_ref.shape[2]
    wide = pick_right(left[0] + left[1], depth_pick[...])
    count = coarse_ref.shape[0]
    coarse_ref[...] = 0.125 * (
        pick_left(rows_pick[:count], wide[:, :width]) + pick_left(rows_pick[count:], wide[:, width:])
    )


def middle_base_kernel(base_ref, left_ref, right_ref, source_ref, out_ref):
    rows = out_ref.shape[1]
    planes = [left_ref[0], base_ref[0], base_ref[1], right_ref[0]]
    for k in range(2):
        centre = planes[k + 1]
        total = planes[k] + planes[k + 2] + cross_sum(centre)
        value = centre + weight * (total - 6.0 * centre - 4.0 * source_ref[k])
        out_ref[k] = value[HALO // 2 : HALO // 2 + rows]


def base_kernel(base_ref, left_ref, right_ref, near_r, far_r, near_ref, far_ref):
    rows = near_ref.shape[1]
    skip = left_ref.shape[0] - base_ref.shape[1]
    for k in range(4):
        before = left_ref[skip:] if k == 0 else base_ref[k - 1]
        after = right_ref[skip:] if k == 3 else base_ref[k + 1]
        centre = base_ref[k]
        total = before + after + cross_sum(centre)
        value = (centre + weight * (total - 6.0 * centre))[HALO : HALO + rows]
        source, out = ((near_r, near_ref) if k < 2 else (far_r, far_ref))
        out[k % 2] = value - weight * source[k % 2]


def stream_kernel(near_ref, far_ref, left_ref, right_ref, near_u, far_u, own_ref, sent_ref):
    sign = sign_of(lax.axis_index("group"))
    planes = [ref[k] for ref in (left_ref, near_ref, far_ref, right_ref) for k in range(2)]
    for plane in range(4):
        star = (near_u if plane < 2 else far_u)[plane % 2]
        (own_ref if plane < 2 else sent_ref)[plane % 2] = star - sign * first_of(planes[plane : plane + 5])


def coarsest_kernel(all_ref, mid_depth, mid_rows, out_ref, source, one, two):
    place = lax.axis_index("tunnel")
    step = 1 - 2 * lax.axis_index("group")
    count = all_ref.shape[0] // 2
    quarter, width = all_ref.shape[1:]
    lower = lax.broadcasted_iota(jnp.int32, (quarter, width), 1) < width // 2
    for k in range(11):
        plane = lax.rem(place + step * (k - 5) + 2 * count, count)
        for part in range(2):
            packed = all_ref[2 * plane + part]
            turned = turn(packed, width // 2, 1)
            source[k, 2 * part * quarter : (2 * part + 1) * quarter] = jnp.where(lower, packed, turned)
            source[k, (2 * part + 1) * quarter : (2 * part + 2) * quarter] = jnp.where(lower, turned, packed)
    for k in range(11):
        one[k] = (-16.0 * weight) * source[k]
    source_at, target = (one, two)
    for sweep_index in range(1, COARSE_SWEEPS):
        for k in range(sweep_index, 11 - sweep_index):
            centre = source_at[k]
            total = source_at[k - 1] + source_at[k + 1] + cross_sum(centre)
            target[k] = centre + weight * (total - 6.0 * centre - 16.0 * source[k])
        source_at, target = (target, source_at)
    for k in range(5):
        out_ref[k] = pick_left(mid_rows[...], pick_right(source_at[k + 3], mid_depth[...]))


def correction_kernel(
    spread_ref, own_mid, left_mid, right_mid,
    near_base, far_base, peer_base, near_v, near_w, peer_vw, solid_ref,
    sum_high, sum_low, diff_high, diff_low, depth_high, depth_low, fine_depth, fine_rows,
    out_ref, potential_ref, base, mid, fine, first_sweep, delta, section,
):
    side = lax.axis_index("group")
    sign = sign_of(side)
    half = near_v.shape[1]
    own_rows = pl.ds(pl.multiple_of(side * half, half), half)
    peer_rows = pl.ds(pl.multiple_of((1 - side) * half, half), half)
    mid_half = own_mid.shape[2]
    own_mid_rows = pl.ds(pl.multiple_of(side * mid_half, mid_half), mid_half)
    peer_mid_rows = pl.ds(pl.multiple_of((1 - side) * mid_half, mid_half), mid_half)
    for k in range(5):
        held = (left_mid, own_mid, right_mid)[k // 2]
        base[k, own_mid_rows] = held[0, k % 2]
        base[k, peer_mid_rows] = held[1, 1 - k % 2]
    for k in range(1, 8):
        centre = spread_ref[k // 2]
        total = spread_ref[(k - 1) // 2] + spread_ref[(k + 1) // 2] + cross_sum(centre)
        mid[k] = centre + weight * (total - 6.0 * centre)
    for k in range(5):
        centre = mid[k + 2]
        total = mid[k + 1] + mid[k + 3] + cross_sum(centre)
        value = base[k] + centre + weight * (total - 6.0 * centre)
        fine[k] = pick_left(fine_rows[...], pick_right(value, fine_depth[...]))
    for j in range(5):
        centre = fine[j]
        shared = centre + weight * (centre + cross_sum(centre) - 6.0 * centre)
        if j > 0:
            first_sweep[2 * j - 1] = shared + weight * fine[j - 1]
        if j < 4:
            first_sweep[2 * j] = shared + weight * fine[j + 1]
    for k in range(6):
        centre = first_sweep[k + 1]
        total = first_sweep[k] + first_sweep[k + 2] + cross_sum(centre)
        delta[k] = centre + weight * (total - 6.0 * centre)
    for k in range(4):
        smooth_part = (near_base if k < 2 else far_base)[k % 2]
        potential_ref[mirror(side, k, 4)] = smooth_part + delta[k + 2, own_rows]
    for k in range(2):
        at = 2 + k
        index = mirror(side, k, 2)
        section[peer_rows] = delta[at, peer_rows] + peer_base[1 - k]
        section[own_rows] = delta[at, own_rows] + near_base[k]
        value = section[...]
        keep = 1.0 - solid_ref[index].astype(f32)
        out_ref[0, index] = sign * first_of([delta[at + offset] for offset in range(-2, 3)])
        out_ref[2, index, own_rows] = near_w[k]
        out_ref[2, index, peer_rows] = peer_vw[1, 1 - k]
        out_ref[2, index] = (out_ref[2, index] - dot_right(value, depth_high[...], depth_low[...])) * keep
        out_ref[1, index, own_rows] = near_v[k]
        out_ref[1, index, peer_rows] = peer_vw[0, 1 - k]
        top, low = (value[:half], value[half:])
        even = dot_left(sum_high[...], sum_low[...], top + low)
        odd = dot_left(diff_high[...], diff_low[...], top - low)
        out_ref[1, index, :half] = (out_ref[1, index, :half] - (even + odd)) * keep[:half]
        out_ref[1, index, half:] = (out_ref[1, index, half:] - (even - odd)) * keep[half:]


def stream_correction_kernel(gradient_ref, own_u, peer_u, solid_ref, out_ref):
    side = lax.axis_index("group")
    half = own_u.shape[1]
    index = pl.program_id(0)
    k = mirror(side, index, 2)
    own_rows = pl.ds(pl.multiple_of(side * half, half), half)
    peer_rows = pl.ds(pl.multiple_of((1 - side) * half, half), half)
    for rows, value in ((own_rows, own_u[k]), (peer_rows, peer_u[1 - k])):
        keep = 1.0 - solid_ref[0, rows].astype(f32)
        out_ref[0, 0, rows] = (value - gradient_ref[0, 0, rows]) * keep


def pair_sums(fine, coarse):
    return (np.arange(fine)[:, None] // 2 == np.arange(coarse)[None, :]).astype(ml_dtypes.bfloat16)


def paired(velocity, obstacle, pressure):
    rows, depth = velocity.shape[2:]
    half = rows // 2
    wide = half + 2 * HALO
    tunnel_size = lax.axis_size("tunnel")
    side = lax.axis_index("group")
    both = ("tunnel", "group")
    own, spread, basis, rows_first = half_tables(rows)
    depth_first, depth_second = wave_tables(depth)
    rows_high, rows_low = high_low(own)
    spread_high, spread_low = high_low(spread)
    spread_all = np.concatenate([spread_high, spread_high, spread_low, np.zeros_like(spread_low)], axis=1)
    basis_both = np.concatenate(high_low(basis), axis=0)
    depth_high, depth_low = high_low(np.concatenate([depth_first.T, depth_second.T], axis=1))
    sum_high, sum_low = high_low((rows_first[:half, :half] + rows_first[:half, half:]) / 2.0)
    diff_high, diff_low = high_low((rows_first[:half, :half] - rows_first[:half, half:]) / 2.0)

    def swap(value):
        return lax.ppermute(value, "group", [(0, 1), (1, 0)])

    ahead_way, behind_way = ([], [])
    for i in range(tunnel_size):
        after, before = ((i + 1) % tunnel_size, (i - 1) % tunnel_size)
        ahead_way += [(2 * i, 2 * after), (2 * i + 1, 2 * before + 1)]
        behind_way += [(2 * i, 2 * before), (2 * i + 1, 2 * after + 1)]

    def ahead(value):
        return lax.ppermute(value, both, ahead_way)

    def behind(value):
        return lax.ppermute(value, both, behind_way)

    def ahead_across(value):
        return lax.ppermute(value, both, [(i, j ^ 1) for i, j in ahead_way])

    def behind_across(value):
        return lax.ppermute(value, both, [(i, j ^ 1) for i, j in behind_way])

    def tied(value, *others):
        return lax.optimization_barrier((value,) + others)[0]

    def half_of(value, which, axis):
        return lax.dynamic_slice_in_dim(value, which * half, half, axis=axis)

    plane = (half, depth)
    two_planes, four_planes = ((2,) + plane, (4,) + plane)
    full = lambda shape: pl.BlockSpec(shape, lambda i: (0,) * len(shape))
    by_plane = lambda shape, at: pl.BlockSpec(
        shape[:at] + (1,) + shape[at + 1 :], lambda i: (0,) * at + (i,) + (0,) * (len(shape) - at - 1)
    )
    tables = (rows_high, rows_low, spread_all, depth_high, depth_low)
    table_specs = [full(table.shape) for table in tables]

    edges = jnp.concatenate([pressure[:, :HALO], pressure[:, half - HALO :]], axis=1)
    pressure_edge = swap(edges)
    tall = jnp.concatenate([pressure_edge[:, HALO:], pressure, pressure_edge[:, :HALO]], axis=1)
    to_ahead = jnp.where(side == 0, tall[1:], tall[:3])
    to_behind = jnp.where(side == 0, tall[:3], tall[1:])
    sent_uv = half_of(velocity[:2], 1 - side, 2)
    peer_uv = swap(sent_uv)
    pressure_left = ahead(to_ahead)
    pressure_right = behind(to_behind)
    raw_own, sent_w = kernel_call(
        own_planes_kernel,
        [(3, 2) + plane, (2, half + 24, depth)],
        [],
        [by_plane(velocity.shape, 1), full(basis_both.shape)] + table_specs,
        3 * 10**9,
        velocity, basis_both, *tables,
        grid=(2,),
        out_specs=[by_plane((3, 2) + plane, 1), by_plane((2, half + 24, depth), 0)],
    )
    peer_w = swap(tied(sent_w, pressure_left, pressure_right))
    own_half = half_of(tied(velocity, sent_w), side, 2)
    one = behind(own_half)
    other_uv = ahead(peer_uv)
    other_w = ahead(peer_w[:, :half])
    solid_peer = swap(half_of(obstacle, 1 - side, 1))
    solid_own = half_of(obstacle, side, 1)
    (raw_peer,) = kernel_call(
        peer_planes_kernel,
        [(3, 2) + plane],
        [],
        [by_plane((2, 2) + plane, 1), by_plane((2, half + 24, depth), 0)] + table_specs,
        3 * 10**9,
        peer_uv, peer_w, *tables,
        grid=(2,),
        out_specs=[by_plane((3, 2) + plane, 1)],
    )
    strip = 64

    def strips(count, first=0):
        return pl.BlockSpec((count, 2, strip, depth), lambda i: (first, 0, i, 0))

    flat = pl.BlockSpec((2, strip, depth), lambda i: (0, i, 0))
    near_u, far_u = kernel_call(
        star_u_kernel,
        [two_planes] * 2,
        [],
        [strips(1)] * 6 + [flat] * 2,
        10**8,
        raw_own, raw_peer, own_half, one, peer_uv, other_uv, solid_own, solid_peer,
        grid=(half // strip,),
        out_specs=[flat] * 2,
    )
    left_u, right_u = (ahead(far_u), behind(near_u))
    basis_strips = basis_both.reshape(16, half // strip, strip).transpose(1, 0, 2).copy()
    near_v, far_v, near_w, far_w, sum_v = kernel_call(
        star_vw_kernel,
        [two_planes] * 4 + [(4, 8, depth)],
        [],
        [strips(3)] * 4 + [strips(2), flat, strips(1, 1), flat, flat, flat]
        + [pl.BlockSpec((1, 16, strip), lambda i: (i, 0, 0))],
        10**8,
        raw_own, raw_peer, tied(own_half, near_u), one, peer_uv, peer_w, other_uv, other_w, solid_own, solid_peer,
        basis_strips,
        grid=(half // strip,),
        out_specs=[flat] * 4 + [full((4, 8, depth))],
    )
    peer_sum_v = swap(sum_v)
    own_depth = (depth_high[:, :depth].copy(), depth_low[:, :depth].copy())
    (cross,) = kernel_call(
        cross_kernel,
        [four_planes],
        [],
        [VMEM] * 8,
        10**9,
        near_v, far_v, near_w, far_w, rows_high, rows_low, *own_depth,
    )
    edge_shape = (4, HALO, depth)
    near_r, far_r, head_r, tail_r = kernel_call(
        source_kernel,
        [two_planes, two_planes, edge_shape, edge_shape],
        [],
        [flat] * 4
        + [pl.BlockSpec((4, strip, depth), lambda i: (0, i, 0)), full((4, 8, depth))]
        + [pl.BlockSpec((strip, spread_all.shape[1]), lambda i: (i, 0))],
        10**8,
        near_u, far_u, left_u, right_u, cross, peer_sum_v, spread_all[:half].copy(),
        grid=(half // strip,),
        out_specs=[flat, flat, full(edge_shape), full(edge_shape)],
    )
    edge_r = jnp.concatenate([head_r, tail_r], axis=1)
    left_r, right_r = (ahead(far_r), behind(near_r))
    edges = swap(edge_r)
    left_edge, right_edge = (ahead(edges[:2]), behind(edges[2:]))
    peer_vw = swap(jnp.stack([tied(far_v, left_edge, right_edge), far_w]))

    mid_rows, mid_depth = (wide // 2, depth // 2)
    message = (mid_rows + wide, depth)
    base_one, mid_source, sent_ahead, sent_behind = kernel_call(
        fine_kernel,
        [(4, wide, depth), (2, mid_rows, mid_depth), message, message],
        [
            pltpu.VMEM((8, wide, depth), f32),
            pltpu.VMEM((10, wide, depth), f32),
            pltpu.VMEM((8, wide, depth), f32),
            pltpu.VMEM((6, wide, depth), f32),
        ],
        [VMEM] * 12,
        10**8,
        tall, pressure_left, pressure_right,
        near_r, far_r, left_r, right_r, edges, left_edge, right_edge,
        pair_sums(depth, mid_depth), pair_sums(wide, mid_rows).T,
    )
    left_one, right_one = (ahead(sent_ahead), behind(sent_behind))
    near_base, far_base = kernel_call(
        base_kernel,
        [two_planes, two_planes],
        [],
        [VMEM] * 5,
        10**8,
        base_one, left_one, right_one, near_r, far_r,
    )
    low_depth = mid_depth // 2
    halves = np.zeros((mid_depth, 2 * mid_depth), ml_dtypes.bfloat16)
    halves[:, :low_depth] = pair_sums(mid_depth, low_depth)
    halves[:, mid_depth + low_depth :] = pair_sums(mid_depth, low_depth)
    own_pairs = pair_sums(half // 2, half // 4).T
    own_pairs = np.pad(own_pairs, ((0, 0), (HALO // 2, HALO // 2)))
    mid_one, low_source = kernel_call(
        middle_kernel,
        [(2, mid_rows, mid_depth), (half // 8, mid_depth)],
        [pltpu.VMEM((6, mid_rows, mid_depth), f32), pltpu.VMEM((4, mid_rows, mid_depth), f32)],
        [VMEM] * 5,
        10**8,
        tied(mid_source, near_base), left_one, right_one, halves, own_pairs,
    )
    left_two, right_two = (ahead(mid_one[1:]), behind(mid_one[:1]))
    (mid_base,) = kernel_call(
        middle_base_kernel,
        [(2, half // 2, mid_depth)],
        [],
        [VMEM] * 4,
        10**7,
        mid_one, tied(left_two, peer_vw), right_two, mid_source,
    )
    peer_mid = swap(mid_base)
    both_mid = jnp.stack([mid_base, peer_mid])
    left_mid, right_mid = (ahead(both_mid), behind(both_mid))
    low_all = lax.all_to_all(
        jnp.broadcast_to(tied(low_source, mid_base), (2 * tunnel_size,) + low_source.shape), both, 0, 0, tiled=True
    )
    left_b, right_b = (ahead(tied(far_base, mid_base)), behind(tied(near_base, mid_base)))
    peer_base = swap(tied(far_base, peer_mid))
    own_u, sent_u = kernel_call(
        stream_kernel,
        [two_planes, two_planes],
        [],
        [VMEM] * 6,
        10**8,
        near_base, far_base, left_b, right_b, near_u, far_u,
    )
    peer_u = swap(sent_u)
    low_plane = (half // 2, mid_depth)
    mid_plane = (half, mid_depth)
    fine_plane = (rows, depth)
    expand_low = np.zeros((mid_depth, mid_depth), ml_dtypes.bfloat16)
    expand_low[:low_depth] = pair_sums(mid_depth, low_depth).T
    (spread_low,) = kernel_call(
        coarsest_kernel,
        [(5,) + mid_plane],
        [pltpu.VMEM((11,) + low_plane, f32)] * 3,
        [VMEM] * 3,
        10**7,
        low_all, expand_low, pair_sums(half, half // 2),
    )
    corrected, potential = kernel_call(
        correction_kernel,
        [(3, 2) + fine_plane, four_planes],
        [
            pltpu.VMEM((5,) + mid_plane, f32),
            pltpu.VMEM((9,) + mid_plane, f32),
            pltpu.VMEM((5,) + fine_plane, f32),
            pltpu.VMEM((8,) + fine_plane, f32),
            pltpu.VMEM((6,) + fine_plane, f32),
            pltpu.VMEM(fine_plane, f32),
        ],
        [VMEM] * 19,
        10**9,
        spread_low, both_mid, left_mid, right_mid, near_base, far_base, peer_base, near_v, near_w, peer_vw, obstacle,
        sum_high, sum_low, diff_high, diff_low, *own_depth,
        pair_sums(depth, mid_depth).T.copy(), pair_sums(rows, half),
    )
    stream = pl.BlockSpec((1, 1) + fine_plane, lambda i: (0, i, 0, 0))
    (corrected,) = kernel_call(
        stream_correction_kernel,
        [corrected.shape],
        [],
        [stream] + [full(two_planes)] * 2 + [by_plane(obstacle.shape, 0)],
        10**7,
        corrected, own_u, peer_u, obstacle,
        grid=(2,),
        out_specs=[stream],
        aliases={0: 0},
    )
    return (corrected, potential)


def step(velocity, obstacle, pressure):
    planes, rows, depth = velocity.shape[1:]
    fits = lax.axis_size("group") == 2 and planes == 2 and pressure.shape[0] == 4
    fits = fits and lax.axis_size("tunnel") > 10 and rows % 512 == 0 and depth % 256 == 0
    if fits:
        return paired(velocity, obstacle, pressure)
    return local(velocity, obstacle, pressure)


def solution(mesh):
    in_specs = (
        P(None, ("tunnel", "group"), None, None),
        P(("tunnel", "group"), None, None),
        P("tunnel", "group", None),
    )
    out_specs = (P(None, ("tunnel", "group"), None, None), P("tunnel", "group", None))
    return jax.shard_map(step, mesh=mesh, in_specs=in_specs, out_specs=out_specs, check_vma=False)
```

```python
import math

import jax
import jax.numpy as jnp
import ml_dtypes
import numpy as np
from jax import lax
from jax.experimental import pallas as pl
from jax.experimental.pallas import tpu as pltpu
from jax.sharding import PartitionSpec as P

LEVELS = 3
SWEEPS = 2
COARSE_SWEEPS = 4


time_step = 0.1
viscosity = 0.05
relax_weight = 0.8
highest = lax.Precision.HIGHEST


def extended(value, sides, width):
    for axis, dim in sides:
        size, length = (lax.axis_size(axis), value.shape[dim])
        up = [(i, (i + 1) % size) for i in range(size)]
        down = [(j, i) for i, j in up]
        last = lax.slice_in_dim(value, length - width, length, axis=dim)
        initial = lax.slice_in_dim(value, 0, width, axis=dim)
        before = lax.ppermute(last, axis, up)
        after = lax.ppermute(initial, axis, down)
        value = jnp.concatenate([before, value, after], axis=dim)
    return value


def compact_tables(count):
    indices = jnp.arange(count, dtype=jnp.int32)
    product = indices[:, None] * indices[None, :] % count
    angles = product.astype(jnp.float32) * (2.0 * math.pi / count)
    cosines = jnp.cos(angles)
    sines = jnp.sin(angles)
    theta = indices.astype(jnp.float32) * (2.0 * math.pi / count)
    first_wave = (14.0 / 9.0 * jnp.sin(theta) + jnp.sin(2.0 * theta) / 18.0) / (
        1.0 + 2.0 / 3.0 * jnp.cos(theta)
    )
    second_wave = (
        24.0 / 11.0 * (1.0 - jnp.cos(theta)) + 3.0 / 22.0 * (1.0 - jnp.cos(2.0 * theta))
    ) / (1.0 + 4.0 / 11.0 * jnp.cos(theta))
    first_matrix = (
        jnp.dot(cosines * first_wave, sines.T, precision=highest)
        - jnp.dot(sines * first_wave, cosines.T, precision=highest)
    ) / count
    second_matrix = (
        -(
            jnp.dot(cosines * second_wave, cosines.T, precision=highest)
            + jnp.dot(sines * second_wave, sines.T, precision=highest)
        )
        / count
    )
    return (first_matrix, second_matrix)


def along_rows(matrix, field):
    return jnp.einsum("ij,...jz->...iz", matrix, field, precision=highest)


def along_depth(matrix, field):
    return jnp.einsum("...j,ij->...i", field, matrix, precision=highest)


def shifted(padded, offset, axis):
    count = padded.shape[axis] - 4
    return lax.slice_in_dim(padded, 2 + offset, 2 + offset + count, axis=axis)


def stream_first(padded, axis):
    ahead = shifted(padded, 1, axis) - shifted(padded, -1, axis)
    further = shifted(padded, 2, axis) - shifted(padded, -2, axis)
    return (8.0 * ahead - further) / 12.0


def stream_second(padded, axis):
    ahead = shifted(padded, 1, axis) + shifted(padded, -1, axis)
    further = shifted(padded, 2, axis) + shifted(padded, -2, axis)
    return (16.0 * ahead - further - 30.0 * shifted(padded, 0, axis)) / 12.0


def padded_neighbours(padded):
    interior = padded[1:-1, 1:-1]
    total = padded[2:, 1:-1] + padded[:-2, 1:-1]
    total = total + padded[1:-1, 2:] + padded[1:-1, :-2]
    return total + jnp.roll(interior, -1, 2) + jnp.roll(interior, 1, 2)


def relax_padded(padded, source_term, scale):
    interior = padded[1:-1, 1:-1]
    return interior + relax_weight / 6.0 * (
        padded_neighbours(padded) - 6.0 * interior - scale * source_term
    )


def faces(field):
    return extended(field, (("tunnel", 0), ("group", 1)), 1)


def thin_sweeps(field, source_term, scale, count):
    for sweep_index in range(count):
        field = relax_padded(faces(field), source_term, scale)
    return field


def smooth(field, source_term, scale, level):
    if level == 0:
        return thin_sweeps(field, source_term, scale, SWEEPS)
    return thin_sweeps(field, source_term, scale, SWEEPS)


def coarsest(source_term, scale):
    return thin_sweeps(jnp.zeros_like(source_term), source_term, scale, COARSE_SWEEPS)


def restrict(field):
    planes, rows, depth = field.shape
    blocks = field.reshape(planes // 2, 2, rows // 2, 2, depth // 2, 2)
    return jnp.sum(blocks, axis=(1, 3, 5)) * 0.125


def prolong(field):
    return jnp.repeat(jnp.repeat(jnp.repeat(field, 2, 0), 2, 1), 2, 2)


def cycle(field, source_term, level):
    scale = 4.0**level
    if level == LEVELS - 1:
        return coarsest(source_term, scale)
    field = smooth(field, source_term, scale, level)
    leftover = source_term - (padded_neighbours(faces(field)) - 6.0 * field) / scale
    coarse_source = restrict(leftover)
    coarse = cycle(jnp.zeros_like(coarse_source), coarse_source, level + 1)
    field = field + prolong(coarse)
    return smooth(field, source_term, scale, level)


def local(velocity, obstacle, pressure):
    row_count = velocity.shape[2]
    depth_count = velocity.shape[3]
    rows_first, rows_second = compact_tables(row_count)
    depth_first, depth_second = compact_tables(depth_count)
    rows_both = jnp.concatenate([rows_first, rows_second], axis=0)
    depth_both = jnp.concatenate([depth_first, depth_second], axis=0)
    keep = 1.0 - obstacle.astype(jnp.float32)
    row_terms = along_rows(rows_both, velocity)
    depth_terms = along_depth(depth_both, velocity)
    transverse = (
        velocity[1] * row_terms[:, :, :row_count] + velocity[2] * depth_terms[..., :depth_count]
    )
    diffusion = row_terms[:, :, row_count:] + depth_terms[..., depth_count:]
    padded = extended(velocity, ((("tunnel", "group"), 1),), 2)
    streamwise = -velocity[0] * stream_first(padded, 1) + viscosity * stream_second(padded, 1)
    tendency = streamwise - transverse + viscosity * diffusion
    star = (velocity + time_step * tendency) * keep
    star_padded = extended(star[0], ((("tunnel", "group"), 0),), 2)
    source = (
        stream_first(star_padded, 0)
        + along_rows(rows_first, star[1])
        + along_depth(depth_first, star[2])
    )
    source_tile = lax.all_to_all(source, "group", split_axis=1, concat_axis=0, tiled=True)
    potential = cycle(pressure, source_tile, 0)
    potential_padded = extended(potential, (("tunnel", 0),), 2)
    streamwise_grad = stream_first(potential_padded, 0)
    returned = lax.all_to_all(
        jnp.stack([potential, streamwise_grad]), "group", split_axis=1, concat_axis=2, tiled=True
    )
    gradient = jnp.stack(
        [returned[1], along_rows(rows_first, returned[0]), along_depth(depth_first, returned[0])]
    )
    corrected = (star - gradient) * keep
    return (corrected, potential)


HALO = 16
weight = relax_weight / 6.0
bf16 = jnp.bfloat16
f32 = jnp.float32
VMEM = pl.BlockSpec(memory_space=pltpu.VMEM)
ANY = pl.BlockSpec(memory_space=pl.ANY)


def wave_tables(count):
    index = np.arange(count)
    angles = 2.0 * np.pi * (np.outer(index, index) % count) / count
    theta = 2.0 * np.pi * index / count
    first_wave = (14.0 / 9.0 * np.sin(theta) + np.sin(2.0 * theta) / 18.0) / (
        1.0 + 2.0 / 3.0 * np.cos(theta)
    )
    second_wave = (
        24.0 / 11.0 * (1.0 - np.cos(theta)) + 3.0 / 22.0 * (1.0 - np.cos(2.0 * theta))
    ) / (1.0 + 4.0 / 11.0 * np.cos(theta))
    cosines, sines = (np.cos(angles), np.sin(angles))
    first = ((cosines * first_wave) @ sines.T - (sines * first_wave) @ cosines.T) / count
    second = -((cosines * second_wave) @ cosines.T + (sines * second_wave) @ sines.T) / count
    return (first, second)


def high_low(table):
    high = table.astype(np.float32).astype(ml_dtypes.bfloat16)
    low = (table - high.astype(np.float64)).astype(np.float32).astype(ml_dtypes.bfloat16)
    return (high, low)


def half_tables(count):
    first, second = wave_tables(count)
    half = count // 2
    index = np.arange(half)
    root_first = (math.sqrt(5.0) - 3.0) / 2.0
    root_second = (math.sqrt(105.0) - 11.0) / 4.0
    basis = np.zeros((8, half))
    basis[0, 0] = 1.0
    basis[1, -1] = 1.0
    basis[2] = root_first**index
    basis[3] = basis[2][::-1]
    basis[4] = root_second**index
    basis[5] = basis[4][::-1]
    spread = []
    for table, used in ((first, (0, 1, 2, 3)), (second, (0, 1, 4, 5))):
        solved = np.linalg.lstsq(basis[list(used)].T, table[:half, half:].T, rcond=None)[0].T
        wide = np.zeros((half, 8))
        wide[:, list(used)] = solved
        spread.append(wide)
    own = np.concatenate([first[:half, :half], second[:half, :half]], axis=0)
    return (own, np.concatenate(spread, axis=0), basis, first)


def split(value):
    high = value.astype(bf16)
    low = (value - high.astype(f32)).astype(bf16)
    return (high, low)


def dot(left, right):
    return jnp.dot(left, right, preferred_element_type=f32)


def dot_left(table_high, table_low, value):
    high, low = split(value)
    return dot(table_high, high) + (dot(table_high, low) + dot(table_low, high))


def dot_right(value, table_high, table_low):
    high, low = split(value)
    return dot(high, table_high) + (dot(low, table_high) + dot(high, table_low))


def pick_left(zero_one, value):
    high, low = split(value)
    return dot(zero_one, high) + dot(zero_one, low)


def pick_right(value, zero_one):
    high, low = split(value)
    return dot(high, zero_one) + dot(low, zero_one)


def summary(basis_both, value):
    high, low = split(value)
    main = dot(basis_both, high)
    rest = dot(basis_both, low)
    return main[:8] + main[8:] + rest[:8]


def summary_operand(value):
    high = value.astype(bf16).astype(f32)
    return jnp.concatenate([high, value - high, high, jnp.zeros_like(high)], axis=0).astype(bf16)


def turn(value, shift, axis):
    return pltpu.roll(value, shift % value.shape[axis], axis)


def cross_sum(value):
    return (turn(value, 1, 0) + turn(value, -1, 0)) + (turn(value, 1, 1) + turn(value, -1, 1))


def first_of(values):
    return (8.0 * (values[3] - values[1]) - (values[4] - values[0])) * (1.0 / 12.0)


def second_of(values):
    return (
        16.0 * (values[3] + values[1]) - (values[4] + values[0]) - 30.0 * values[2]
    ) * (1.0 / 12.0)


def kernel_call(body, outs, scratch, specs, flops, *args, grid=None, out_specs=None, aliases=None):
    total = sum(math.prod(a.shape) * a.dtype.itemsize for a in args)
    total += sum(4 * math.prod(s) for s in outs)
    options = {} if grid is None else {"grid": grid}
    if aliases is not None:
        options["input_output_aliases"] = aliases
    return pl.pallas_call(
        body,
        out_shape=[jax.ShapeDtypeStruct(s, f32) for s in outs],
        in_specs=specs,
        out_specs=[VMEM] * len(outs) if out_specs is None else out_specs,
        scratch_shapes=scratch,
        compiler_params=pltpu.CompilerParams(vmem_limit_bytes=36 * 1024 * 1024),
        cost_estimate=pl.CostEstimate(flops=flops, bytes_accessed=total if flops > 1 else 1, transcendentals=0),
        **options,
    )(*args)


def mirror(side, index, count):
    return index + side * (count - 1 - 2 * index)


def sign_of(side):
    return (1 - 2 * side).astype(f32)


def transverse(u, v, w, value, other_sum, rows_high, rows_low, spread, depth_high, depth_low):
    half, width = value.shape
    high, low = split(value)
    across = (
        dot(rows_high[...], high)
        + (dot(rows_high[...], low) + dot(rows_low[...], high))
        + dot(spread[...], summary_operand(other_sum))
    )
    along = dot(high, depth_high[...]) + (dot(low, depth_high[...]) + dot(high, depth_low[...]))
    advect = v * across[:half] + w * along[:, :width]
    return value + time_step * (viscosity * (across[half:] + along[:, width:]) - advect)


def own_planes_kernel(
    velocity_ref, basis_ref, rows_high, rows_low, spread, depth_high, depth_low, out_ref, sent_ref
):
    side = lax.axis_index("group")
    half = basis_ref.shape[1]
    own = pl.ds(pl.multiple_of(side * half, half), half)
    other = pl.ds(pl.multiple_of((1 - side) * half, half), half)
    u, v, w = (velocity_ref[c, 0, own] for c in range(3))
    sent_ref[0, :half] = velocity_ref[2, 0, other]
    for c in range(3):
        value = velocity_ref[c, 0, own]
        kept = summary(basis_ref[...], velocity_ref[c, 0, other])
        sent_ref[0, half + 8 * c : half + 8 * c + 8] = summary(basis_ref[...], value)
        out_ref[c, 0] = transverse(u, v, w, value, kept, rows_high, rows_low, spread, depth_high, depth_low)


def peer_planes_kernel(
    uv_ref, w_ref, rows_high, rows_low, spread, depth_high, depth_low, out_ref
):
    half = uv_ref.shape[2]
    u, v, w = (uv_ref[0, 0], uv_ref[1, 0], w_ref[0, :half])
    for c in range(3):
        other_sum = w_ref[0, half + 8 * c : half + 8 * c + 8]
        out_ref[c, 0] = transverse(
            u, v, w, (u, v, w)[c], other_sum, rows_high, rows_low, spread, depth_high, depth_low
        )


def star_planes(side, planes, raws, solids, u_of, outs):
    sign = sign_of(side) * (time_step / 12.0)
    for plane in range(4):
        index = mirror(side, plane % 2, 2)
        keep = 1.0 - solids[plane // 2][index].astype(f32)
        near = planes[plane : plane + 5]
        first = 8.0 * (near[3] - near[1]) - (near[4] - near[0])
        second = 16.0 * (near[3] + near[1]) - (near[4] + near[0]) - 30.0 * near[2]
        raw = raws[plane // 2][index]
        outs[plane // 2][plane % 2] = (
            raw + (time_step * viscosity / 12.0) * second - (u_of(plane) * sign) * first
        ) * keep


def eight(side, groups):
    return [group[mirror(side, k, 2)] for group in groups for k in range(2)]


def star_u_kernel(raw_own, raw_peer, own_ref, one_ref, peers, others, solid_own, solid_peer, near_ref, far_ref):
    side = lax.axis_index("group")
    planes = eight(side, (others.at[0], own_ref.at[0], peers.at[0], one_ref.at[0]))
    star_planes(
        side, planes, (raw_own.at[0], raw_peer.at[0]), (solid_own, solid_peer),
        lambda plane: planes[plane + 2], (near_ref, far_ref),
    )


def star_vw_kernel(
    raw_own, raw_peer, own_ref, one_ref, peers, peer_w, others, other_w, solid_own, solid_peer, basis_ref,
    near_v, far_v, near_w, far_w, sum_ref,
):
    side = lax.axis_index("group")
    step = pl.program_id(0)

    def u_of(plane):
        return (own_ref if plane < 2 else peers)[0, mirror(side, plane % 2, 2)]

    for c, peer, other, outs in (
        (1, peers.at[1], others.at[0], (near_v, far_v)),
        (2, peer_w, other_w, (near_w, far_w)),
    ):
        planes = eight(side, (other, own_ref.at[c], peer, one_ref.at[c]))
        star_planes(side, planes, (raw_own.at[c], raw_peer.at[c]), (solid_own, solid_peer), u_of, outs)

    @pl.when(step == 0)
    def _():
        sum_ref[...] = jnp.zeros_like(sum_ref)

    for plane in range(4):
        sum_ref[plane] += summary(basis_ref[0], (near_v if plane < 2 else far_v)[plane % 2])


def cross_kernel(near_v, far_v, near_w, far_w, rows_high, rows_low, depth_high, depth_low, out_ref):
    half = near_v.shape[1]
    for plane in range(4):
        v, w = ((near_v, near_w) if plane < 2 else (far_v, far_w))
        out_ref[plane] = dot_left(rows_high[:half], rows_low[:half], v[plane % 2]) + dot_right(
            w[plane % 2], depth_high[...], depth_low[...]
        )


def source_kernel(
    near_u, far_u, left_ref, right_ref, cross_ref, sum_ref, spread, near_r, far_r, head, tail
):
    sign = sign_of(lax.axis_index("group"))
    rows = cross_ref.shape[1]
    step = pl.program_id(0)
    planes = [ref[k] for ref in (left_ref, near_u, far_u, right_ref) for k in range(2)]
    values = []
    for plane in range(4):
        value = sign * first_of(planes[plane : plane + 5]) + cross_ref[plane]
        value = value + dot(spread[...], summary_operand(sum_ref[3 - plane]))
        (near_r if plane < 2 else far_r)[plane % 2] = value
        values.append(value)

    @pl.when(step == 0)
    def _():
        for plane in range(4):
            head[plane] = values[plane][:HALO]

    @pl.when(step == pl.num_programs(0) - 1)
    def _():
        for plane in range(4):
            tail[plane] = values[plane][rows - HALO :]


def fine_kernel(
    pressure_tall, pressure_left, pressure_right,
    near_r, far_r, left_ref, right_ref, edge_ref, left_edge, right_edge, depth_pick, rows_pick,
    base_ref, coarse_ref, ahead_ref, behind_ref, source_ref, one, two,
):
    side = lax.axis_index("group")
    half = near_r.shape[1]

    def fill(target, at, body, edge):
        target[at, HALO : HALO + half] = body
        target[at, :HALO] = edge[HALO:]
        target[at, HALO + half :] = edge[:HALO]

    for plane in range(2):
        fill(source_ref, plane, left_ref[plane], left_edge[1 - plane])
        fill(source_ref, 2 + plane, near_r[plane], edge_ref[3 - plane])
        fill(source_ref, 4 + plane, far_r[plane], edge_ref[1 - plane])
        fill(source_ref, 6 + plane, right_ref[plane], right_edge[1 - plane])
    pressure = [pressure_left.at[mirror(side, k, 3)] for k in range(3)]
    pressure += [pressure_tall.at[mirror(side, k, 4)] for k in range(4)]
    pressure += [pressure_right.at[mirror(side, k, 3)] for k in range(3)]
    for k in range(8):
        centre = pressure[k + 1][...]
        total = pressure[k][...] + pressure[k + 2][...] + cross_sum(centre)
        one[k] = centre + weight * (total - 6.0 * centre - source_ref[k])
    for k in range(6):
        centre = one[k + 1]
        total = one[k] + one[k + 2] + cross_sum(centre)
        two[k] = centre + weight * (total - 6.0 * centre - source_ref[k + 1])
    for pair in range(2):
        left = []
        for k in (2 * pair, 2 * pair + 1):
            centre = two[k + 1]
            total = two[k] + two[k + 2] + cross_sum(centre)
            residual = source_ref[k + 2] - (total - 6.0 * centre)
            base_ref[k] = centre - weight * residual
            left.append(residual)
        coarse = 0.125 * pick_left(rows_pick[...], pick_right(left[0] + left[1], depth_pick[...]))
        coarse_ref[pair] = coarse
        rows, width = coarse.shape
        ahead_ref[:rows, width * pair : width * (pair + 1)] = coarse
        behind_ref[:rows, width * pair : width * (pair + 1)] = coarse
    ahead_ref[rows:] = base_ref[3]
    behind_ref[rows:] = base_ref[0]


def middle_kernel(own_ref, left_ref, right_ref, depth_pick, rows_pick, base_ref, coarse_ref, one, two):
    rows, width = own_ref.shape[1:]
    source = []
    for ref in (left_ref, own_ref, right_ref):
        for k in range(2):
            source.append(ref[k] if ref is own_ref else ref[:rows, width * k : width * (k + 1)])
    for k in range(6):
        one[k] = (-4.0 * weight) * source[k]
    for k in range(4):
        centre = one[k + 1]
        total = one[k] + one[k + 2] + cross_sum(centre)
        two[k] = centre + weight * (total - 6.0 * centre - 4.0 * source[k + 1])
    left = []
    for k in range(2):
        centre = two[k + 1]
        total = two[k] + two[k + 2] + cross_sum(centre)
        residual = source[k + 2] - 0.25 * (total - 6.0 * centre)
        base_ref[k] = centre - (4.0 * weight) * residual
        left.append(residual)
    width = own_ref.shape[2]
    wide = pick_right(left[0] + left[1], depth_pick[...])
    count = coarse_ref.shape[0]
    coarse_ref[...] = 0.125 * (
        pick_left(rows_pick[:count], wide[:, :width]) + pick_left(rows_pick[count:], wide[:, width:])
    )


def middle_base_kernel(base_ref, left_ref, right_ref, source_ref, out_ref):
    rows = out_ref.shape[1]
    planes = [left_ref[0], base_ref[0], base_ref[1], right_ref[0]]
    for k in range(2):
        centre = planes[k + 1]
        total = planes[k] + planes[k + 2] + cross_sum(centre)
        value = centre + weight * (total - 6.0 * centre - 4.0 * source_ref[k])
        out_ref[k] = value[HALO // 2 : HALO // 2 + rows]


def base_kernel(base_ref, left_ref, right_ref, near_r, far_r, near_ref, far_ref):
    rows = near_ref.shape[1]
    skip = left_ref.shape[0] - base_ref.shape[1]
    for k in range(4):
        before = left_ref[skip:] if k == 0 else base_ref[k - 1]
        after = right_ref[skip:] if k == 3 else base_ref[k + 1]
        centre = base_ref[k]
        total = before + after + cross_sum(centre)
        value = (centre + weight * (total - 6.0 * centre))[HALO : HALO + rows]
        source, out = ((near_r, near_ref) if k < 2 else (far_r, far_ref))
        out[k % 2] = value - weight * source[k % 2]


def stream_kernel(near_ref, far_ref, left_ref, right_ref, near_u, far_u, own_ref, sent_ref):
    sign = sign_of(lax.axis_index("group"))
    planes = [ref[k] for ref in (left_ref, near_ref, far_ref, right_ref) for k in range(2)]
    for plane in range(4):
        star = (near_u if plane < 2 else far_u)[plane % 2]
        (own_ref if plane < 2 else sent_ref)[plane % 2] = star - sign * first_of(planes[plane : plane + 5])


def coarsest_kernel(all_ref, mid_depth, mid_rows, out_ref, source, one, two):
    place = lax.axis_index("tunnel")
    step = 1 - 2 * lax.axis_index("group")
    count = all_ref.shape[0] // 2
    quarter, width = all_ref.shape[1:]
    lower = lax.broadcasted_iota(jnp.int32, (quarter, width), 1) < width // 2
    for k in range(11):
        plane = lax.rem(place + step * (k - 5) + 2 * count, count)
        for part in range(2):
            packed = all_ref[2 * plane + part]
            turned = turn(packed, width // 2, 1)
            source[k, 2 * part * quarter : (2 * part + 1) * quarter] = jnp.where(lower, packed, turned)
            source[k, (2 * part + 1) * quarter : (2 * part + 2) * quarter] = jnp.where(lower, turned, packed)
    for k in range(11):
        one[k] = (-16.0 * weight) * source[k]
    source_at, target = (one, two)
    for sweep_index in range(1, COARSE_SWEEPS):
        for k in range(sweep_index, 11 - sweep_index):
            centre = source_at[k]
            total = source_at[k - 1] + source_at[k + 1] + cross_sum(centre)
            target[k] = centre + weight * (total - 6.0 * centre - 16.0 * source[k])
        source_at, target = (target, source_at)
    for k in range(5):
        out_ref[k] = pick_left(mid_rows[...], pick_right(source_at[k + 3], mid_depth[...]))


def correction_kernel(
    spread_ref, own_mid, left_mid, right_mid,
    near_base, far_base, peer_base, near_v, near_w, peer_vw, solid_ref,
    sum_high, sum_low, diff_high, diff_low, depth_high, depth_low, fine_depth, fine_rows,
    out_ref, potential_ref, base, mid, fine, first_sweep, delta,
):
    side = lax.axis_index("group")
    sign = sign_of(side)
    half = near_v.shape[1]
    own_rows = pl.ds(pl.multiple_of(side * half, half), half)
    peer_rows = pl.ds(pl.multiple_of((1 - side) * half, half), half)
    mid_half = own_mid.shape[2]
    own_mid_rows = pl.ds(pl.multiple_of(side * mid_half, mid_half), mid_half)
    peer_mid_rows = pl.ds(pl.multiple_of((1 - side) * mid_half, mid_half), mid_half)
    for k in range(5):
        held = (left_mid, own_mid, right_mid)[k // 2]
        base[k, own_mid_rows] = held[0, k % 2]
        base[k, peer_mid_rows] = held[1, 1 - k % 2]
    for k in range(1, 8):
        centre = spread_ref[k // 2]
        total = spread_ref[(k - 1) // 2] + spread_ref[(k + 1) // 2] + cross_sum(centre)
        mid[k] = centre + weight * (total - 6.0 * centre)
    for k in range(5):
        centre = mid[k + 2]
        total = mid[k + 1] + mid[k + 3] + cross_sum(centre)
        value = base[k] + centre + weight * (total - 6.0 * centre)
        fine[k] = pick_left(fine_rows[...], pick_right(value, fine_depth[...]))
    for j in range(5):
        centre = fine[j]
        shared = centre + weight * (centre + cross_sum(centre) - 6.0 * centre)
        if j > 0:
            first_sweep[2 * j - 1] = shared + weight * fine[j - 1]
        if j < 4:
            first_sweep[2 * j] = shared + weight * fine[j + 1]
    for k in range(6):
        centre = first_sweep[k + 1]
        total = first_sweep[k] + first_sweep[k + 2] + cross_sum(centre)
        delta[k] = centre + weight * (total - 6.0 * centre)
    for k in range(4):
        smooth_part = (near_base if k < 2 else far_base)[k % 2]
        potential_ref[mirror(side, k, 4)] = smooth_part + delta[k + 2, own_rows]
    for k in range(2):
        at = 2 + k
        index = mirror(side, k, 2)
        out_ref[0, index] = sign * first_of([delta[at + offset] for offset in range(-2, 3)])
        own = delta[at, own_rows] + near_base[k]
        peer = delta[at, peer_rows] + peer_base[1 - k]
        even = dot_left(sum_high[...], sum_low[...], own + peer)
        odd = dot_left(diff_high[...], diff_low[...], own - peer)
        for rows, value, gradient, v, w in (
            (own_rows, own, even + odd, near_v[k], near_w[k]),
            (peer_rows, peer, even - odd, peer_vw[0, 1 - k], peer_vw[1, 1 - k]),
        ):
            keep = 1.0 - solid_ref[index, rows].astype(f32)
            out_ref[1, index, rows] = (v - gradient) * keep
            out_ref[2, index, rows] = (w - dot_right(value, depth_high[...], depth_low[...])) * keep


def stream_correction_kernel(gradient_ref, own_u, peer_u, solid_ref, out_ref):
    side = lax.axis_index("group")
    half = own_u.shape[1]
    index = pl.program_id(0)
    k = mirror(side, index, 2)
    own_rows = pl.ds(pl.multiple_of(side * half, half), half)
    peer_rows = pl.ds(pl.multiple_of((1 - side) * half, half), half)
    for rows, value in ((own_rows, own_u[k]), (peer_rows, peer_u[1 - k])):
        keep = 1.0 - solid_ref[0, rows].astype(f32)
        out_ref[0, 0, rows] = (value - gradient_ref[0, 0, rows]) * keep


def pair_sums(fine, coarse):
    return (np.arange(fine)[:, None] // 2 == np.arange(coarse)[None, :]).astype(ml_dtypes.bfloat16)


def paired(velocity, obstacle, pressure):
    rows, depth = velocity.shape[2:]
    half = rows // 2
    wide = half + 2 * HALO
    tunnel_size = lax.axis_size("tunnel")
    side = lax.axis_index("group")
    both = ("tunnel", "group")
    own, spread, basis, rows_first = half_tables(rows)
    depth_first, depth_second = wave_tables(depth)
    rows_high, rows_low = high_low(own)
    spread_high, spread_low = high_low(spread)
    spread_all = np.concatenate([spread_high, spread_high, spread_low, np.zeros_like(spread_low)], axis=1)
    basis_both = np.concatenate(high_low(basis), axis=0)
    depth_high, depth_low = high_low(np.concatenate([depth_first.T, depth_second.T], axis=1))
    sum_high, sum_low = high_low((rows_first[:half, :half] + rows_first[:half, half:]) / 2.0)
    diff_high, diff_low = high_low((rows_first[:half, :half] - rows_first[:half, half:]) / 2.0)

    def swap(value):
        return lax.ppermute(value, "group", [(0, 1), (1, 0)])

    ahead_way, behind_way = ([], [])
    for i in range(tunnel_size):
        after, before = ((i + 1) % tunnel_size, (i - 1) % tunnel_size)
        ahead_way += [(2 * i, 2 * after), (2 * i + 1, 2 * before + 1)]
        behind_way += [(2 * i, 2 * before), (2 * i + 1, 2 * after + 1)]

    def ahead(value):
        return lax.ppermute(value, both, ahead_way)

    def behind(value):
        return lax.ppermute(value, both, behind_way)

    def ahead_across(value):
        return lax.ppermute(value, both, [(i, j ^ 1) for i, j in ahead_way])

    def behind_across(value):
        return lax.ppermute(value, both, [(i, j ^ 1) for i, j in behind_way])

    def tied(value, *others):
        return lax.optimization_barrier((value,) + others)[0]

    def half_of(value, which, axis):
        return lax.dynamic_slice_in_dim(value, which * half, half, axis=axis)

    plane = (half, depth)
    two_planes, four_planes = ((2,) + plane, (4,) + plane)
    full = lambda shape: pl.BlockSpec(shape, lambda i: (0,) * len(shape))
    by_plane = lambda shape, at: pl.BlockSpec(
        shape[:at] + (1,) + shape[at + 1 :], lambda i: (0,) * at + (i,) + (0,) * (len(shape) - at - 1)
    )
    tables = (rows_high, rows_low, spread_all, depth_high, depth_low)
    table_specs = [full(table.shape) for table in tables]

    edges = jnp.concatenate([pressure[:, :HALO], pressure[:, half - HALO :]], axis=1)
    pressure_edge = swap(edges)
    tall = jnp.concatenate([pressure_edge[:, HALO:], pressure, pressure_edge[:, :HALO]], axis=1)
    to_ahead = jnp.where(side == 0, tall[1:], tall[:3])
    to_behind = jnp.where(side == 0, tall[:3], tall[1:])
    sent_uv = half_of(velocity[:2], 1 - side, 2)
    peer_uv = swap(sent_uv)
    pressure_left = ahead(to_ahead)
    pressure_right = behind(to_behind)
    raw_own, sent_w = kernel_call(
        own_planes_kernel,
        [(3, 2) + plane, (2, half + 24, depth)],
        [],
        [by_plane(velocity.shape, 1), full(basis_both.shape)] + table_specs,
        3 * 10**9,
        velocity, basis_both, *tables,
        grid=(2,),
        out_specs=[by_plane((3, 2) + plane, 1), by_plane((2, half + 24, depth), 0)],
    )
    peer_w = swap(tied(sent_w, pressure_left, pressure_right))
    own_half = half_of(tied(velocity, sent_w), side, 2)
    one = behind(own_half)
    other_uv = ahead(peer_uv)
    solid_peer = swap(half_of(obstacle, 1 - side, 1))
    solid_own = half_of(obstacle, side, 1)
    (raw_peer,) = kernel_call(
        peer_planes_kernel,
        [(3, 2) + plane],
        [],
        [by_plane((2, 2) + plane, 1), by_plane((2, half + 24, depth), 0)] + table_specs,
        3 * 10**9,
        peer_uv, peer_w, *tables,
        grid=(2,),
        out_specs=[by_plane((3, 2) + plane, 1)],
    )
    other_w = ahead(tied(peer_w, raw_peer, solid_peer)[:, :half])
    strip = 64

    def strips(count, first=0):
        return pl.BlockSpec((count, 2, strip, depth), lambda i: (first, 0, i, 0))

    flat = pl.BlockSpec((2, strip, depth), lambda i: (0, i, 0))
    near_u, far_u = kernel_call(
        star_u_kernel,
        [two_planes] * 2,
        [],
        [strips(1)] * 6 + [flat] * 2,
        10**8,
        raw_own, raw_peer, own_half, one, peer_uv, other_uv, solid_own, solid_peer,
        grid=(half // strip,),
        out_specs=[flat] * 2,
    )
    left_u, right_u = (ahead(far_u), behind(near_u))
    basis_strips = basis_both.reshape(16, half // strip, strip).transpose(1, 0, 2).copy()
    near_v, far_v, near_w, far_w, sum_v = kernel_call(
        star_vw_kernel,
        [two_planes] * 4 + [(4, 8, depth)],
        [],
        [strips(3)] * 4 + [strips(2), flat, strips(1, 1), flat, flat, flat]
        + [pl.BlockSpec((1, 16, strip), lambda i: (i, 0, 0))],
        10**8,
        raw_own, raw_peer, tied(own_half, near_u), one, peer_uv, peer_w, other_uv, other_w, solid_own, solid_peer,
        basis_strips,
        grid=(half // strip,),
        out_specs=[flat] * 4 + [full((4, 8, depth))],
    )
    peer_sum_v = swap(sum_v)
    own_depth = (depth_high[:, :depth].copy(), depth_low[:, :depth].copy())
    (cross,) = kernel_call(
        cross_kernel,
        [four_planes],
        [],
        [VMEM] * 8,
        10**9,
        near_v, far_v, near_w, far_w, rows_high, rows_low, *own_depth,
    )
    edge_shape = (4, HALO, depth)
    near_r, far_r, head_r, tail_r = kernel_call(
        source_kernel,
        [two_planes, two_planes, edge_shape, edge_shape],
        [],
        [flat] * 4
        + [pl.BlockSpec((4, strip, depth), lambda i: (0, i, 0)), full((4, 8, depth))]
        + [pl.BlockSpec((strip, spread_all.shape[1]), lambda i: (i, 0))],
        10**8,
        near_u, far_u, left_u, right_u, cross, peer_sum_v, spread_all[:half].copy(),
        grid=(half // strip,),
        out_specs=[flat, flat, full(edge_shape), full(edge_shape)],
    )
    edge_r = jnp.concatenate([head_r, tail_r], axis=1)
    left_r, right_r = (ahead(far_r), behind(near_r))
    edges = swap(edge_r)
    left_edge, right_edge = (ahead(edges[:2]), behind(edges[2:]))
    peer_vw = swap(jnp.stack([tied(far_v, left_edge, right_edge), far_w]))

    mid_rows, mid_depth = (wide // 2, depth // 2)
    message = (mid_rows + wide, depth)
    base_one, mid_source, sent_ahead, sent_behind = kernel_call(
        fine_kernel,
        [(4, wide, depth), (2, mid_rows, mid_depth), message, message],
        [
            pltpu.VMEM((8, wide, depth), f32),
            pltpu.VMEM((8, wide, depth), f32),
            pltpu.VMEM((6, wide, depth), f32),
        ],
        [VMEM] * 12,
        10**8,
        tall, pressure_left, pressure_right,
        near_r, far_r, left_r, right_r, edges, left_edge, right_edge,
        pair_sums(depth, mid_depth), pair_sums(wide, mid_rows).T,
    )
    left_one, right_one = (ahead(sent_ahead), behind(sent_behind))
    near_base, far_base = kernel_call(
        base_kernel,
        [two_planes, two_planes],
        [],
        [VMEM] * 5,
        10**8,
        base_one, left_one, right_one, near_r, far_r,
    )
    low_depth = mid_depth // 2
    halves = np.zeros((mid_depth, 2 * mid_depth), ml_dtypes.bfloat16)
    halves[:, :low_depth] = pair_sums(mid_depth, low_depth)
    halves[:, mid_depth + low_depth :] = pair_sums(mid_depth, low_depth)
    own_pairs = pair_sums(half // 2, half // 4).T
    own_pairs = np.pad(own_pairs, ((0, 0), (HALO // 2, HALO // 2)))
    mid_one, low_source = kernel_call(
        middle_kernel,
        [(2, mid_rows, mid_depth), (half // 8, mid_depth)],
        [pltpu.VMEM((6, mid_rows, mid_depth), f32), pltpu.VMEM((4, mid_rows, mid_depth), f32)],
        [VMEM] * 5,
        10**8,
        tied(mid_source, near_base), left_one, right_one, halves, own_pairs,
    )
    left_two, right_two = (ahead(mid_one[1:]), behind(mid_one[:1]))
    (mid_base,) = kernel_call(
        middle_base_kernel,
        [(2, half // 2, mid_depth)],
        [],
        [VMEM] * 4,
        10**7,
        mid_one, tied(left_two, peer_vw), right_two, mid_source,
    )
    peer_mid = swap(mid_base)
    both_mid = jnp.stack([mid_base, peer_mid])
    left_mid, right_mid = (ahead(both_mid), behind(both_mid))
    low_all = lax.all_to_all(
        jnp.broadcast_to(tied(low_source, mid_base), (2 * tunnel_size,) + low_source.shape), both, 0, 0, tiled=True
    )
    left_b, right_b = (ahead(tied(far_base, mid_base)), behind(tied(near_base, mid_base)))
    peer_base = swap(tied(far_base, peer_mid))
    low_plane = (half // 2, mid_depth)
    mid_plane = (half, mid_depth)
    expand_low = np.zeros((mid_depth, mid_depth), ml_dtypes.bfloat16)
    expand_low[:low_depth] = pair_sums(mid_depth, low_depth).T
    (spread_low,) = kernel_call(
        coarsest_kernel,
        [(5,) + mid_plane],
        [pltpu.VMEM((11,) + low_plane, f32)] * 3,
        [VMEM] * 3,
        10**7,
        low_all, expand_low, pair_sums(half, half // 2),
    )
    own_u, sent_u = kernel_call(
        stream_kernel,
        [two_planes, two_planes],
        [],
        [VMEM] * 6,
        10**8,
        near_base, far_base, left_b, tied(right_b, spread_low, left_mid, right_mid), near_u, far_u,
    )
    peer_u = swap(sent_u)
    fine_plane = (rows, depth)
    corrected, potential = kernel_call(
        correction_kernel,
        [(3, 2) + fine_plane, four_planes],
        [
            pltpu.VMEM((5,) + mid_plane, f32),
            pltpu.VMEM((9,) + mid_plane, f32),
            pltpu.VMEM((5,) + fine_plane, f32),
            pltpu.VMEM((8,) + fine_plane, f32),
            pltpu.VMEM((6,) + fine_plane, f32),
        ],
        [VMEM] * 19,
        10**9,
        spread_low, both_mid, left_mid, right_mid, near_base, far_base, peer_base, near_v, near_w, peer_vw, obstacle,
        sum_high, sum_low, diff_high, diff_low, *own_depth,
        pair_sums(depth, mid_depth).T.copy(), pair_sums(rows, half),
    )
    stream = pl.BlockSpec((1, 1) + fine_plane, lambda i: (0, i, 0, 0))
    (corrected,) = kernel_call(
        stream_correction_kernel,
        [corrected.shape],
        [],
        [stream] + [full(two_planes)] * 2 + [by_plane(obstacle.shape, 0)],
        10**7,
        corrected, own_u, peer_u, obstacle,
        grid=(2,),
        out_specs=[stream],
        aliases={0: 0},
    )
    return (corrected, potential)


def step(velocity, obstacle, pressure):
    planes, rows, depth = velocity.shape[1:]
    fits = lax.axis_size("group") == 2 and planes == 2 and pressure.shape[0] == 4
    fits = fits and lax.axis_size("tunnel") > 10 and rows % 512 == 0 and depth % 256 == 0
    if fits:
        return paired(velocity, obstacle, pressure)
    return local(velocity, obstacle, pressure)


def solution(mesh):
    in_specs = (
        P(None, ("tunnel", "group"), None, None),
        P(("tunnel", "group"), None, None),
        P("tunnel", "group", None),
    )
    out_specs = (P(None, ("tunnel", "group"), None, None), P("tunnel", "group", None))
    return jax.shard_map(step, mesh=mesh, in_specs=in_specs, out_specs=out_specs, check_vma=False)
```

```python
import math

import jax
import jax.numpy as jnp
import ml_dtypes
import numpy as np
from jax import lax
from jax.experimental import pallas as pl
from jax.experimental.pallas import tpu as pltpu
from jax.sharding import PartitionSpec as P

LEVELS = 3
SWEEPS = 2
COARSE_SWEEPS = 4


time_step = 0.1
viscosity = 0.05
relax_weight = 0.8
highest = lax.Precision.HIGHEST


def extended(value, sides, width):
    for axis, dim in sides:
        size, length = (lax.axis_size(axis), value.shape[dim])
        up = [(i, (i + 1) % size) for i in range(size)]
        down = [(j, i) for i, j in up]
        last = lax.slice_in_dim(value, length - width, length, axis=dim)
        initial = lax.slice_in_dim(value, 0, width, axis=dim)
        before = lax.ppermute(last, axis, up)
        after = lax.ppermute(initial, axis, down)
        value = jnp.concatenate([before, value, after], axis=dim)
    return value


def compact_tables(count):
    indices = jnp.arange(count, dtype=jnp.int32)
    product = indices[:, None] * indices[None, :] % count
    angles = product.astype(jnp.float32) * (2.0 * math.pi / count)
    cosines = jnp.cos(angles)
    sines = jnp.sin(angles)
    theta = indices.astype(jnp.float32) * (2.0 * math.pi / count)
    first_wave = (14.0 / 9.0 * jnp.sin(theta) + jnp.sin(2.0 * theta) / 18.0) / (
        1.0 + 2.0 / 3.0 * jnp.cos(theta)
    )
    second_wave = (
        24.0 / 11.0 * (1.0 - jnp.cos(theta)) + 3.0 / 22.0 * (1.0 - jnp.cos(2.0 * theta))
    ) / (1.0 + 4.0 / 11.0 * jnp.cos(theta))
    first_matrix = (
        jnp.dot(cosines * first_wave, sines.T, precision=highest)
        - jnp.dot(sines * first_wave, cosines.T, precision=highest)
    ) / count
    second_matrix = (
        -(
            jnp.dot(cosines * second_wave, cosines.T, precision=highest)
            + jnp.dot(sines * second_wave, sines.T, precision=highest)
        )
        / count
    )
    return (first_matrix, second_matrix)


def along_rows(matrix, field):
    return jnp.einsum("ij,...jz->...iz", matrix, field, precision=highest)


def along_depth(matrix, field):
    return jnp.einsum("...j,ij->...i", field, matrix, precision=highest)


def shifted(padded, offset, axis):
    count = padded.shape[axis] - 4
    return lax.slice_in_dim(padded, 2 + offset, 2 + offset + count, axis=axis)


def stream_first(padded, axis):
    ahead = shifted(padded, 1, axis) - shifted(padded, -1, axis)
    further = shifted(padded, 2, axis) - shifted(padded, -2, axis)
    return (8.0 * ahead - further) / 12.0


def stream_second(padded, axis):
    ahead = shifted(padded, 1, axis) + shifted(padded, -1, axis)
    further = shifted(padded, 2, axis) + shifted(padded, -2, axis)
    return (16.0 * ahead - further - 30.0 * shifted(padded, 0, axis)) / 12.0


def padded_neighbours(padded):
    interior = padded[1:-1, 1:-1]
    total = padded[2:, 1:-1] + padded[:-2, 1:-1]
    total = total + padded[1:-1, 2:] + padded[1:-1, :-2]
    return total + jnp.roll(interior, -1, 2) + jnp.roll(interior, 1, 2)


def relax_padded(padded, source_term, scale):
    interior = padded[1:-1, 1:-1]
    return interior + relax_weight / 6.0 * (
        padded_neighbours(padded) - 6.0 * interior - scale * source_term
    )


def faces(field):
    return extended(field, (("tunnel", 0), ("group", 1)), 1)


def thin_sweeps(field, source_term, scale, count):
    for sweep_index in range(count):
        field = relax_padded(faces(field), source_term, scale)
    return field


def smooth(field, source_term, scale, level):
    if level == 0:
        return thin_sweeps(field, source_term, scale, SWEEPS)
    return thin_sweeps(field, source_term, scale, SWEEPS)


def coarsest(source_term, scale):
    return thin_sweeps(jnp.zeros_like(source_term), source_term, scale, COARSE_SWEEPS)


def restrict(field):
    planes, rows, depth = field.shape
    blocks = field.reshape(planes // 2, 2, rows // 2, 2, depth // 2, 2)
    return jnp.sum(blocks, axis=(1, 3, 5)) * 0.125


def prolong(field):
    return jnp.repeat(jnp.repeat(jnp.repeat(field, 2, 0), 2, 1), 2, 2)


def cycle(field, source_term, level):
    scale = 4.0**level
    if level == LEVELS - 1:
        return coarsest(source_term, scale)
    field = smooth(field, source_term, scale, level)
    leftover = source_term - (padded_neighbours(faces(field)) - 6.0 * field) / scale
    coarse_source = restrict(leftover)
    coarse = cycle(jnp.zeros_like(coarse_source), coarse_source, level + 1)
    field = field + prolong(coarse)
    return smooth(field, source_term, scale, level)


def local(velocity, obstacle, pressure):
    row_count = velocity.shape[2]
    depth_count = velocity.shape[3]
    rows_first, rows_second = compact_tables(row_count)
    depth_first, depth_second = compact_tables(depth_count)
    rows_both = jnp.concatenate([rows_first, rows_second], axis=0)
    depth_both = jnp.concatenate([depth_first, depth_second], axis=0)
    keep = 1.0 - obstacle.astype(jnp.float32)
    row_terms = along_rows(rows_both, velocity)
    depth_terms = along_depth(depth_both, velocity)
    transverse = (
        velocity[1] * row_terms[:, :, :row_count] + velocity[2] * depth_terms[..., :depth_count]
    )
    diffusion = row_terms[:, :, row_count:] + depth_terms[..., depth_count:]
    padded = extended(velocity, ((("tunnel", "group"), 1),), 2)
    streamwise = -velocity[0] * stream_first(padded, 1) + viscosity * stream_second(padded, 1)
    tendency = streamwise - transverse + viscosity * diffusion
    star = (velocity + time_step * tendency) * keep
    star_padded = extended(star[0], ((("tunnel", "group"), 0),), 2)
    source = (
        stream_first(star_padded, 0)
        + along_rows(rows_first, star[1])
        + along_depth(depth_first, star[2])
    )
    source_tile = lax.all_to_all(source, "group", split_axis=1, concat_axis=0, tiled=True)
    potential = cycle(pressure, source_tile, 0)
    potential_padded = extended(potential, (("tunnel", 0),), 2)
    streamwise_grad = stream_first(potential_padded, 0)
    returned = lax.all_to_all(
        jnp.stack([potential, streamwise_grad]), "group", split_axis=1, concat_axis=2, tiled=True
    )
    gradient = jnp.stack(
        [returned[1], along_rows(rows_first, returned[0]), along_depth(depth_first, returned[0])]
    )
    corrected = (star - gradient) * keep
    return (corrected, potential)


HALO = 16
weight = relax_weight / 6.0
bf16 = jnp.bfloat16
f32 = jnp.float32
VMEM = pl.BlockSpec(memory_space=pltpu.VMEM)
ANY = pl.BlockSpec(memory_space=pl.ANY)


def wave_tables(count):
    index = np.arange(count)
    angles = 2.0 * np.pi * (np.outer(index, index) % count) / count
    theta = 2.0 * np.pi * index / count
    first_wave = (14.0 / 9.0 * np.sin(theta) + np.sin(2.0 * theta) / 18.0) / (
        1.0 + 2.0 / 3.0 * np.cos(theta)
    )
    second_wave = (
        24.0 / 11.0 * (1.0 - np.cos(theta)) + 3.0 / 22.0 * (1.0 - np.cos(2.0 * theta))
    ) / (1.0 + 4.0 / 11.0 * np.cos(theta))
    cosines, sines = (np.cos(angles), np.sin(angles))
    first = ((cosines * first_wave) @ sines.T - (sines * first_wave) @ cosines.T) / count
    second = -((cosines * second_wave) @ cosines.T + (sines * second_wave) @ sines.T) / count
    return (first, second)


def high_low(table):
    high = table.astype(np.float32).astype(ml_dtypes.bfloat16)
    low = (table - high.astype(np.float64)).astype(np.float32).astype(ml_dtypes.bfloat16)
    return (high, low)


def half_tables(count):
    first, second = wave_tables(count)
    half = count // 2
    index = np.arange(half)
    root_first = (math.sqrt(5.0) - 3.0) / 2.0
    root_second = (math.sqrt(105.0) - 11.0) / 4.0
    basis = np.zeros((8, half))
    basis[0, 0] = 1.0
    basis[1, -1] = 1.0
    basis[2] = root_first**index
    basis[3] = basis[2][::-1]
    basis[4] = root_second**index
    basis[5] = basis[4][::-1]
    spread = []
    for table, used in ((first, (0, 1, 2, 3)), (second, (0, 1, 4, 5))):
        solved = np.linalg.lstsq(basis[list(used)].T, table[:half, half:].T, rcond=None)[0].T
        wide = np.zeros((half, 8))
        wide[:, list(used)] = solved
        spread.append(wide)
    own = np.concatenate([first[:half, :half], second[:half, :half]], axis=0)
    return (own, np.concatenate(spread, axis=0), basis, first)


def split(value):
    high = value.astype(bf16)
    low = (value - high.astype(f32)).astype(bf16)
    return (high, low)


def dot(left, right):
    return jnp.dot(left, right, preferred_element_type=f32)


def dot_left(table_high, table_low, value):
    high, low = split(value)
    return dot(table_high, high) + (dot(table_high, low) + dot(table_low, high))


def dot_right(value, table_high, table_low):
    high, low = split(value)
    return dot(high, table_high) + (dot(low, table_high) + dot(high, table_low))


def pick_left(zero_one, value):
    high, low = split(value)
    return dot(zero_one, high) + dot(zero_one, low)


def pick_right(value, zero_one):
    high, low = split(value)
    return dot(high, zero_one) + dot(low, zero_one)


def summary(basis_both, value):
    high, low = split(value)
    main = dot(basis_both, high)
    rest = dot(basis_both, low)
    return main[:8] + main[8:] + rest[:8]


def summary_operand(value):
    high = value.astype(bf16).astype(f32)
    return jnp.concatenate([high, value - high, high, jnp.zeros_like(high)], axis=0).astype(bf16)


def turn(value, shift, axis):
    return pltpu.roll(value, shift % value.shape[axis], axis)


def cross_sum(value):
    return (turn(value, 1, 0) + turn(value, -1, 0)) + (turn(value, 1, 1) + turn(value, -1, 1))


def first_of(values):
    return (8.0 * (values[3] - values[1]) - (values[4] - values[0])) * (1.0 / 12.0)


def second_of(values):
    return (
        16.0 * (values[3] + values[1]) - (values[4] + values[0]) - 30.0 * values[2]
    ) * (1.0 / 12.0)


def kernel_call(body, outs, scratch, specs, flops, *args, grid=None, out_specs=None, aliases=None):
    total = sum(math.prod(a.shape) * a.dtype.itemsize for a in args)
    total += sum(4 * math.prod(s) for s in outs)
    options = {} if grid is None else {"grid": grid}
    if aliases is not None:
        options["input_output_aliases"] = aliases
    return pl.pallas_call(
        body,
        out_shape=[jax.ShapeDtypeStruct(s, f32) for s in outs],
        in_specs=specs,
        out_specs=[VMEM] * len(outs) if out_specs is None else out_specs,
        scratch_shapes=scratch,
        compiler_params=pltpu.CompilerParams(vmem_limit_bytes=36 * 1024 * 1024),
        cost_estimate=pl.CostEstimate(flops=flops, bytes_accessed=total if flops > 1 else 1, transcendentals=0),
        **options,
    )(*args)


def mirror(side, index, count):
    return index + side * (count - 1 - 2 * index)


def sign_of(side):
    return (1 - 2 * side).astype(f32)


def transverse(u, v, w, value, other_sum, rows_high, rows_low, spread, depth_high, depth_low):
    half, width = value.shape
    high, low = split(value)
    across = (
        dot(rows_high[...], high)
        + (dot(rows_high[...], low) + dot(rows_low[...], high))
        + dot(spread[...], summary_operand(other_sum))
    )
    along = dot(high, depth_high[...]) + (dot(low, depth_high[...]) + dot(high, depth_low[...]))
    advect = v * across[:half] + w * along[:, :width]
    return value + time_step * (viscosity * (across[half:] + along[:, width:]) - advect)


def own_planes_kernel(
    velocity_ref, basis_ref, rows_high, rows_low, spread, depth_high, depth_low, out_ref, sent_ref
):
    side = lax.axis_index("group")
    half = basis_ref.shape[1]
    own = pl.ds(pl.multiple_of(side * half, half), half)
    other = pl.ds(pl.multiple_of((1 - side) * half, half), half)
    u, v, w = (velocity_ref[c, 0, own] for c in range(3))
    sent_ref[0, :half] = velocity_ref[2, 0, other]
    for c in range(3):
        value = velocity_ref[c, 0, own]
        kept = summary(basis_ref[...], velocity_ref[c, 0, other])
        sent_ref[0, half + 8 * c : half + 8 * c + 8] = summary(basis_ref[...], value)
        out_ref[c, 0] = transverse(u, v, w, value, kept, rows_high, rows_low, spread, depth_high, depth_low)


def peer_planes_kernel(
    uv_ref, w_ref, rows_high, rows_low, spread, depth_high, depth_low, out_ref
):
    half = uv_ref.shape[2]
    u, v, w = (uv_ref[0, 0], uv_ref[1, 0], w_ref[0, :half])
    for c in range(3):
        other_sum = w_ref[0, half + 8 * c : half + 8 * c + 8]
        out_ref[c, 0] = transverse(
            u, v, w, (u, v, w)[c], other_sum, rows_high, rows_low, spread, depth_high, depth_low
        )


def star_planes(side, planes, raws, solids, u_of, outs):
    sign = sign_of(side) * (time_step / 12.0)
    for plane in range(4):
        index = mirror(side, plane % 2, 2)
        keep = 1.0 - solids[plane // 2][index].astype(f32)
        near = planes[plane : plane + 5]
        first = 8.0 * (near[3] - near[1]) - (near[4] - near[0])
        second = 16.0 * (near[3] + near[1]) - (near[4] + near[0]) - 30.0 * near[2]
        raw = raws[plane // 2][index]
        outs[plane // 2][plane % 2] = (
            raw + (time_step * viscosity / 12.0) * second - (u_of(plane) * sign) * first
        ) * keep


def eight(side, groups):
    return [group[mirror(side, k, 2)] for group in groups for k in range(2)]


def star_u_kernel(raw_own, raw_peer, own_ref, one_ref, peers, others, solid_own, solid_peer, near_ref, far_ref):
    side = lax.axis_index("group")
    planes = eight(side, (others.at[0], own_ref.at[0], peers.at[0], one_ref.at[0]))
    star_planes(
        side, planes, (raw_own.at[0], raw_peer.at[0]), (solid_own, solid_peer),
        lambda plane: planes[plane + 2], (near_ref, far_ref),
    )


def star_vw_kernel(
    raw_own, raw_peer, own_ref, one_ref, peers, peer_w, others, other_w, solid_own, solid_peer, basis_ref,
    near_v, far_v, near_w, far_w, sum_ref,
):
    side = lax.axis_index("group")
    step = pl.program_id(0)

    def u_of(plane):
        return (own_ref if plane < 2 else peers)[0, mirror(side, plane % 2, 2)]

    for c, peer, other, outs in (
        (1, peers.at[1], others.at[0], (near_v, far_v)),
        (2, peer_w, other_w, (near_w, far_w)),
    ):
        planes = eight(side, (other, own_ref.at[c], peer, one_ref.at[c]))
        star_planes(side, planes, (raw_own.at[c], raw_peer.at[c]), (solid_own, solid_peer), u_of, outs)

    @pl.when(step == 0)
    def _():
        sum_ref[...] = jnp.zeros_like(sum_ref)

    for plane in range(4):
        sum_ref[plane] += summary(basis_ref[0], (near_v if plane < 2 else far_v)[plane % 2])


def cross_kernel(near_v, far_v, near_w, far_w, rows_high, rows_low, depth_high, depth_low, out_ref):
    half = near_v.shape[1]
    for plane in range(4):
        v, w = ((near_v, near_w) if plane < 2 else (far_v, far_w))
        out_ref[plane] = dot_left(rows_high[:half], rows_low[:half], v[plane % 2]) + dot_right(
            w[plane % 2], depth_high[...], depth_low[...]
        )


def source_kernel(
    near_u, far_u, left_ref, right_ref, cross_ref, sum_ref, spread, near_r, far_r, head, tail
):
    sign = sign_of(lax.axis_index("group"))
    rows = cross_ref.shape[1]
    step = pl.program_id(0)
    planes = [ref[k] for ref in (left_ref, near_u, far_u, right_ref) for k in range(2)]
    values = []
    for plane in range(4):
        value = sign * first_of(planes[plane : plane + 5]) + cross_ref[plane]
        value = value + dot(spread[...], summary_operand(sum_ref[3 - plane]))
        (near_r if plane < 2 else far_r)[plane % 2] = value
        values.append(value)

    @pl.when(step == 0)
    def _():
        for plane in range(4):
            head[plane] = values[plane][:HALO]

    @pl.when(step == pl.num_programs(0) - 1)
    def _():
        for plane in range(4):
            tail[plane] = values[plane][rows - HALO :]


def fine_kernel(
    pressure_tall, pressure_left, pressure_right,
    near_r, far_r, left_ref, right_ref, edge_ref, left_edge, right_edge, depth_pick, rows_pick,
    base_ref, coarse_ref, ahead_ref, behind_ref, source_ref, one, two,
):
    side = lax.axis_index("group")
    half = near_r.shape[1]

    def fill(target, at, body, edge):
        target[at, HALO : HALO + half] = body
        target[at, :HALO] = edge[HALO:]
        target[at, HALO + half :] = edge[:HALO]

    for plane in range(2):
        fill(source_ref, plane, left_ref[plane], left_edge[1 - plane])
        fill(source_ref, 2 + plane, near_r[plane], edge_ref[3 - plane])
        fill(source_ref, 4 + plane, far_r[plane], edge_ref[1 - plane])
        fill(source_ref, 6 + plane, right_ref[plane], right_edge[1 - plane])
    pressure = [pressure_left.at[mirror(side, k, 3)] for k in range(3)]
    pressure += [pressure_tall.at[mirror(side, k, 4)] for k in range(4)]
    pressure += [pressure_right.at[mirror(side, k, 3)] for k in range(3)]
    for k in range(8):
        centre = pressure[k + 1][...]
        total = pressure[k][...] + pressure[k + 2][...] + cross_sum(centre)
        one[k] = centre + weight * (total - 6.0 * centre - source_ref[k])
    for k in range(6):
        centre = one[k + 1]
        total = one[k] + one[k + 2] + cross_sum(centre)
        two[k] = centre + weight * (total - 6.0 * centre - source_ref[k + 1])
    for pair in range(2):
        left = []
        for k in (2 * pair, 2 * pair + 1):
            centre = two[k + 1]
            total = two[k] + two[k + 2] + cross_sum(centre)
            residual = source_ref[k + 2] - (total - 6.0 * centre)
            base_ref[k] = centre - weight * residual
            left.append(residual)
        coarse = 0.125 * pick_left(rows_pick[...], pick_right(left[0] + left[1], depth_pick[...]))
        coarse_ref[pair] = coarse
        rows, width = coarse.shape
        ahead_ref[:rows, width * pair : width * (pair + 1)] = coarse
        behind_ref[:rows, width * pair : width * (pair + 1)] = coarse
    ahead_ref[rows:] = base_ref[3]
    behind_ref[rows:] = base_ref[0]


def middle_kernel(own_ref, left_ref, right_ref, depth_pick, rows_pick, base_ref, coarse_ref, one, two):
    rows, width = own_ref.shape[1:]
    source = []
    for ref in (left_ref, own_ref, right_ref):
        for k in range(2):
            source.append(ref[k] if ref is own_ref else ref[:rows, width * k : width * (k + 1)])
    for k in range(6):
        one[k] = (-4.0 * weight) * source[k]
    for k in range(4):
        centre = one[k + 1]
        total = one[k] + one[k + 2] + cross_sum(centre)
        two[k] = centre + weight * (total - 6.0 * centre - 4.0 * source[k + 1])
    left = []
    for k in range(2):
        centre = two[k + 1]
        total = two[k] + two[k + 2] + cross_sum(centre)
        residual = source[k + 2] - 0.25 * (total - 6.0 * centre)
        base_ref[k] = centre - (4.0 * weight) * residual
        left.append(residual)
    width = own_ref.shape[2]
    wide = pick_right(left[0] + left[1], depth_pick[...])
    count = coarse_ref.shape[0]
    coarse_ref[...] = 0.125 * (
        pick_left(rows_pick[:count], wide[:, :width]) + pick_left(rows_pick[count:], wide[:, width:])
    )


def middle_base_kernel(base_ref, left_ref, right_ref, source_ref, out_ref):
    rows = out_ref.shape[1]
    planes = [left_ref[0], base_ref[0], base_ref[1], right_ref[0]]
    for k in range(2):
        centre = planes[k + 1]
        total = planes[k] + planes[k + 2] + cross_sum(centre)
        value = centre + weight * (total - 6.0 * centre - 4.0 * source_ref[k])
        out_ref[k] = value[HALO // 2 : HALO // 2 + rows]


def base_kernel(base_ref, left_ref, right_ref, near_r, far_r, near_ref, far_ref):
    rows = near_ref.shape[1]
    skip = left_ref.shape[0] - base_ref.shape[1]
    for k in range(4):
        before = left_ref[skip:] if k == 0 else base_ref[k - 1]
        after = right_ref[skip:] if k == 3 else base_ref[k + 1]
        centre = base_ref[k]
        total = before + after + cross_sum(centre)
        value = (centre + weight * (total - 6.0 * centre))[HALO : HALO + rows]
        source, out = ((near_r, near_ref) if k < 2 else (far_r, far_ref))
        out[k % 2] = value - weight * source[k % 2]


def stream_kernel(near_ref, far_ref, left_ref, right_ref, near_u, far_u, own_ref, sent_ref):
    sign = sign_of(lax.axis_index("group"))
    planes = [ref[k] for ref in (left_ref, near_ref, far_ref, right_ref) for k in range(2)]
    for plane in range(4):
        star = (near_u if plane < 2 else far_u)[plane % 2]
        (own_ref if plane < 2 else sent_ref)[plane % 2] = star - sign * first_of(planes[plane : plane + 5])


def coarsest_kernel(all_ref, mid_depth, mid_rows, out_ref, source, one, two):
    place = lax.axis_index("tunnel")
    step = 1 - 2 * lax.axis_index("group")
    count = all_ref.shape[0] // 2
    quarter, width = all_ref.shape[1:]
    lower = lax.broadcasted_iota(jnp.int32, (quarter, width), 1) < width // 2
    for k in range(11):
        plane = lax.rem(place + step * (k - 5) + 2 * count, count)
        for part in range(2):
            packed = all_ref[2 * plane + part]
            turned = turn(packed, width // 2, 1)
            source[k, 2 * part * quarter : (2 * part + 1) * quarter] = jnp.where(lower, packed, turned)
            source[k, (2 * part + 1) * quarter : (2 * part + 2) * quarter] = jnp.where(lower, turned, packed)
    for k in range(11):
        one[k] = (-16.0 * weight) * source[k]
    source_at, target = (one, two)
    for sweep_index in range(1, COARSE_SWEEPS):
        for k in range(sweep_index, 11 - sweep_index):
            centre = source_at[k]
            total = source_at[k - 1] + source_at[k + 1] + cross_sum(centre)
            target[k] = centre + weight * (total - 6.0 * centre - 16.0 * source[k])
        source_at, target = (target, source_at)
    for k in range(5):
        out_ref[k] = pick_left(mid_rows[...], pick_right(source_at[k + 3], mid_depth[...]))


def correction_kernel(
    spread_ref, own_mid, left_mid, right_mid,
    near_base, far_base, peer_base, near_v, near_w, peer_vw, solid_ref,
    sum_high, sum_low, diff_high, diff_low, depth_high, depth_low, fine_depth, fine_rows,
    out_ref, potential_ref, base, mid, fine, first_sweep, delta,
):
    side = lax.axis_index("group")
    sign = sign_of(side)
    half = near_v.shape[1]
    own_rows = pl.ds(pl.multiple_of(side * half, half), half)
    peer_rows = pl.ds(pl.multiple_of((1 - side) * half, half), half)
    mid_half = own_mid.shape[2]
    own_mid_rows = pl.ds(pl.multiple_of(side * mid_half, mid_half), mid_half)
    peer_mid_rows = pl.ds(pl.multiple_of((1 - side) * mid_half, mid_half), mid_half)
    for k in range(5):
        held = (left_mid, own_mid, right_mid)[k // 2]
        base[k, own_mid_rows] = held[0, k % 2]
        base[k, peer_mid_rows] = held[1, 1 - k % 2]
    for k in range(1, 8):
        centre = spread_ref[k // 2]
        total = spread_ref[(k - 1) // 2] + spread_ref[(k + 1) // 2] + cross_sum(centre)
        mid[k] = centre + weight * (total - 6.0 * centre)
    for k in range(5):
        centre = mid[k + 2]
        total = mid[k + 1] + mid[k + 3] + cross_sum(centre)
        value = base[k] + centre + weight * (total - 6.0 * centre)
        fine[k] = pick_left(fine_rows[...], pick_right(value, fine_depth[...]))
    for j in range(5):
        centre = fine[j]
        shared = centre + weight * (centre + cross_sum(centre) - 6.0 * centre)
        if j > 0:
            first_sweep[2 * j - 1] = shared + weight * fine[j - 1]
        if j < 4:
            first_sweep[2 * j] = shared + weight * fine[j + 1]
    for k in range(6):
        centre = first_sweep[k + 1]
        total = first_sweep[k] + first_sweep[k + 2] + cross_sum(centre)
        delta[k] = centre + weight * (total - 6.0 * centre)
    for k in range(4):
        smooth_part = (near_base if k < 2 else far_base)[k % 2]
        potential_ref[mirror(side, k, 4)] = smooth_part + delta[k + 2, own_rows]
    for k in range(2):
        at = 2 + k
        index = mirror(side, k, 2)
        out_ref[0, index] = sign * first_of([delta[at + offset] for offset in range(-2, 3)])
        own = delta[at, own_rows] + near_base[k]
        peer = delta[at, peer_rows] + peer_base[1 - k]
        even = dot_left(sum_high[...], sum_low[...], own + peer)
        odd = dot_left(diff_high[...], diff_low[...], own - peer)
        for rows, value, gradient, v, w in (
            (own_rows, own, even + odd, near_v[k], near_w[k]),
            (peer_rows, peer, even - odd, peer_vw[0, 1 - k], peer_vw[1, 1 - k]),
        ):
            keep = 1.0 - solid_ref[index, rows].astype(f32)
            out_ref[1, index, rows] = (v - gradient) * keep
            out_ref[2, index, rows] = (w - dot_right(value, depth_high[...], depth_low[...])) * keep


def stream_correction_kernel(gradient_ref, own_u, peer_u, solid_ref, out_ref):
    side = lax.axis_index("group")
    half = own_u.shape[1]
    index = pl.program_id(0)
    k = mirror(side, index, 2)
    own_rows = pl.ds(pl.multiple_of(side * half, half), half)
    peer_rows = pl.ds(pl.multiple_of((1 - side) * half, half), half)
    for rows, value in ((own_rows, own_u[k]), (peer_rows, peer_u[1 - k])):
        keep = 1.0 - solid_ref[0, rows].astype(f32)
        out_ref[0, 0, rows] = (value - gradient_ref[0, 0, rows]) * keep


def pair_sums(fine, coarse):
    return (np.arange(fine)[:, None] // 2 == np.arange(coarse)[None, :]).astype(ml_dtypes.bfloat16)


def paired(velocity, obstacle, pressure):
    rows, depth = velocity.shape[2:]
    half = rows // 2
    wide = half + 2 * HALO
    tunnel_size = lax.axis_size("tunnel")
    side = lax.axis_index("group")
    both = ("tunnel", "group")
    own, spread, basis, rows_first = half_tables(rows)
    depth_first, depth_second = wave_tables(depth)
    rows_high, rows_low = high_low(own)
    spread_high, spread_low = high_low(spread)
    spread_all = np.concatenate([spread_high, spread_high, spread_low, np.zeros_like(spread_low)], axis=1)
    basis_both = np.concatenate(high_low(basis), axis=0)
    depth_high, depth_low = high_low(np.concatenate([depth_first.T, depth_second.T], axis=1))
    sum_high, sum_low = high_low((rows_first[:half, :half] + rows_first[:half, half:]) / 2.0)
    diff_high, diff_low = high_low((rows_first[:half, :half] - rows_first[:half, half:]) / 2.0)

    def swap(value):
        return lax.ppermute(value, "group", [(0, 1), (1, 0)])

    ahead_way, behind_way = ([], [])
    for i in range(tunnel_size):
        after, before = ((i + 1) % tunnel_size, (i - 1) % tunnel_size)
        ahead_way += [(2 * i, 2 * after), (2 * i + 1, 2 * before + 1)]
        behind_way += [(2 * i, 2 * before), (2 * i + 1, 2 * after + 1)]

    def ahead(value):
        return lax.ppermute(value, both, ahead_way)

    def behind(value):
        return lax.ppermute(value, both, behind_way)

    def ahead_across(value):
        return lax.ppermute(value, both, [(i, j ^ 1) for i, j in ahead_way])

    def behind_across(value):
        return lax.ppermute(value, both, [(i, j ^ 1) for i, j in behind_way])

    def tied(value, *others):
        return lax.optimization_barrier((value,) + others)[0]

    def half_of(value, which, axis):
        return lax.dynamic_slice_in_dim(value, which * half, half, axis=axis)

    plane = (half, depth)
    two_planes, four_planes = ((2,) + plane, (4,) + plane)
    full = lambda shape: pl.BlockSpec(shape, lambda i: (0,) * len(shape))
    by_plane = lambda shape, at: pl.BlockSpec(
        shape[:at] + (1,) + shape[at + 1 :], lambda i: (0,) * at + (i,) + (0,) * (len(shape) - at - 1)
    )
    tables = (rows_high, rows_low, spread_all, depth_high, depth_low)
    table_specs = [full(table.shape) for table in tables]

    edges = jnp.concatenate([pressure[:, :HALO], pressure[:, half - HALO :]], axis=1)
    pressure_edge = swap(edges)
    tall = jnp.concatenate([pressure_edge[:, HALO:], pressure, pressure_edge[:, :HALO]], axis=1)
    to_ahead = jnp.where(side == 0, tall[1:], tall[:3])
    to_behind = jnp.where(side == 0, tall[:3], tall[1:])
    sent_uv = half_of(velocity[:2], 1 - side, 2)
    peer_uv = swap(sent_uv)
    pressure_left = ahead(to_ahead)
    pressure_right = behind(to_behind)
    raw_own, sent_w = kernel_call(
        own_planes_kernel,
        [(3, 2) + plane, (2, half + 24, depth)],
        [],
        [by_plane(velocity.shape, 1), full(basis_both.shape)] + table_specs,
        3 * 10**9,
        velocity, basis_both, *tables,
        grid=(2,),
        out_specs=[by_plane((3, 2) + plane, 1), by_plane((2, half + 24, depth), 0)],
    )
    peer_w = swap(tied(sent_w, pressure_left, pressure_right))
    own_half = half_of(tied(velocity, sent_w), side, 2)
    one = behind(own_half)
    other_uv = ahead(tied(peer_uv, sent_w))
    other_w = ahead(peer_w[:, :half])
    solid_peer = swap(half_of(obstacle, 1 - side, 1))
    solid_own = half_of(obstacle, side, 1)
    (raw_peer,) = kernel_call(
        peer_planes_kernel,
        [(3, 2) + plane],
        [],
        [by_plane((2, 2) + plane, 1), by_plane((2, half + 24, depth), 0)] + table_specs,
        3 * 10**9,
        peer_uv, peer_w, *tables,
        grid=(2,),
        out_specs=[by_plane((3, 2) + plane, 1)],
    )
    strip = 64

    def strips(count, first=0):
        return pl.BlockSpec((count, 2, strip, depth), lambda i: (first, 0, i, 0))

    flat = pl.BlockSpec((2, strip, depth), lambda i: (0, i, 0))
    near_u, far_u = kernel_call(
        star_u_kernel,
        [two_planes] * 2,
        [],
        [strips(1)] * 6 + [flat] * 2,
        10**8,
        raw_own, raw_peer, own_half, one, peer_uv, other_uv, solid_own, solid_peer,
        grid=(half // strip,),
        out_specs=[flat] * 2,
    )
    left_u, right_u = (ahead(far_u), behind(near_u))
    basis_strips = basis_both.reshape(16, half // strip, strip).transpose(1, 0, 2).copy()
    near_v, far_v, near_w, far_w, sum_v = kernel_call(
        star_vw_kernel,
        [two_planes] * 4 + [(4, 8, depth)],
        [],
        [strips(3)] * 4 + [strips(2), flat, strips(1, 1), flat, flat, flat]
        + [pl.BlockSpec((1, 16, strip), lambda i: (i, 0, 0))],
        10**8,
        raw_own, raw_peer, tied(own_half, near_u), one, peer_uv, peer_w, other_uv, other_w, solid_own, solid_peer,
        basis_strips,
        grid=(half // strip,),
        out_specs=[flat] * 4 + [full((4, 8, depth))],
    )
    peer_sum_v = swap(sum_v)
    own_depth = (depth_high[:, :depth].copy(), depth_low[:, :depth].copy())
    (cross,) = kernel_call(
        cross_kernel,
        [four_planes],
        [],
        [VMEM] * 8,
        10**9,
        near_v, far_v, near_w, far_w, rows_high, rows_low, *own_depth,
    )
    edge_shape = (4, HALO, depth)
    near_r, far_r, head_r, tail_r = kernel_call(
        source_kernel,
        [two_planes, two_planes, edge_shape, edge_shape],
        [],
        [flat] * 4
        + [pl.BlockSpec((4, strip, depth), lambda i: (0, i, 0)), full((4, 8, depth))]
        + [pl.BlockSpec((strip, spread_all.shape[1]), lambda i: (i, 0))],
        10**8,
        near_u, far_u, left_u, right_u, cross, peer_sum_v, spread_all[:half].copy(),
        grid=(half // strip,),
        out_specs=[flat, flat, full(edge_shape), full(edge_shape)],
    )
    edge_r = jnp.concatenate([head_r, tail_r], axis=1)
    left_r, right_r = (ahead(far_r), behind(near_r))
    edges = swap(edge_r)
    left_edge, right_edge = (ahead(edges[:2]), behind(edges[2:]))
    peer_vw = swap(jnp.stack([tied(far_v, left_edge, right_edge), far_w]))

    mid_rows, mid_depth = (wide // 2, depth // 2)
    message = (mid_rows + wide, depth)
    base_one, mid_source, sent_ahead, sent_behind = kernel_call(
        fine_kernel,
        [(4, wide, depth), (2, mid_rows, mid_depth), message, message],
        [
            pltpu.VMEM((8, wide, depth), f32),
            pltpu.VMEM((8, wide, depth), f32),
            pltpu.VMEM((6, wide, depth), f32),
        ],
        [VMEM] * 12,
        10**8,
        tall, pressure_left, pressure_right,
        near_r, far_r, left_r, right_r, edges, left_edge, right_edge,
        pair_sums(depth, mid_depth), pair_sums(wide, mid_rows).T,
    )
    left_one, right_one = (ahead(sent_ahead), behind(sent_behind))
    near_base, far_base = kernel_call(
        base_kernel,
        [two_planes, two_planes],
        [],
        [VMEM] * 5,
        10**8,
        base_one, left_one, right_one, near_r, far_r,
    )
    low_depth = mid_depth // 2
    halves = np.zeros((mid_depth, 2 * mid_depth), ml_dtypes.bfloat16)
    halves[:, :low_depth] = pair_sums(mid_depth, low_depth)
    halves[:, mid_depth + low_depth :] = pair_sums(mid_depth, low_depth)
    own_pairs = pair_sums(half // 2, half // 4).T
    own_pairs = np.pad(own_pairs, ((0, 0), (HALO // 2, HALO // 2)))
    mid_one, low_source = kernel_call(
        middle_kernel,
        [(2, mid_rows, mid_depth), (half // 8, mid_depth)],
        [pltpu.VMEM((6, mid_rows, mid_depth), f32), pltpu.VMEM((4, mid_rows, mid_depth), f32)],
        [VMEM] * 5,
        10**8,
        tied(mid_source, near_base), left_one, right_one, halves, own_pairs,
    )
    left_two, right_two = (ahead(mid_one[1:]), behind(mid_one[:1]))
    (mid_base,) = kernel_call(
        middle_base_kernel,
        [(2, half // 2, mid_depth)],
        [],
        [VMEM] * 4,
        10**7,
        mid_one, tied(left_two, peer_vw), right_two, mid_source,
    )
    peer_mid = swap(mid_base)
    both_mid = jnp.stack([mid_base, peer_mid])
    left_mid, right_mid = (ahead(both_mid), behind(both_mid))
    low_all = lax.all_to_all(
        jnp.broadcast_to(tied(low_source, left_two, right_two), (2 * tunnel_size,) + low_source.shape), both, 0, 0, tiled=True
    )
    left_b, right_b = (ahead(tied(far_base, mid_base)), behind(tied(near_base, mid_base)))
    peer_base = swap(tied(far_base, peer_mid))
    low_plane = (half // 2, mid_depth)
    mid_plane = (half, mid_depth)
    expand_low = np.zeros((mid_depth, mid_depth), ml_dtypes.bfloat16)
    expand_low[:low_depth] = pair_sums(mid_depth, low_depth).T
    (spread_low,) = kernel_call(
        coarsest_kernel,
        [(5,) + mid_plane],
        [pltpu.VMEM((11,) + low_plane, f32)] * 3,
        [VMEM] * 3,
        10**7,
        low_all, expand_low, pair_sums(half, half // 2),
    )
    own_u, sent_u = kernel_call(
        stream_kernel,
        [two_planes, two_planes],
        [],
        [VMEM] * 6,
        10**8,
        near_base, far_base, left_b, tied(right_b, spread_low, left_mid, right_mid), near_u, far_u,
    )
    peer_u = swap(sent_u)
    fine_plane = (rows, depth)
    corrected, potential = kernel_call(
        correction_kernel,
        [(3, 2) + fine_plane, four_planes],
        [
            pltpu.VMEM((5,) + mid_plane, f32),
            pltpu.VMEM((9,) + mid_plane, f32),
            pltpu.VMEM((5,) + fine_plane, f32),
            pltpu.VMEM((8,) + fine_plane, f32),
            pltpu.VMEM((6,) + fine_plane, f32),
        ],
        [VMEM] * 19,
        10**9,
        spread_low, both_mid, left_mid, right_mid, near_base, far_base, peer_base, near_v, near_w, peer_vw, obstacle,
        sum_high, sum_low, diff_high, diff_low, *own_depth,
        pair_sums(depth, mid_depth).T.copy(), pair_sums(rows, half),
    )
    stream = pl.BlockSpec((1, 1) + fine_plane, lambda i: (0, i, 0, 0))
    (corrected,) = kernel_call(
        stream_correction_kernel,
        [corrected.shape],
        [],
        [stream] + [full(two_planes)] * 2 + [by_plane(obstacle.shape, 0)],
        10**7,
        corrected, own_u, peer_u, obstacle,
        grid=(2,),
        out_specs=[stream],
        aliases={0: 0},
    )
    return (corrected, potential)


def step(velocity, obstacle, pressure):
    planes, rows, depth = velocity.shape[1:]
    fits = lax.axis_size("group") == 2 and planes == 2 and pressure.shape[0] == 4
    fits = fits and lax.axis_size("tunnel") > 10 and rows % 512 == 0 and depth % 256 == 0
    if fits:
        return paired(velocity, obstacle, pressure)
    return local(velocity, obstacle, pressure)


def solution(mesh):
    in_specs = (
        P(None, ("tunnel", "group"), None, None),
        P(("tunnel", "group"), None, None),
        P("tunnel", "group", None),
    )
    out_specs = (P(None, ("tunnel", "group"), None, None), P("tunnel", "group", None))
    return jax.shard_map(step, mesh=mesh, in_specs=in_specs, out_specs=out_specs, check_vma=False)
```

```python
import math

import jax
import jax.numpy as jnp
import ml_dtypes
import numpy as np
from jax import lax
from jax.experimental import pallas as pl
from jax.experimental.pallas import tpu as pltpu
from jax.sharding import PartitionSpec as P

LEVELS = 3
SWEEPS = 2
COARSE_SWEEPS = 4


time_step = 0.1
viscosity = 0.05
relax_weight = 0.8
highest = lax.Precision.HIGHEST


def extended(value, sides, width):
    for axis, dim in sides:
        size, length = (lax.axis_size(axis), value.shape[dim])
        up = [(i, (i + 1) % size) for i in range(size)]
        down = [(j, i) for i, j in up]
        last = lax.slice_in_dim(value, length - width, length, axis=dim)
        initial = lax.slice_in_dim(value, 0, width, axis=dim)
        before = lax.ppermute(last, axis, up)
        after = lax.ppermute(initial, axis, down)
        value = jnp.concatenate([before, value, after], axis=dim)
    return value


def compact_tables(count):
    indices = jnp.arange(count, dtype=jnp.int32)
    product = indices[:, None] * indices[None, :] % count
    angles = product.astype(jnp.float32) * (2.0 * math.pi / count)
    cosines = jnp.cos(angles)
    sines = jnp.sin(angles)
    theta = indices.astype(jnp.float32) * (2.0 * math.pi / count)
    first_wave = (14.0 / 9.0 * jnp.sin(theta) + jnp.sin(2.0 * theta) / 18.0) / (
        1.0 + 2.0 / 3.0 * jnp.cos(theta)
    )
    second_wave = (
        24.0 / 11.0 * (1.0 - jnp.cos(theta)) + 3.0 / 22.0 * (1.0 - jnp.cos(2.0 * theta))
    ) / (1.0 + 4.0 / 11.0 * jnp.cos(theta))
    first_matrix = (
        jnp.dot(cosines * first_wave, sines.T, precision=highest)
        - jnp.dot(sines * first_wave, cosines.T, precision=highest)
    ) / count
    second_matrix = (
        -(
            jnp.dot(cosines * second_wave, cosines.T, precision=highest)
            + jnp.dot(sines * second_wave, sines.T, precision=highest)
        )
        / count
    )
    return (first_matrix, second_matrix)


def along_rows(matrix, field):
    return jnp.einsum("ij,...jz->...iz", matrix, field, precision=highest)


def along_depth(matrix, field):
    return jnp.einsum("...j,ij->...i", field, matrix, precision=highest)


def shifted(padded, offset, axis):
    count = padded.shape[axis] - 4
    return lax.slice_in_dim(padded, 2 + offset, 2 + offset + count, axis=axis)


def stream_first(padded, axis):
    ahead = shifted(padded, 1, axis) - shifted(padded, -1, axis)
    further = shifted(padded, 2, axis) - shifted(padded, -2, axis)
    return (8.0 * ahead - further) / 12.0


def stream_second(padded, axis):
    ahead = shifted(padded, 1, axis) + shifted(padded, -1, axis)
    further = shifted(padded, 2, axis) + shifted(padded, -2, axis)
    return (16.0 * ahead - further - 30.0 * shifted(padded, 0, axis)) / 12.0


def padded_neighbours(padded):
    interior = padded[1:-1, 1:-1]
    total = padded[2:, 1:-1] + padded[:-2, 1:-1]
    total = total + padded[1:-1, 2:] + padded[1:-1, :-2]
    return total + jnp.roll(interior, -1, 2) + jnp.roll(interior, 1, 2)


def relax_padded(padded, source_term, scale):
    interior = padded[1:-1, 1:-1]
    return interior + relax_weight / 6.0 * (
        padded_neighbours(padded) - 6.0 * interior - scale * source_term
    )


def faces(field):
    return extended(field, (("tunnel", 0), ("group", 1)), 1)


def thin_sweeps(field, source_term, scale, count):
    for sweep_index in range(count):
        field = relax_padded(faces(field), source_term, scale)
    return field


def smooth(field, source_term, scale, level):
    if level == 0:
        return thin_sweeps(field, source_term, scale, SWEEPS)
    return thin_sweeps(field, source_term, scale, SWEEPS)


def coarsest(source_term, scale):
    return thin_sweeps(jnp.zeros_like(source_term), source_term, scale, COARSE_SWEEPS)


def restrict(field):
    planes, rows, depth = field.shape
    blocks = field.reshape(planes // 2, 2, rows // 2, 2, depth // 2, 2)
    return jnp.sum(blocks, axis=(1, 3, 5)) * 0.125


def prolong(field):
    return jnp.repeat(jnp.repeat(jnp.repeat(field, 2, 0), 2, 1), 2, 2)


def cycle(field, source_term, level):
    scale = 4.0**level
    if level == LEVELS - 1:
        return coarsest(source_term, scale)
    field = smooth(field, source_term, scale, level)
    leftover = source_term - (padded_neighbours(faces(field)) - 6.0 * field) / scale
    coarse_source = restrict(leftover)
    coarse = cycle(jnp.zeros_like(coarse_source), coarse_source, level + 1)
    field = field + prolong(coarse)
    return smooth(field, source_term, scale, level)


def local(velocity, obstacle, pressure):
    row_count = velocity.shape[2]
    depth_count = velocity.shape[3]
    rows_first, rows_second = compact_tables(row_count)
    depth_first, depth_second = compact_tables(depth_count)
    rows_both = jnp.concatenate([rows_first, rows_second], axis=0)
    depth_both = jnp.concatenate([depth_first, depth_second], axis=0)
    keep = 1.0 - obstacle.astype(jnp.float32)
    row_terms = along_rows(rows_both, velocity)
    depth_terms = along_depth(depth_both, velocity)
    transverse = (
        velocity[1] * row_terms[:, :, :row_count] + velocity[2] * depth_terms[..., :depth_count]
    )
    diffusion = row_terms[:, :, row_count:] + depth_terms[..., depth_count:]
    padded = extended(velocity, ((("tunnel", "group"), 1),), 2)
    streamwise = -velocity[0] * stream_first(padded, 1) + viscosity * stream_second(padded, 1)
    tendency = streamwise - transverse + viscosity * diffusion
    star = (velocity + time_step * tendency) * keep
    star_padded = extended(star[0], ((("tunnel", "group"), 0),), 2)
    source = (
        stream_first(star_padded, 0)
        + along_rows(rows_first, star[1])
        + along_depth(depth_first, star[2])
    )
    source_tile = lax.all_to_all(source, "group", split_axis=1, concat_axis=0, tiled=True)
    potential = cycle(pressure, source_tile, 0)
    potential_padded = extended(potential, (("tunnel", 0),), 2)
    streamwise_grad = stream_first(potential_padded, 0)
    returned = lax.all_to_all(
        jnp.stack([potential, streamwise_grad]), "group", split_axis=1, concat_axis=2, tiled=True
    )
    gradient = jnp.stack(
        [returned[1], along_rows(rows_first, returned[0]), along_depth(depth_first, returned[0])]
    )
    corrected = (star - gradient) * keep
    return (corrected, potential)


HALO = 16
weight = relax_weight / 6.0
bf16 = jnp.bfloat16
f32 = jnp.float32
VMEM = pl.BlockSpec(memory_space=pltpu.VMEM)
ANY = pl.BlockSpec(memory_space=pl.ANY)


def wave_tables(count):
    index = np.arange(count)
    angles = 2.0 * np.pi * (np.outer(index, index) % count) / count
    theta = 2.0 * np.pi * index / count
    first_wave = (14.0 / 9.0 * np.sin(theta) + np.sin(2.0 * theta) / 18.0) / (
        1.0 + 2.0 / 3.0 * np.cos(theta)
    )
    second_wave = (
        24.0 / 11.0 * (1.0 - np.cos(theta)) + 3.0 / 22.0 * (1.0 - np.cos(2.0 * theta))
    ) / (1.0 + 4.0 / 11.0 * np.cos(theta))
    cosines, sines = (np.cos(angles), np.sin(angles))
    first = ((cosines * first_wave) @ sines.T - (sines * first_wave) @ cosines.T) / count
    second = -((cosines * second_wave) @ cosines.T + (sines * second_wave) @ sines.T) / count
    return (first, second)


def high_low(table):
    high = table.astype(np.float32).astype(ml_dtypes.bfloat16)
    low = (table - high.astype(np.float64)).astype(np.float32).astype(ml_dtypes.bfloat16)
    return (high, low)


def half_tables(count):
    first, second = wave_tables(count)
    half = count // 2
    index = np.arange(half)
    root_first = (math.sqrt(5.0) - 3.0) / 2.0
    root_second = (math.sqrt(105.0) - 11.0) / 4.0
    basis = np.zeros((8, half))
    basis[0, 0] = 1.0
    basis[1, -1] = 1.0
    basis[2] = root_first**index
    basis[3] = basis[2][::-1]
    basis[4] = root_second**index
    basis[5] = basis[4][::-1]
    spread = []
    for table, used in ((first, (0, 1, 2, 3)), (second, (0, 1, 4, 5))):
        solved = np.linalg.lstsq(basis[list(used)].T, table[:half, half:].T, rcond=None)[0].T
        wide = np.zeros((half, 8))
        wide[:, list(used)] = solved
        spread.append(wide)
    own = np.concatenate([first[:half, :half], second[:half, :half]], axis=0)
    return (own, np.concatenate(spread, axis=0), basis, first)


def split(value):
    high = value.astype(bf16)
    low = (value - high.astype(f32)).astype(bf16)
    return (high, low)


def dot(left, right):
    return jnp.dot(left, right, preferred_element_type=f32)


def dot_left(table_high, table_low, value):
    high, low = split(value)
    return dot(table_high, high) + (dot(table_high, low) + dot(table_low, high))


def dot_right(value, table_high, table_low):
    high, low = split(value)
    return dot(high, table_high) + (dot(low, table_high) + dot(high, table_low))


def pick_left(zero_one, value):
    high, low = split(value)
    return dot(zero_one, high) + dot(zero_one, low)


def pick_right(value, zero_one):
    high, low = split(value)
    return dot(high, zero_one) + dot(low, zero_one)


def summary(basis_both, value):
    high, low = split(value)
    main = dot(basis_both, high)
    rest = dot(basis_both, low)
    return main[:8] + main[8:] + rest[:8]


def summary_operand(value):
    high = value.astype(bf16).astype(f32)
    return jnp.concatenate([high, value - high, high, jnp.zeros_like(high)], axis=0).astype(bf16)


def turn(value, shift, axis):
    return pltpu.roll(value, shift % value.shape[axis], axis)


def cross_sum(value):
    return (turn(value, 1, 0) + turn(value, -1, 0)) + (turn(value, 1, 1) + turn(value, -1, 1))


def first_of(values):
    return (8.0 * (values[3] - values[1]) - (values[4] - values[0])) * (1.0 / 12.0)


def second_of(values):
    return (
        16.0 * (values[3] + values[1]) - (values[4] + values[0]) - 30.0 * values[2]
    ) * (1.0 / 12.0)


def kernel_call(body, outs, scratch, specs, flops, *args, grid=None, out_specs=None, aliases=None):
    total = sum(math.prod(a.shape) * a.dtype.itemsize for a in args)
    total += sum(4 * math.prod(s) for s in outs)
    options = {} if grid is None else {"grid": grid}
    if aliases is not None:
        options["input_output_aliases"] = aliases
    return pl.pallas_call(
        body,
        out_shape=[jax.ShapeDtypeStruct(s, f32) for s in outs],
        in_specs=specs,
        out_specs=[VMEM] * len(outs) if out_specs is None else out_specs,
        scratch_shapes=scratch,
        compiler_params=pltpu.CompilerParams(vmem_limit_bytes=36 * 1024 * 1024),
        cost_estimate=pl.CostEstimate(flops=flops, bytes_accessed=total if flops > 1 else 1, transcendentals=0),
        **options,
    )(*args)


def mirror(side, index, count):
    return index + side * (count - 1 - 2 * index)


def sign_of(side):
    return (1 - 2 * side).astype(f32)


def transverse(u, v, w, value, other_sum, rows_high, rows_low, spread, depth_high, depth_low):
    half, width = value.shape
    high, low = split(value)
    across = (
        dot(rows_high[...], high)
        + (dot(rows_high[...], low) + dot(rows_low[...], high))
        + dot(spread[...], summary_operand(other_sum))
    )
    along = dot(high, depth_high[...]) + (dot(low, depth_high[...]) + dot(high, depth_low[...]))
    advect = v * across[:half] + w * along[:, :width]
    return value + time_step * (viscosity * (across[half:] + along[:, width:]) - advect)


def own_planes_kernel(
    velocity_ref, basis_ref, rows_high, rows_low, spread, depth_high, depth_low, out_ref, sent_ref
):
    side = lax.axis_index("group")
    half = basis_ref.shape[1]
    own = pl.ds(pl.multiple_of(side * half, half), half)
    other = pl.ds(pl.multiple_of((1 - side) * half, half), half)
    u, v, w = (velocity_ref[c, 0, own] for c in range(3))
    sent_ref[0, :half] = velocity_ref[2, 0, other]
    for c in range(3):
        value = velocity_ref[c, 0, own]
        kept = summary(basis_ref[...], velocity_ref[c, 0, other])
        sent_ref[0, half + 8 * c : half + 8 * c + 8] = summary(basis_ref[...], value)
        out_ref[c, 0] = transverse(u, v, w, value, kept, rows_high, rows_low, spread, depth_high, depth_low)


def peer_planes_kernel(
    uv_ref, w_ref, rows_high, rows_low, spread, depth_high, depth_low, out_ref
):
    half = uv_ref.shape[2]
    u, v, w = (uv_ref[0, 0], uv_ref[1, 0], w_ref[0, :half])
    for c in range(3):
        other_sum = w_ref[0, half + 8 * c : half + 8 * c + 8]
        out_ref[c, 0] = transverse(
            u, v, w, (u, v, w)[c], other_sum, rows_high, rows_low, spread, depth_high, depth_low
        )


def star_planes(side, planes, raws, solids, u_of, outs):
    sign = sign_of(side) * (time_step / 12.0)
    for plane in range(4):
        index = mirror(side, plane % 2, 2)
        keep = 1.0 - solids[plane // 2][index].astype(f32)
        near = planes[plane : plane + 5]
        first = 8.0 * (near[3] - near[1]) - (near[4] - near[0])
        second = 16.0 * (near[3] + near[1]) - (near[4] + near[0]) - 30.0 * near[2]
        raw = raws[plane // 2][index]
        outs[plane // 2][plane % 2] = (
            raw + (time_step * viscosity / 12.0) * second - (u_of(plane) * sign) * first
        ) * keep


def eight(side, groups):
    return [group[mirror(side, k, 2)] for group in groups for k in range(2)]


def star_u_kernel(raw_own, raw_peer, own_ref, one_ref, peers, others, solid_own, solid_peer, near_ref, far_ref):
    side = lax.axis_index("group")
    planes = eight(side, (others.at[0], own_ref.at[0], peers.at[0], one_ref.at[0]))
    star_planes(
        side, planes, (raw_own.at[0], raw_peer.at[0]), (solid_own, solid_peer),
        lambda plane: planes[plane + 2], (near_ref, far_ref),
    )


def star_vw_kernel(
    raw_own, raw_peer, own_ref, one_ref, peers, peer_w, others, other_w, solid_own, solid_peer, basis_ref,
    near_v, far_v, near_w, far_w, sum_ref,
):
    side = lax.axis_index("group")
    step = pl.program_id(0)

    def u_of(plane):
        return (own_ref if plane < 2 else peers)[0, mirror(side, plane % 2, 2)]

    for c, peer, other, outs in (
        (1, peers.at[1], others.at[0], (near_v, far_v)),
        (2, peer_w, other_w, (near_w, far_w)),
    ):
        planes = eight(side, (other, own_ref.at[c], peer, one_ref.at[c]))
        star_planes(side, planes, (raw_own.at[c], raw_peer.at[c]), (solid_own, solid_peer), u_of, outs)

    @pl.when(step == 0)
    def _():
        sum_ref[...] = jnp.zeros_like(sum_ref)

    for plane in range(4):
        sum_ref[plane] += summary(basis_ref[0], (near_v if plane < 2 else far_v)[plane % 2])


def cross_kernel(near_v, far_v, near_w, far_w, rows_high, rows_low, depth_high, depth_low, out_ref):
    half = near_v.shape[1]
    for plane in range(4):
        v, w = ((near_v, near_w) if plane < 2 else (far_v, far_w))
        out_ref[plane] = dot_left(rows_high[:half], rows_low[:half], v[plane % 2]) + dot_right(
            w[plane % 2], depth_high[...], depth_low[...]
        )


def source_kernel(
    near_u, far_u, left_ref, right_ref, cross_ref, sum_ref, spread, near_r, far_r, head, tail
):
    sign = sign_of(lax.axis_index("group"))
    rows = cross_ref.shape[1]
    step = pl.program_id(0)
    planes = [ref[k] for ref in (left_ref, near_u, far_u, right_ref) for k in range(2)]
    values = []
    for plane in range(4):
        value = sign * first_of(planes[plane : plane + 5]) + cross_ref[plane]
        value = value + dot(spread[...], summary_operand(sum_ref[3 - plane]))
        (near_r if plane < 2 else far_r)[plane % 2] = value
        values.append(value)

    @pl.when(step == 0)
    def _():
        for plane in range(4):
            head[plane] = values[plane][:HALO]

    @pl.when(step == pl.num_programs(0) - 1)
    def _():
        for plane in range(4):
            tail[plane] = values[plane][rows - HALO :]


def fine_kernel(
    pressure_tall, pressure_left, pressure_right,
    near_r, far_r, left_ref, right_ref, edge_ref, left_edge, right_edge, depth_pick, rows_pick,
    base_ref, coarse_ref, ahead_ref, behind_ref, source_ref, one, two,
):
    side = lax.axis_index("group")
    half = near_r.shape[1]

    def fill(target, at, body, edge):
        target[at, HALO : HALO + half] = body
        target[at, :HALO] = edge[HALO:]
        target[at, HALO + half :] = edge[:HALO]

    for plane in range(2):
        fill(source_ref, plane, left_ref[plane], left_edge[1 - plane])
        fill(source_ref, 2 + plane, near_r[plane], edge_ref[3 - plane])
        fill(source_ref, 4 + plane, far_r[plane], edge_ref[1 - plane])
        fill(source_ref, 6 + plane, right_ref[plane], right_edge[1 - plane])
    pressure = [pressure_left.at[mirror(side, k, 3)] for k in range(3)]
    pressure += [pressure_tall.at[mirror(side, k, 4)] for k in range(4)]
    pressure += [pressure_right.at[mirror(side, k, 3)] for k in range(3)]
    for k in range(8):
        centre = pressure[k + 1][...]
        total = pressure[k][...] + pressure[k + 2][...] + cross_sum(centre)
        one[k] = centre + weight * (total - 6.0 * centre - source_ref[k])
    for k in range(6):
        centre = one[k + 1]
        total = one[k] + one[k + 2] + cross_sum(centre)
        two[k] = centre + weight * (total - 6.0 * centre - source_ref[k + 1])
    for pair in range(2):
        left = []
        for k in (2 * pair, 2 * pair + 1):
            centre = two[k + 1]
            total = two[k] + two[k + 2] + cross_sum(centre)
            residual = source_ref[k + 2] - (total - 6.0 * centre)
            base_ref[k] = centre - weight * residual
            left.append(residual)
        coarse = 0.125 * pick_left(rows_pick[...], pick_right(left[0] + left[1], depth_pick[...]))
        coarse_ref[pair] = coarse
        rows, width = coarse.shape
        ahead_ref[:rows, width * pair : width * (pair + 1)] = coarse
        behind_ref[:rows, width * pair : width * (pair + 1)] = coarse
    ahead_ref[rows:] = base_ref[3]
    behind_ref[rows:] = base_ref[0]


def middle_kernel(own_ref, left_ref, right_ref, depth_pick, rows_pick, base_ref, coarse_ref, one, two):
    rows, width = own_ref.shape[1:]
    source = []
    for ref in (left_ref, own_ref, right_ref):
        for k in range(2):
            source.append(ref[k] if ref is own_ref else ref[:rows, width * k : width * (k + 1)])
    for k in range(6):
        one[k] = (-4.0 * weight) * source[k]
    for k in range(4):
        centre = one[k + 1]
        total = one[k] + one[k + 2] + cross_sum(centre)
        two[k] = centre + weight * (total - 6.0 * centre - 4.0 * source[k + 1])
    left = []
    for k in range(2):
        centre = two[k + 1]
        total = two[k] + two[k + 2] + cross_sum(centre)
        residual = source[k + 2] - 0.25 * (total - 6.0 * centre)
        base_ref[k] = centre - (4.0 * weight) * residual
        left.append(residual)
    width = own_ref.shape[2]
    wide = pick_right(left[0] + left[1], depth_pick[...])
    count = coarse_ref.shape[0]
    coarse_ref[...] = 0.125 * (
        pick_left(rows_pick[:count], wide[:, :width]) + pick_left(rows_pick[count:], wide[:, width:])
    )


def middle_base_kernel(base_ref, left_ref, right_ref, source_ref, out_ref):
    rows = out_ref.shape[1]
    planes = [left_ref[0], base_ref[0], base_ref[1], right_ref[0]]
    for k in range(2):
        centre = planes[k + 1]
        total = planes[k] + planes[k + 2] + cross_sum(centre)
        value = centre + weight * (total - 6.0 * centre - 4.0 * source_ref[k])
        out_ref[k] = value[HALO // 2 : HALO // 2 + rows]


def base_kernel(base_ref, left_ref, right_ref, near_r, far_r, near_ref, far_ref):
    rows = near_ref.shape[1]
    skip = left_ref.shape[0] - base_ref.shape[1]
    for k in range(4):
        before = left_ref[skip:] if k == 0 else base_ref[k - 1]
        after = right_ref[skip:] if k == 3 else base_ref[k + 1]
        centre = base_ref[k]
        total = before + after + cross_sum(centre)
        value = (centre + weight * (total - 6.0 * centre))[HALO : HALO + rows]
        source, out = ((near_r, near_ref) if k < 2 else (far_r, far_ref))
        out[k % 2] = value - weight * source[k % 2]


def stream_kernel(near_ref, far_ref, left_ref, right_ref, near_u, far_u, own_ref, sent_ref):
    sign = sign_of(lax.axis_index("group"))
    planes = [ref[k] for ref in (left_ref, near_ref, far_ref, right_ref) for k in range(2)]
    for plane in range(4):
        star = (near_u if plane < 2 else far_u)[plane % 2]
        (own_ref if plane < 2 else sent_ref)[plane % 2] = star - sign * first_of(planes[plane : plane + 5])


def coarsest_kernel(all_ref, mid_depth, mid_rows, out_ref, source, one, two):
    place = lax.axis_index("tunnel")
    step = 1 - 2 * lax.axis_index("group")
    count = all_ref.shape[0] // 2
    quarter, width = all_ref.shape[1:]
    lower = lax.broadcasted_iota(jnp.int32, (quarter, width), 1) < width // 2
    for k in range(11):
        plane = lax.rem(place + step * (k - 5) + 2 * count, count)
        for part in range(2):
            packed = all_ref[2 * plane + part]
            turned = turn(packed, width // 2, 1)
            source[k, 2 * part * quarter : (2 * part + 1) * quarter] = jnp.where(lower, packed, turned)
            source[k, (2 * part + 1) * quarter : (2 * part + 2) * quarter] = jnp.where(lower, turned, packed)
    for k in range(11):
        one[k] = (-16.0 * weight) * source[k]
    source_at, target = (one, two)
    for sweep_index in range(1, COARSE_SWEEPS):
        for k in range(sweep_index, 11 - sweep_index):
            centre = source_at[k]
            total = source_at[k - 1] + source_at[k + 1] + cross_sum(centre)
            target[k] = centre + weight * (total - 6.0 * centre - 16.0 * source[k])
        source_at, target = (target, source_at)
    for k in range(5):
        out_ref[k] = pick_left(mid_rows[...], pick_right(source_at[k + 3], mid_depth[...]))


def correction_kernel(
    spread_ref, own_mid, left_mid, right_mid,
    near_base, far_base, peer_base, near_v, near_w, peer_vw, solid_ref,
    sum_high, sum_low, diff_high, diff_low, depth_high, depth_low, fine_depth, fine_rows,
    out_ref, potential_ref, base, mid, fine, first_sweep, delta,
):
    side = lax.axis_index("group")
    sign = sign_of(side)
    half = near_v.shape[1]
    own_rows = pl.ds(pl.multiple_of(side * half, half), half)
    peer_rows = pl.ds(pl.multiple_of((1 - side) * half, half), half)
    mid_half = own_mid.shape[2]
    own_mid_rows = pl.ds(pl.multiple_of(side * mid_half, mid_half), mid_half)
    peer_mid_rows = pl.ds(pl.multiple_of((1 - side) * mid_half, mid_half), mid_half)
    for k in range(5):
        held = left_mid if k < 2 else own_mid
        base[k, own_mid_rows] = right_mid[0] if k == 4 else held[0, k % 2]
        base[k, peer_mid_rows] = right_mid[1] if k == 4 else held[1, 1 - k % 2]
    for k in range(1, 8):
        centre = spread_ref[k // 2]
        total = spread_ref[(k - 1) // 2] + spread_ref[(k + 1) // 2] + cross_sum(centre)
        mid[k] = centre + weight * (total - 6.0 * centre)
    for k in range(5):
        centre = mid[k + 2]
        total = mid[k + 1] + mid[k + 3] + cross_sum(centre)
        value = base[k] + centre + weight * (total - 6.0 * centre)
        fine[k] = pick_left(fine_rows[...], pick_right(value, fine_depth[...]))
    for j in range(5):
        centre = fine[j]
        shared = centre + weight * (centre + cross_sum(centre) - 6.0 * centre)
        if j > 0:
            first_sweep[2 * j - 1] = shared + weight * fine[j - 1]
        if j < 4:
            first_sweep[2 * j] = shared + weight * fine[j + 1]
    for k in range(6):
        centre = first_sweep[k + 1]
        total = first_sweep[k] + first_sweep[k + 2] + cross_sum(centre)
        delta[k] = centre + weight * (total - 6.0 * centre)
    for k in range(4):
        smooth_part = (near_base if k < 2 else far_base)[k % 2]
        potential_ref[mirror(side, k, 4)] = smooth_part + delta[k + 2, own_rows]
    for k in range(2):
        at = 2 + k
        index = mirror(side, k, 2)
        out_ref[0, index] = sign * first_of([delta[at + offset] for offset in range(-2, 3)])
        own = delta[at, own_rows] + near_base[k]
        peer = delta[at, peer_rows] + peer_base[1 - k]
        even = dot_left(sum_high[...], sum_low[...], own + peer)
        odd = dot_left(diff_high[...], diff_low[...], own - peer)
        for rows, value, gradient, v, w in (
            (own_rows, own, even + odd, near_v[k], near_w[k]),
            (peer_rows, peer, even - odd, peer_vw[0, 1 - k], peer_vw[1, 1 - k]),
        ):
            keep = 1.0 - solid_ref[index, rows].astype(f32)
            out_ref[1, index, rows] = (v - gradient) * keep
            out_ref[2, index, rows] = (w - dot_right(value, depth_high[...], depth_low[...])) * keep


def stream_correction_kernel(gradient_ref, own_u, peer_u, solid_ref, out_ref):
    side = lax.axis_index("group")
    half = own_u.shape[1]
    index = pl.program_id(0)
    k = mirror(side, index, 2)
    own_rows = pl.ds(pl.multiple_of(side * half, half), half)
    peer_rows = pl.ds(pl.multiple_of((1 - side) * half, half), half)
    for rows, value in ((own_rows, own_u[k]), (peer_rows, peer_u[1 - k])):
        keep = 1.0 - solid_ref[0, rows].astype(f32)
        out_ref[0, 0, rows] = (value - gradient_ref[0, 0, rows]) * keep


def pair_sums(fine, coarse):
    return (np.arange(fine)[:, None] // 2 == np.arange(coarse)[None, :]).astype(ml_dtypes.bfloat16)


def paired(velocity, obstacle, pressure):
    rows, depth = velocity.shape[2:]
    half = rows // 2
    wide = half + 2 * HALO
    tunnel_size = lax.axis_size("tunnel")
    side = lax.axis_index("group")
    both = ("tunnel", "group")
    own, spread, basis, rows_first = half_tables(rows)
    depth_first, depth_second = wave_tables(depth)
    rows_high, rows_low = high_low(own)
    spread_high, spread_low = high_low(spread)
    spread_all = np.concatenate([spread_high, spread_high, spread_low, np.zeros_like(spread_low)], axis=1)
    basis_both = np.concatenate(high_low(basis), axis=0)
    depth_high, depth_low = high_low(np.concatenate([depth_first.T, depth_second.T], axis=1))
    sum_high, sum_low = high_low((rows_first[:half, :half] + rows_first[:half, half:]) / 2.0)
    diff_high, diff_low = high_low((rows_first[:half, :half] - rows_first[:half, half:]) / 2.0)

    def swap(value):
        return lax.ppermute(value, "group", [(0, 1), (1, 0)])

    ahead_way, behind_way = ([], [])
    for i in range(tunnel_size):
        after, before = ((i + 1) % tunnel_size, (i - 1) % tunnel_size)
        ahead_way += [(2 * i, 2 * after), (2 * i + 1, 2 * before + 1)]
        behind_way += [(2 * i, 2 * before), (2 * i + 1, 2 * after + 1)]

    def ahead(value):
        return lax.ppermute(value, both, ahead_way)

    def behind(value):
        return lax.ppermute(value, both, behind_way)

    def ahead_across(value):
        return lax.ppermute(value, both, [(i, j ^ 1) for i, j in ahead_way])

    def behind_across(value):
        return lax.ppermute(value, both, [(i, j ^ 1) for i, j in behind_way])

    def tied(value, *others):
        return lax.optimization_barrier((value,) + others)[0]

    def half_of(value, which, axis):
        return lax.dynamic_slice_in_dim(value, which * half, half, axis=axis)

    plane = (half, depth)
    two_planes, four_planes = ((2,) + plane, (4,) + plane)
    full = lambda shape: pl.BlockSpec(shape, lambda i: (0,) * len(shape))
    by_plane = lambda shape, at: pl.BlockSpec(
        shape[:at] + (1,) + shape[at + 1 :], lambda i: (0,) * at + (i,) + (0,) * (len(shape) - at - 1)
    )
    tables = (rows_high, rows_low, spread_all, depth_high, depth_low)
    table_specs = [full(table.shape) for table in tables]

    edges = jnp.concatenate([pressure[:, :HALO], pressure[:, half - HALO :]], axis=1)
    pressure_edge = swap(edges)
    tall = jnp.concatenate([pressure_edge[:, HALO:], pressure, pressure_edge[:, :HALO]], axis=1)
    to_ahead = jnp.where(side == 0, tall[1:], tall[:3])
    to_behind = jnp.where(side == 0, tall[:3], tall[1:])
    sent_uv = half_of(velocity[:2], 1 - side, 2)
    peer_uv = swap(sent_uv)
    pressure_left = ahead(to_ahead)
    pressure_right = behind(to_behind)
    raw_own, sent_w = kernel_call(
        own_planes_kernel,
        [(3, 2) + plane, (2, half + 24, depth)],
        [],
        [by_plane(velocity.shape, 1), full(basis_both.shape)] + table_specs,
        3 * 10**9,
        velocity, basis_both, *tables,
        grid=(2,),
        out_specs=[by_plane((3, 2) + plane, 1), by_plane((2, half + 24, depth), 0)],
    )
    peer_w = swap(tied(sent_w, pressure_left, pressure_right))
    own_half = half_of(tied(velocity, sent_w), side, 2)
    one = behind(own_half)
    other_uv = ahead(tied(peer_uv, sent_w))
    other_w = ahead(peer_w[:, :half])
    solid_peer = swap(half_of(obstacle, 1 - side, 1))
    solid_own = half_of(obstacle, side, 1)
    (raw_peer,) = kernel_call(
        peer_planes_kernel,
        [(3, 2) + plane],
        [],
        [by_plane((2, 2) + plane, 1), by_plane((2, half + 24, depth), 0)] + table_specs,
        3 * 10**9,
        peer_uv, peer_w, *tables,
        grid=(2,),
        out_specs=[by_plane((3, 2) + plane, 1)],
    )
    strip = 64

    def strips(count, first=0):
        return pl.BlockSpec((count, 2, strip, depth), lambda i: (first, 0, i, 0))

    flat = pl.BlockSpec((2, strip, depth), lambda i: (0, i, 0))
    near_u, far_u = kernel_call(
        star_u_kernel,
        [two_planes] * 2,
        [],
        [strips(1)] * 6 + [flat] * 2,
        10**8,
        raw_own, raw_peer, own_half, one, peer_uv, other_uv, solid_own, solid_peer,
        grid=(half // strip,),
        out_specs=[flat] * 2,
    )
    left_u, right_u = (ahead(far_u), behind(near_u))
    basis_strips = basis_both.reshape(16, half // strip, strip).transpose(1, 0, 2).copy()
    near_v, far_v, near_w, far_w, sum_v = kernel_call(
        star_vw_kernel,
        [two_planes] * 4 + [(4, 8, depth)],
        [],
        [strips(3)] * 4 + [strips(2), flat, strips(1, 1), flat, flat, flat]
        + [pl.BlockSpec((1, 16, strip), lambda i: (i, 0, 0))],
        10**8,
        raw_own, raw_peer, tied(own_half, near_u), one, peer_uv, peer_w, other_uv, other_w, solid_own, solid_peer,
        basis_strips,
        grid=(half // strip,),
        out_specs=[flat] * 4 + [full((4, 8, depth))],
    )
    peer_sum_v = swap(sum_v)
    own_depth = (depth_high[:, :depth].copy(), depth_low[:, :depth].copy())
    (cross,) = kernel_call(
        cross_kernel,
        [four_planes],
        [],
        [VMEM] * 8,
        10**9,
        near_v, far_v, near_w, far_w, rows_high, rows_low, *own_depth,
    )
    edge_shape = (4, HALO, depth)
    near_r, far_r, head_r, tail_r = kernel_call(
        source_kernel,
        [two_planes, two_planes, edge_shape, edge_shape],
        [],
        [flat] * 4
        + [pl.BlockSpec((4, strip, depth), lambda i: (0, i, 0)), full((4, 8, depth))]
        + [pl.BlockSpec((strip, spread_all.shape[1]), lambda i: (i, 0))],
        10**8,
        near_u, far_u, left_u, right_u, cross, peer_sum_v, spread_all[:half].copy(),
        grid=(half // strip,),
        out_specs=[flat, flat, full(edge_shape), full(edge_shape)],
    )
    edge_r = jnp.concatenate([head_r, tail_r], axis=1)
    left_r, right_r = (ahead(far_r), behind(near_r))
    edges = swap(edge_r)
    left_edge, right_edge = (ahead(edges[:2]), behind(edges[2:]))
    peer_vw = swap(jnp.stack([tied(far_v, left_edge, right_edge), far_w]))

    mid_rows, mid_depth = (wide // 2, depth // 2)
    message = (mid_rows + wide, depth)
    base_one, mid_source, sent_ahead, sent_behind = kernel_call(
        fine_kernel,
        [(4, wide, depth), (2, mid_rows, mid_depth), message, message],
        [
            pltpu.VMEM((8, wide, depth), f32),
            pltpu.VMEM((8, wide, depth), f32),
            pltpu.VMEM((6, wide, depth), f32),
        ],
        [VMEM] * 12,
        10**8,
        tall, pressure_left, pressure_right,
        near_r, far_r, left_r, right_r, edges, left_edge, right_edge,
        pair_sums(depth, mid_depth), pair_sums(wide, mid_rows).T,
    )
    left_one, right_one = (ahead(sent_ahead), behind(sent_behind))
    near_base, far_base = kernel_call(
        base_kernel,
        [two_planes, two_planes],
        [],
        [VMEM] * 5,
        10**8,
        base_one, left_one, right_one, near_r, far_r,
    )
    low_depth = mid_depth // 2
    halves = np.zeros((mid_depth, 2 * mid_depth), ml_dtypes.bfloat16)
    halves[:, :low_depth] = pair_sums(mid_depth, low_depth)
    halves[:, mid_depth + low_depth :] = pair_sums(mid_depth, low_depth)
    own_pairs = pair_sums(half // 2, half // 4).T
    own_pairs = np.pad(own_pairs, ((0, 0), (HALO // 2, HALO // 2)))
    mid_one, low_source = kernel_call(
        middle_kernel,
        [(2, mid_rows, mid_depth), (half // 8, mid_depth)],
        [pltpu.VMEM((6, mid_rows, mid_depth), f32), pltpu.VMEM((4, mid_rows, mid_depth), f32)],
        [VMEM] * 5,
        10**8,
        tied(mid_source, near_base), left_one, right_one, halves, own_pairs,
    )
    left_two, right_two = (ahead(mid_one[1:]), behind(mid_one[:1]))
    (mid_base,) = kernel_call(
        middle_base_kernel,
        [(2, half // 2, mid_depth)],
        [],
        [VMEM] * 4,
        10**7,
        mid_one, tied(left_two, peer_vw), right_two, mid_source,
    )
    peer_mid = swap(mid_base)
    both_mid = jnp.stack([mid_base, peer_mid])
    left_mid, right_mid = (ahead(both_mid), behind(jnp.stack([mid_base[0], peer_mid[1]])))
    low_all = lax.all_to_all(
        jnp.broadcast_to(tied(low_source, left_two, right_two), (2 * tunnel_size,) + low_source.shape), both, 0, 0, tiled=True
    )
    left_b, right_b = (ahead(tied(far_base, mid_base)), behind(tied(near_base, mid_base)))
    peer_base = swap(tied(far_base, peer_mid))
    low_plane = (half // 2, mid_depth)
    mid_plane = (half, mid_depth)
    expand_low = np.zeros((mid_depth, mid_depth), ml_dtypes.bfloat16)
    expand_low[:low_depth] = pair_sums(mid_depth, low_depth).T
    (spread_low,) = kernel_call(
        coarsest_kernel,
        [(5,) + mid_plane],
        [pltpu.VMEM((11,) + low_plane, f32)] * 3,
        [VMEM] * 3,
        10**7,
        low_all, expand_low, pair_sums(half, half // 2),
    )
    own_u, sent_u = kernel_call(
        stream_kernel,
        [two_planes, two_planes],
        [],
        [VMEM] * 6,
        10**8,
        near_base, far_base, left_b, tied(right_b, spread_low, left_mid, right_mid), near_u, far_u,
    )
    peer_u = swap(sent_u)
    fine_plane = (rows, depth)
    corrected, potential = kernel_call(
        correction_kernel,
        [(3, 2) + fine_plane, four_planes],
        [
            pltpu.VMEM((5,) + mid_plane, f32),
            pltpu.VMEM((9,) + mid_plane, f32),
            pltpu.VMEM((5,) + fine_plane, f32),
            pltpu.VMEM((8,) + fine_plane, f32),
            pltpu.VMEM((6,) + fine_plane, f32),
        ],
        [VMEM] * 19,
        10**9,
        spread_low, both_mid, left_mid, right_mid, near_base, far_base, peer_base, near_v, near_w, peer_vw, obstacle,
        sum_high, sum_low, diff_high, diff_low, *own_depth,
        pair_sums(depth, mid_depth).T.copy(), pair_sums(rows, half),
    )
    stream = pl.BlockSpec((1, 1) + fine_plane, lambda i: (0, i, 0, 0))
    (corrected,) = kernel_call(
        stream_correction_kernel,
        [corrected.shape],
        [],
        [stream] + [full(two_planes)] * 2 + [by_plane(obstacle.shape, 0)],
        10**7,
        corrected, own_u, peer_u, obstacle,
        grid=(2,),
        out_specs=[stream],
        aliases={0: 0},
    )
    return (corrected, potential)


def step(velocity, obstacle, pressure):
    planes, rows, depth = velocity.shape[1:]
    fits = lax.axis_size("group") == 2 and planes == 2 and pressure.shape[0] == 4
    fits = fits and lax.axis_size("tunnel") > 10 and rows % 512 == 0 and depth % 256 == 0
    if fits:
        return paired(velocity, obstacle, pressure)
    return local(velocity, obstacle, pressure)


def solution(mesh):
    in_specs = (
        P(None, ("tunnel", "group"), None, None),
        P(("tunnel", "group"), None, None),
        P("tunnel", "group", None),
    )
    out_specs = (P(None, ("tunnel", "group"), None, None), P("tunnel", "group", None))
    return jax.shard_map(step, mesh=mesh, in_specs=in_specs, out_specs=out_specs, check_vma=False)
```
